32 devices in a mesh: dp: 2 (over core), blk: 16 (over z, y, x).
Axes of the slice: x: 2, y: 2, z: 4, core: 2. Of those that a mesh axis runs over, the one named last changes fastest.
Arguments:
- tokens: float32 [2, 2048, 768], P('dp', 'blk'), may hold values from -6 to 6
- cotangent: float32 [2, 2048, 768], P('dp', 'blk'), may hold values from -6 to 6
- mixer_weight: float32 [768, 3200], P(None, 'blk'), may hold values from -0.21875 to 0.21875
- widen_weight: float32 [2, 768, 1536], P(None, None, 'blk'), may hold values from -0.21875 to 0.21875
- narrow_weight: float32 [2, 1536, 768], P(None, None, 'blk'), may hold values from -0.15625 to 0.15625
- vectors: float32 [12288], replicated, may hold values from -8 to 8
- averager: float32 [4, 768, 16], replicated, may hold values from -181.01934 to 181.01934
- bias_index: int32 [4095], replicated, may hold values from 0 to 127, as said below
- mixer_rows: float32 [768], replicated, may hold values from 2.625168e-08 to 1.0500672e-07
- mixer_cols: float32 [3200], P('blk'), may hold values from 2.625168e-08 to 1.0500672e-07
- widen_rows: float32 [2, 768], replicated, may hold values from 2.625168e-08 to 1.0500672e-07
- widen_cols: float32 [2, 1536], P(None, 'blk'), may hold values from 2.625168e-08 to 1.0500672e-07
- narrow_rows: float32 [2, 1536], replicated, may hold values from 2.625168e-08 to 1.0500672e-07
- narrow_cols: float32 [2, 768], P(None, 'blk'), may hold values from 2.625168e-08 to 1.0500672e-07
- vector_moment: float32 [12288], replicated, may hold values from 1.0500672e-07 to 4.1450022e-07
- averager_moment: float32 [4, 768, 16], replicated, may hold values from 2.625168e-08 to 1.0500672e-07
Outputs:
- block_out: float32 [2, 2048, 768], P('dp', 'blk')
- tokens_grad: float32 [2, 2048, 768], P('dp', 'blk')
- mixer_grad: float32 [768, 3200], P(None, 'blk')
- widen_grad: float32 [2, 768, 1536], P(None, None, 'blk')
- narrow_grad: float32 [2, 1536, 768], P(None, None, 'blk')
- vector_grad: float32 [12288], replicated
- averager_grad: float32 [4, 768, 16], replicated
- mixer_new: float32 [768, 3200], P(None, 'blk')
- widen_new: float32 [2, 768, 1536], P(None, None, 'blk')
- narrow_new: float32 [2, 1536, 768], P(None, None, 'blk')
- vector_new: float32 [12288], replicated
- averager_new: float32 [4, 768, 16], replicated
- rows_mixer: float32 [768], replicated
- cols_mixer: float32 [3200], P('blk')
- rows_widen: float32 [2, 768], replicated
- cols_widen: float32 [2, 1536], P(None, 'blk')
- rows_narrow: float32 [2, 1536], replicated
- cols_narrow: float32 [2, 768], P(None, 'blk')
- moment_vector: float32 [12288], replicated
- moment_averager: float32 [4, 768, 16], replicated
- clip_norm: float32 [], replicated
The draws below stay inside these ranges and needn't reach their ends.
Inputs may be any that keep to these rules, and one draw needn't show every extreme that they name: `bias_index`: entry 2047 + k is the table row for a key k positions after its query; k = 0 takes row 0.
All inputs are finite; a program needn't handle non-finite values.
Results may differ from the reference program's by a relative error of at most 0.015.
Values may be sent and summed in bfloat16 or wider, within the bound.
A program may use at most 192 MiB of HBM per device.

```python
import math
import jax
import jax.numpy as jnp
from jax import lax

D = 768
ZD = 128
VD = 1536
FF = 1536
NH = 16
TOK_DEV = 128
NB = 128
STEP = 10
SEQ = 2048
ITEMS = 2
MX = 3200
NVEC = 12288


def draw_vectors(key, part):
    key = jax.random.fold_in(key, 11)
    noise = jnp.clip(jax.random.normal(key, (NVEC,), jnp.float32), -4.0, 4.0)
    bias_end = MX + 2 * VD + 2 * D
    rising = 0.6 + 1.2 * jnp.arange(D, dtype=jnp.float32) / D
    gain_one = rising * (1.0 + 0.15 * noise[bias_end:bias_end + D])
    shift_one = 0.3 * noise[bias_end + D:bias_end + 2 * D]
    gain_two = rising * (1.0 + 0.15 * noise[bias_end + 2 * D:bias_end + 3 * D])
    shift_two = 0.3 * noise[bias_end + 3 * D:bias_end + 4 * D]
    omega_part = noise[bias_end + 4 * D:bias_end + 5 * D]
    start_pair = bias_end + 5 * D
    qk_gain = 2.0 * noise[start_pair:start_pair + 2 * ZD]
    qk_shift = 0.3 * noise[start_pair + 2 * ZD:start_pair + 4 * ZD]
    table_part = noise[start_pair + 4 * ZD:]
    return jnp.concatenate([0.3 * noise[:bias_end], gain_one, shift_one, gain_two, shift_two, omega_part, qk_gain, qk_shift, table_part])


def draw_averager(key, part):
    key = jax.random.fold_in(key, 5)
    subkeys = jax.random.split(key, 5)
    mixing_raw = jax.random.uniform(subkeys[0], (D, NH), jnp.float32, -1.0, 1.0)
    mixing = jax.nn.sigmoid(mixing_raw)
    floor_log = jnp.log(jnp.float32(0.25 / SEQ))
    ceiling_log = jnp.log(jnp.float32(0.05))
    target = jnp.exp(floor_log + jax.random.uniform(subkeys[1], (D, NH), jnp.float32) * (ceiling_log - floor_log))
    damping = target / mixing
    damping_raw = jnp.log(damping / (1.0 - damping))
    spread = 0.5 + jax.random.uniform(subkeys[2], (D, NH), jnp.float32)
    signs = jnp.where(jax.random.uniform(subkeys[3], (D, NH), jnp.float32) < 0.5, -1.0, 1.0)
    beta_part = signs * spread * jnp.sqrt(2.0 * mixing / damping)
    gamma_part = jnp.clip(jax.random.normal(subkeys[4], (D, NH), jnp.float32), -4.0, 4.0)
    return jnp.stack([damping_raw, mixing_raw, beta_part, gamma_part])


def draw_bias_index(key, part):
    key = jax.random.fold_in(key, 7)
    half_count = NB // 2
    boundaries = (jax.random.permutation(key, SEQ - 1)[:half_count - 1] + 1).astype(jnp.int32)
    offsets = jnp.arange(2 * SEQ - 1, dtype=jnp.int32) - (SEQ - 1)
    magnitude = jnp.abs(offsets)
    bucket = jnp.sum((boundaries[None, :] <= magnitude[:, None]).astype(jnp.int32), axis=1)
    return (bucket + half_count * (offsets > 0).astype(jnp.int32)).astype(jnp.int32)


def block_levels(stream_key, shape, shards, low, high):
    gain = 1.0
    for axis_at, blocks in shards:
        draws = jax.random.uniform(jax.random.fold_in(jax.random.fold_in(stream_key, 6), axis_at), (blocks,), jnp.float32, low / len(shards), high / len(shards))
        gain = gain * jnp.repeat(jnp.exp(draws), shape[axis_at] // blocks).reshape((-1,) + (1,) * (len(shape) - 1 - axis_at))
    return gain


def bell_draw(rng, dims, scale, bound, shards=(), kind=jnp.bfloat16):
    gain = block_levels(rng, dims, shards, -0.22, 0.18) if shards else 1.0
    values = jax.random.normal(rng, dims, jnp.float32) * scale * gain
    return jnp.minimum(jnp.maximum(values, -bound), bound).astype(kind)


def setup_inputs(seed: int = 0) -> dict:
    seeds = jax.random.split(jax.random.key(seed), 17)
    return {
        "tokens": bell_draw(seeds[0], (ITEMS, SEQ, D), 1.0, 6.0, ((0, 2), (1, 16)), jnp.float32),
        "cotangent": bell_draw(seeds[1], (ITEMS, SEQ, D), 1.0, 6.0, ((0, 2), (1, 16)), jnp.float32),
        "mixer_weight": bell_draw(seeds[2], (D, MX), D ** -0.5, 0.21875, ((1, 16),), jnp.float32),
        "widen_weight": bell_draw(seeds[3], (2, D, VD), D ** -0.5, 0.21875, ((2, 16),), jnp.float32),
        "narrow_weight": bell_draw(seeds[4], (2, VD, D), VD ** -0.5, 0.15625, ((2, 16),), jnp.float32),
        "vectors": draw_vectors(jax.random.fold_in(seeds[16], 71), 0),
        "averager": draw_averager(jax.random.fold_in(seeds[16], 71), 0),
        "bias_index": draw_bias_index(jax.random.fold_in(seeds[16], 71), 0),
        "mixer_rows": jnp.clip(jnp.exp(jax.random.uniform(seeds[8], (D,), jnp.float32, math.log(2.6251679940969552e-08), math.log(1.0500671976387821e-07))), 2.6251679940969552e-08, 1.0500671976387821e-07),
        "mixer_cols": jnp.clip(jnp.exp(math.log(1.0500671976387821e-07) - 1.3862944 * jax.random.uniform(seeds[9], (MX,), jnp.float32) ** block_levels(seeds[9], (MX,), ((0, 16),), -0.2, 0.2)), 2.6251679940969552e-08, 1.0500671976387821e-07),
        "widen_rows": jnp.clip(jnp.exp(jax.random.uniform(seeds[10], (2, D), jnp.float32, math.log(2.6251679940969552e-08), math.log(1.0500671976387821e-07))), 2.6251679940969552e-08, 1.0500671976387821e-07),
        "widen_cols": jnp.clip(jnp.exp(math.log(1.0500671976387821e-07) - 1.3862944 * jax.random.uniform(seeds[11], (2, VD), jnp.float32) ** block_levels(seeds[11], (2, VD), ((1, 16),), -0.2, 0.2)), 2.6251679940969552e-08, 1.0500671976387821e-07),
        "narrow_rows": jnp.clip(jnp.exp(jax.random.uniform(seeds[12], (2, VD), jnp.float32, math.log(2.6251679940969552e-08), math.log(1.0500671976387821e-07))), 2.6251679940969552e-08, 1.0500671976387821e-07),
        "narrow_cols": jnp.clip(jnp.exp(math.log(1.0500671976387821e-07) - 1.3862944 * jax.random.uniform(seeds[13], (2, D), jnp.float32) ** block_levels(seeds[13], (2, D), ((1, 16),), -0.2, 0.2)), 2.6251679940969552e-08, 1.0500671976387821e-07),
        "vector_moment": jnp.clip(jnp.exp(jax.random.uniform(seeds[14], (NVEC,), jnp.float32, math.log(1.0500671976387821e-07), math.log(4.145002208133519e-07))), 1.0500671976387821e-07, 4.145002208133519e-07),
        "averager_moment": jnp.clip(jnp.exp(jax.random.uniform(seeds[15], (4, D, NH), jnp.float32, math.log(2.6251679940969552e-08), math.log(1.0500671976387821e-07))), 2.6251679940969552e-08, 1.0500671976387821e-07),
    }


EPS_NORM = 1e-05
EPS_ONE = 1e-30
EPS_TWO = 0.001
CLIP_NORM = 1.0
CLIP_UPDATE = 1.0
RATE = 0.5

@jax.custom_vjp
def low(v):
    return lax.optimization_barrier(v.astype(jnp.bfloat16)).astype(jnp.float32)

@jax.custom_vjp
def low_back(v):
    return v

def low_keep(v):
    return (low(v), None)

def low_pass(kept, grad):
    return (grad,)

def back_keep(v):
    return (v, None)

def back_low(kept, grad):
    return (low(grad),)
low.defvjp(low_keep, low_pass)
low_back.defvjp(back_keep, back_low)

def matmul(left_side, right_side):
    return jnp.dot(left_side, right_side, precision=lax.Precision.HIGHEST, preferred_element_type=jnp.float32)

def pieces(vectors):
    widths = (MX, VD, D, FF, D, D, D, D, D, D, 2 * ZD, 2 * ZD, NB)
    collected = []
    offset = 0
    for width in widths:
        collected.append(vectors[offset:offset + width])
        offset = offset + width
    return collected

def layer_norm(values, norm_gain, norm_shift):
    centered = values - lax.optimization_barrier(jnp.mean(values, axis=-1, keepdims=True))
    inverse = lax.rsqrt(lax.optimization_barrier(jnp.mean(centered * centered, axis=-1, keepdims=True)) + EPS_NORM)
    return centered * inverse * norm_gain + norm_shift

def moving_average(values, averager):
    damping = jax.nn.sigmoid(averager[0])
    mixing = jax.nn.sigmoid(averager[1])
    decays = 1.0 - damping * mixing
    inflow = damping * averager[2]
    outflow = averager[3] * NH ** (-0.5)

    def token_step(carried, row_values):
        carried = decays * carried + inflow * row_values[:, None]
        return (carried, lax.optimization_barrier(jnp.sum(carried * outflow, axis=1)))

    def block_step(carried, block_values):
        return lax.scan(token_step, carried, block_values)
    initial = jnp.zeros((D, NH), jnp.float32)
    _, result = lax.scan(jax.checkpoint(block_step), initial, values.reshape(SEQ // TOK_DEV, TOK_DEV, D))
    return result.reshape(SEQ, D)

def attention(queries, key_rows, value_rows, bias_row):
    block_rows = min(512, SEQ)

    def one_block(first_row):
        query_block = lax.dynamic_slice_in_dim(queries, first_row, block_rows, 0)
        places = jnp.arange(SEQ, dtype=jnp.int32)[None, :] - (first_row + jnp.arange(block_rows, dtype=jnp.int32))[:, None] + (SEQ - 1)
        scores = low_back(matmul(query_block, key_rows.T) + jnp.take(bias_row, places))
        return matmul(low(jax.nn.softmax(scores, axis=-1)), value_rows)
    starts = jnp.arange(SEQ // block_rows, dtype=jnp.int32) * block_rows
    return lax.map(jax.checkpoint(one_block), starts).reshape(SEQ, VD)

def forward(inputs, mixer, widen, narrow, vectors, averager, bias_index):
    bias_mixer, bias_value, bias_hidden, bias_expand, bias_project, gain_one, shift_one, gain_two, shift_two, omega_scale, qk_gain, qk_shift, bias_table = pieces(vectors)
    pre_act = moving_average(inputs, averager) + omega_scale * inputs
    prime_low = low(jax.nn.silu(pre_act))
    mixed_out = low_back(matmul(prime_low, low(mixer)) + bias_mixer)
    update_gate = jax.nn.sigmoid(mixed_out[:, :D])
    shared = jax.nn.silu(mixed_out[:, D:D + ZD])
    reset_gate = jax.nn.silu(mixed_out[:, D + ZD:D + ZD + VD])
    hidden_x = mixed_out[:, D + ZD + VD:]
    queries = low((shared * qk_gain[:ZD] + qk_shift[:ZD]) * ZD ** (-0.5))
    key_rows = low(shared * qk_gain[ZD:] + qk_shift[ZD:])
    value_pre = low_back(matmul(low(inputs), low(widen[0])) + bias_value)
    value_rows = low(jax.nn.silu(value_pre))
    bias_row = bias_table[bias_index]
    attended = low_back(attention(queries, key_rows, value_rows, bias_row))
    gated_low = low(reset_gate * attended)
    hidden_pre = low_back(hidden_x + matmul(gated_low, low(narrow[0])) + bias_hidden)
    residual_one = inputs + update_gate * (jax.nn.silu(hidden_pre) - inputs)
    layer_one = layer_norm(residual_one, gain_one, shift_one)
    expand_pre = low_back(matmul(low(layer_one), low(widen[1])) + bias_expand)
    project_two = low_back(matmul(low(jax.nn.silu(expand_pre)), low(narrow[1])) + bias_project)
    return layer_norm(layer_one + project_two, gain_two, shift_two)

def factored(weight, gradient, row_state, column_state, decay_rate):
    square = gradient * gradient + EPS_ONE
    rows_new = decay_rate * row_state + (1.0 - decay_rate) * lax.optimization_barrier(jnp.mean(square, axis=2))
    columns_new = decay_rate * column_state + (1.0 - decay_rate) * lax.optimization_barrier(jnp.mean(square, axis=1))
    scale_new = rows_new[:, :, None] * columns_new[:, None, :] / lax.optimization_barrier(jnp.mean(rows_new, axis=1))[:, None, None]
    update = gradient * lax.rsqrt(scale_new)
    rms_update = jnp.sqrt(lax.optimization_barrier(jnp.mean(update * update, axis=(1, 2))))
    update = update / jnp.maximum(1.0, rms_update / CLIP_UPDATE)[:, None, None]
    rms_weight = jnp.sqrt(lax.optimization_barrier(jnp.mean(weight * weight, axis=(1, 2))))
    return (weight - RATE * jnp.maximum(EPS_TWO, rms_weight)[:, None, None] * update, rows_new, columns_new)

def plain_update(weight, gradient, moment, decay_rate):
    moment_new = decay_rate * moment + (1.0 - decay_rate) * (gradient * gradient + EPS_ONE)
    update = gradient * lax.rsqrt(moment_new)
    rms_update = jnp.sqrt(jnp.mean(update * update))
    update = update / jnp.maximum(1.0, rms_update / CLIP_UPDATE)
    rms_weight = jnp.sqrt(jnp.mean(weight * weight))
    return (weight - RATE * jnp.maximum(EPS_TWO, rms_weight) * update, moment_new)

def reference(tokens, cotangent, mixer_weight, widen_weight, narrow_weight, vectors, averager, bias_index, mixer_rows, mixer_cols, widen_rows, widen_cols, narrow_rows, narrow_cols, vector_moment, averager_moment):
    params = (mixer_weight, widen_weight, narrow_weight, vectors, averager)

    def layer_pair(inputs, mixer, widen, narrow, vector_in, average_in):
        return forward(inputs, mixer, widen, narrow, vector_in, average_in, bias_index)

    def item_step(totals, item_pair):
        outputs, pullback = jax.vjp(layer_pair, item_pair[0], *params)
        gradients = pullback(item_pair[1])
        summed = tuple((totals[member] + gradients[member + 1] for member in range(5)))
        return (summed, (outputs, gradients[0]))
    zero_grads = tuple((jnp.zeros_like(parameter) for parameter in params))
    totals, (block_out, tokens_grad) = lax.scan(item_step, zero_grads, (tokens, cotangent))
    squares = jnp.sum(totals[0] * totals[0]) + jnp.sum(totals[1] * totals[1]) + jnp.sum(totals[2] * totals[2])
    squares = squares + jnp.sum(totals[3] * totals[3]) + jnp.sum(totals[4] * totals[4])
    clip_norm = jnp.sqrt(squares)
    factor = jnp.minimum(1.0, CLIP_NORM / clip_norm)
    clipped = tuple((gradient * factor for gradient in totals))
    decay_rate = 1.0 - STEP ** (-0.8)
    mixer_new, rows_mixer, cols_mixer = factored(mixer_weight[None], clipped[0][None], mixer_rows[None], mixer_cols[None], decay_rate)
    widen_new, rows_widen, cols_widen = factored(widen_weight, clipped[1], widen_rows, widen_cols, decay_rate)
    narrow_new, rows_narrow, cols_narrow = factored(narrow_weight, clipped[2], narrow_rows, narrow_cols, decay_rate)
    vector_new, moment_vector = plain_update(vectors, clipped[3], vector_moment, decay_rate)
    averager_new, moment_averager = plain_update(averager, clipped[4], averager_moment, decay_rate)
    return (block_out, tokens_grad, clipped[0], clipped[1], clipped[2], clipped[3], clipped[4], mixer_new[0], widen_new, narrow_new, vector_new, averager_new, rows_mixer[0], cols_mixer[0], rows_widen, cols_widen, rows_narrow, cols_narrow, moment_vector, moment_averager, clip_norm)
```

```python
import functools
import jax
import jax.numpy as jnp
from jax import lax
from jax.experimental import pallas as pl
from jax.experimental.pallas import tpu as pltpu
from jax.sharding import PartitionSpec as P

D = 768
ZD = 128
VD = 1536
FF = 1536
NH = 16
NB = 128
STEP = 10
MX = 3200
EPS_NORM = 1e-05
EPS_ONE = 1e-30
EPS_TWO = 0.001
CLIP_NORM = 1.0
CLIP_UPDATE = 1.0
RATE = 0.5

OFF_MX = 0
OFF_V = MX
OFF_H = OFF_V + VD
OFF_UP = OFF_H + D
OFF_DOWN = OFF_UP + FF
OFF_G1 = OFF_DOWN + D
OFF_S1 = OFF_G1 + D
OFF_G2 = OFF_S1 + D
OFF_S2 = OFF_G2 + D
OFF_OM = OFF_S2 + D
OFF_QG = OFF_OM + D
OFF_QS = OFF_QG + 2 * ZD
OFF_TB = OFF_QS + 2 * ZD
NVEC = OFF_TB + NB

MESH = pl.DeviceIdType.MESH
BF = jnp.bfloat16
F32 = jnp.float32
NN = (((1,), (0,)), ((), ()))
NT = (((1,), (1,)), ((), ()))
TN = (((0,), (0,)), ((), ()))


def dot(a, b, dims=NN):
    return lax.dot_general(a, b, dims, preferred_element_type=F32)


def sigmoid(v):
    return jax.nn.sigmoid(v)


def silu(v):
    return v * sigmoid(v)


def silu_grad(v):
    s = sigmoid(v)
    return s * (1.0 + v * (1.0 - s))


class Place:
    def __init__(self, lines):
        self.lines = lines
        self.dp = lax.axis_index("dp")
        blk = lax.axis_index("blk")
        self.blk = blk
        self.c = self.dp % 2
        self.g = blk // 4
        self.p = blk % 4
        self.b = self.p // 2
        self.a = self.p % 2
        self.na = 1 - self.a
        self.nb = 1 - self.b

    def sib(self):
        return (self.dp + 1 - 2 * self.c, self.blk)

    def at(self, g, b, a):
        return (self.dp, g * 4 + b * 2 + a)

    def line(self, k):
        return (self.g + k) % self.lines

    def plane(self, k):
        return (self.p + k) % 4

    def pick(self, first, second):
        return first + self.c * (second - first)


def vec(ref, off, width):
    parts = []
    while width > 0:
        row, lane = off // D, off % D
        take = min(width, D - lane)
        parts.append(ref[row : row + 1, lane : lane + take])
        off, width = off + take, width - take
    return parts[0] if len(parts) == 1 else jnp.concatenate(parts, axis=1)


def greet(me, others):
    bar = pltpu.get_barrier_semaphore()
    for dev in others:
        pl.semaphore_signal(bar, inc=1, device_id=dev, device_id_type=MESH)
    pl.semaphore_wait(bar, len(others))


def close_peers(me):
    out = [me.sib()]
    for k in range(1, me.lines):
        out.append(me.at(me.line(k), me.b, me.a))
    for k in range(1, 4):
        q = me.plane(k)
        out.append(me.at(me.g, q // 2, q % 2))
    return out


def rcopy(src, dst, ssem, rsem, dev):
    return pltpu.make_async_remote_copy(
        src_ref=src, dst_ref=dst, send_sem=ssem, recv_sem=rsem, device_id=dev, device_id_type=MESH
    )


class Gather:
    def __init__(self, me, W, ssem, rsem):
        self.me, self.W, self.ssem, self.rsem = me, W, ssem, rsem
        self.half = W.shape[-1] // 2
        self.G = me.lines
        self.started = []

    def cols(self, c):
        return pl.ds(pl.multiple_of(c * self.half, 128), self.half)

    def one(self, g, b, a, c):
        return self.W.at[g, b, a, :, self.cols(c)]

    def many(self, b, a, c):
        return self.W.at[:, b, a, :, self.cols(c)]

    def go(self, src, slot, dev):
        cp = rcopy(src, src, self.ssem.at[slot], self.rsem.at[slot], dev)
        cp.start()
        self.started.append(cp)

    def await_in(self, ref, slot):
        rcopy(ref, ref, self.ssem.at[slot], self.rsem.at[slot], self.me.sib()).wait_recv()

    def z(self):
        me = self.me
        for k in range(1, self.G):
            self.go(self.one(me.g, me.b, me.a, me.c), k, me.at(me.line(k), me.b, me.a))

    def first(self):
        me, G = self.me, self.G
        for k in range(1, G):
            self.await_in(self.one((me.g + G - k) % G, me.b, me.a, me.c), k)
        own = self.many(me.b, me.a, me.c)
        self.go(own, G, me.at(me.g, me.b, me.na))
        self.go(own, G + 1, me.at(me.g, me.nb, me.a))
        self.go(own, G + 3, me.sib())

    def second(self):
        me, G = self.me, self.G
        x = self.many(me.b, me.na, me.c)
        y = self.many(me.nb, me.a, me.c)
        self.await_in(x, G)
        self.await_in(y, G + 1)
        fwd = self.many(me.pick(me.b, me.nb), me.pick(me.na, me.a), me.c)
        self.go(fwd, G + 2, me.at(me.g, me.pick(me.nb, me.b), me.pick(me.a, me.na)))
        self.go(x, G + 4, me.sib())
        self.go(y, G + 5, me.sib())

    def third(self):
        me, G = self.me, self.G
        d = self.many(me.nb, me.na, me.c)
        self.await_in(d, G + 2)
        self.go(d, G + 6, me.sib())

    def done(self):
        me, G = self.me, self.G
        o = 1 - me.c
        self.await_in(self.many(me.b, me.a, o), G + 3)
        self.await_in(self.many(me.b, me.na, o), G + 4)
        self.await_in(self.many(me.nb, me.a, o), G + 5)
        self.await_in(self.many(me.nb, me.na, o), G + 6)

    def drain(self):
        for cp in self.started:
            cp.wait_send()


def gather_slots(G):
    return G + 7


def decays_of(avg_ref):
    damp = sigmoid(avg_ref[0])
    mix = sigmoid(avg_ref[1])
    dec = 1.0 - damp * mix
    return damp, mix, dec, damp * avg_ref[2], avg_ref[3] * NH ** (-0.5)


def power(v, n):
    while n > 1:
        v = v * v
        n = n // 2
    return v


def ma_pass(x_ref, h, dec, inf, outf, pre_ref, keep=None):
    def step(i, h):
        if keep is not None:
            keep[i] = h
        xs = x_ref[pl.ds(i * 8, 8), :]
        rows = []
        for r in range(8):
            h = dec * h + inf * xs[r : r + 1]
            if pre_ref is not None:
                rows.append(jnp.sum(outf * h, axis=0, keepdims=True))
        if pre_ref is not None:
            pre_ref[pl.ds(i * 8, 8), :] = jnp.concatenate(rows, axis=0)
        return h

    return lax.fori_loop(0, x_ref.shape[0] // 8, step, h)


def toeplitz_block(bias_ref, m):
    w = jnp.concatenate([bias_ref[pl.ds(m, 1), :], bias_ref[pl.ds(m + 1, 1), :]], axis=1)
    return pltpu.roll(jnp.broadcast_to(w, (128, 256)), 1, 1, stride=1, stride_axis=0)[:, 128:]


def as_rows(col):
    return jnp.broadcast_to(col, (128, 128)).T[0:8]


def as_col(rows):
    return jnp.broadcast_to(rows[0:1], (128, 128)).T[:, 0:1]


def fwd_kernel(
    G, rows,
    x_ref, wid_ref, mix_ref, nar_ref, avg_ref, vec_ref, bias_ref,
    w0_o, mx_o, n0_o, w1_o, n1_o, mixed_o, pre_o, ent_o, att_o, lse_o, s_o, q_o, k_o, v_o, vp_o, xb_o,
    w0, mx, n0, w1, n1, mxc, fin, ftot, ob, oin, lout, lin, xb, qb, kb, brow,
    agss, agrs, xss, xrs, fss, frs, qss, qrs, oss, ors, outs,
):
    me = Place(G)
    T = x_ref.shape[0]
    rm, rw, rn = rows
    own = {"g": me.g, "b": me.b, "a": me.a}
    w0[me.g, me.b, me.a] = wid_ref[0].astype(BF)
    w1[me.g, me.b, me.a] = wid_ref[1].astype(BF)
    mx[me.g, me.b, me.a] = mix_ref[...].astype(BF)
    n0[me.g, me.b, me.a] = nar_ref[0].astype(BF)
    n1[me.g, me.b, me.a] = nar_ref[1].astype(BF)
    xb[me.g] = x_ref[...].astype(BF)
    greet(me, close_peers(me))
    ga = [Gather(me, W, agss.at[i], agrs.at[i]) for i, W in enumerate((w0, mx, n0, w1, n1))]
    gw0, gmx, gn0, gw1, gn1 = ga
    sent = []

    def go(src, dst, ss, rs, dev):
        cp = rcopy(src, dst, ss, rs, dev)
        cp.start()
        sent.append(cp)

    def got(ref, ss, rs):
        rcopy(ref, ref, ss, rs, me.sib()).wait_recv()

    def line_send(ref_at, ss, rs):
        for k in range(1, G):
            go(ref_at(me.g), ref_at(me.g), ss.at[k], rs.at[k], me.at(me.line(k), me.b, me.a))

    def line_got(ref_at, ss, rs):
        for k in range(1, G):
            got(ref_at((me.g + G - k) % G), ss.at[k], rs.at[k])

    def plane_send(ref_at, ss, rs):
        for k in range(1, 4):
            q = me.plane(k)
            go(ref_at(me.p), ref_at(me.p), ss.at[k], rs.at[k], me.at(me.g, q // 2, q % 2))

    def plane_got(ref_at, ss, rs):
        for k in range(1, 4):
            got(ref_at((me.p + 4 - k) % 4), ss.at[k], rs.at[k])

    gw0.z()
    line_send(lambda i: xb.at[i], xss, xrs)
    gmx.z()
    damp, mix, dec, inf, outf = decays_of(avg_ref)
    zero = jnp.zeros((NH, D), F32)
    fin[me.p] = ma_pass(x_ref, zero, dec, inf, outf, None)
    plane_send(lambda i: fin.at[i], fss.at[0], frs.at[0])
    gn0.z()
    gw0.first()
    plane_got(lambda i: fin.at[i], fss.at[0], frs.at[0])
    whole = power(dec, T)
    tot = fin[0]
    for q in range(1, 4):
        tot = whole * tot + fin[q]
    ftot[me.g] = tot
    line_send(lambda i: ftot.at[i], fss.at[1], frs.at[1])
    gmx.first()
    gw0.second()
    gw1.z()
    line_got(lambda i: ftot.at[i], fss.at[1], frs.at[1])
    ent = zero
    whole4 = power(whole, 4)
    for i in range(G - 1):
        ent = jnp.where(i < me.g, whole4 * ent + ftot[i], ent)
    for q in range(3):
        ent = jnp.where(q < me.p, whole * ent + fin[q], ent)
    gn1.z()
    ma_pass(x_ref, ent, dec, inf, outf, pre_o, ent_o)
    pre = pre_o[...] + vec(vec_ref, OFF_OM, D) * x_ref[...]
    pre_o[...] = pre
    gn0.first()
    gw0.third()
    gmx.second()
    gw0.done()
    line_got(lambda i: xb.at[i], xss, xrs)
    step = max(1, G // 2)
    wide = step * 4 * rw
    for i in range(G // step):
        wblk = w0[i * step : (i + 1) * step].reshape(wide, D)
        for gg in range(G):
            vp = dot(xb[gg], wblk, NT) + vec(vec_ref, OFF_V + i * wide, wide)
            vp_o[gg * T : (gg + 1) * T, i * wide : (i + 1) * wide] = silu_grad(vp).astype(BF)
            v_o[gg * T : (gg + 1) * T, i * wide : (i + 1) * wide] = silu(vp).astype(BF)
    gw1.first()
    gn0.second()
    gmx.third()
    gmx.done()
    cols = MX // (4 * G)
    for i in range(4 * G):
        mxc[i * cols : (i + 1) * cols] = mx[i // 4, (i // 2) % 2, i % 2, :cols]
    prime = silu(pre_o[...]).astype(BF)
    for i in range(5):
        w = MX // 5
        mixed_o[:, i * w : (i + 1) * w] = (
            dot(prime, mxc[i * w : (i + 1) * w], NT) + vec(vec_ref, OFF_MX + i * w, w)
        )
    shared = silu(mixed_o[:, D : D + ZD])
    scaling = ZD ** (-0.5)
    qb[me.p] = (
        (shared * vec(vec_ref, OFF_QG, ZD) + vec(vec_ref, OFF_QS, ZD)) * scaling
    ).astype(BF)
    kb[me.g] = (
        shared * vec(vec_ref, OFF_QG + ZD, ZD) + vec(vec_ref, OFF_QS + ZD, ZD)
    ).astype(BF)
    plane_send(lambda i: qb.at[i], qss.at[0], qrs.at[0])
    line_send(lambda i: kb.at[i], qss.at[1], qrs.at[1])
    gn1.first()
    gw1.second()
    gn0.third()
    plane_got(lambda i: qb.at[i], qss.at[0], qrs.at[0])
    line_got(lambda i: kb.at[i], qss.at[1], qrs.at[1])
    first_row = me.p - 4 * me.g - 4 + 4 * G
    table = jnp.broadcast_to(vec(vec_ref, OFF_TB, NB), (128, NB)).T
    for r in range(4 * G + 1):
        hit = bias_ref[pl.ds(first_row + r, 1), :] == lax.broadcasted_iota(jnp.int32, (NB, 128), 0)
        brow[r : r + 1] = jnp.sum(jnp.where(hit, table, 0.0), axis=0, keepdims=True)
    kall = kb[...].reshape(G * T, ZD)
    for kk in range(1, 4):
        i = (me.p + kk) % 4
        attend_block(G, T, me, i, qb, kall, v_o, brow, s_o, ob, lout, None)
        go(ob.at[i], oin.at[me.p], oss.at[kk], ors.at[kk], me.at(me.g, i // 2, i % 2))
        go(lout.at[i], lin.at[me.p], oss.at[4 + kk], ors.at[4 + kk], me.at(me.g, i // 2, i % 2))
    gn1.second()
    gw1.third()
    attend_block(G, T, me, me.p, qb, kall, v_o, brow, s_o, ob, lout, att_o)
    lin[me.p] = lout[me.p]
    gn0.done()
    gn1.third()
    for k in range(1, 4):
        got(oin.at[(me.p + 4 - k) % 4], oss.at[k], ors.at[k])
        got(lin.at[(me.p + 4 - k) % 4], oss.at[4 + k], ors.at[4 + k])
    ls = [as_col(lin[j]) for j in range(4)]
    peak = functools.reduce(jnp.maximum, ls)
    lse = peak + jnp.log(functools.reduce(jnp.add, [jnp.exp(l - peak) for l in ls]))
    mine = as_col(lout[me.p])
    att_o[...] = att_o[...] * jnp.exp(mine - lse)
    for k in range(1, 4):
        j = (me.p + k) % 4
        wj = jnp.exp(as_col(lin[j]) - lse)
        att_o[...] += oin[j].astype(F32) * wj
    lse_o[...] = as_rows(lse)
    xb_o[...] = xb[...]
    q_o[...] = qb[...]
    k_o[...] = kb[...]
    gw1.done()
    gn1.done()
    for ga_ in ga:
        ga_.drain()
    for cp in sent:
        cp.wait_send()
    pairs = [(w0, w0_o), (mxc, mx_o), (n0, n0_o), (w1, w1_o), (n1, n1_o)]
    cps = [pltpu.make_async_copy(s, d, outs.at[i]) for i, (s, d) in enumerate(pairs)]
    for cp in cps:
        cp.start()
    for cp in cps:
        cp.wait()


def attend_block(G, T, me, i, q_o, kall, v_o, brow, s_o, ob, lout, att_o):
    s = dot(q_o[i], kall, NT)
    tops = []
    for kk in range(G):
        m = 4 * kk - i + 3
        tops.append(toeplitz_block(brow, m))
    s = s + jnp.concatenate(tops, axis=1)
    s_o[i] = s
    top = jnp.max(s, axis=1, keepdims=True)
    e = jnp.exp(s - top)
    tot = jnp.sum(e, axis=1, keepdims=True)
    o = dot(e.astype(BF), v_o[...]) / tot
    if att_o is None:
        ob[i] = o.astype(BF)
    else:
        att_o[...] = o
    lout[i] = as_rows(top + jnp.log(tot))


def forward_call(G, x, wid, mix, nar, avg, vec, bias):
    T = x.shape[0]
    rm, rw, rn = mix.shape[0], wid.shape[1], nar.shape[1]
    A = jax.ShapeDtypeStruct
    slots = gather_slots(G)
    out_shape = (
        A((G, 2, 2, rw, D), BF), A((MX, D), BF), A((G, 2, 2, rn, VD), BF), A((G, 2, 2, rw, D), BF), A((G, 2, 2, rn, FF), BF),
        A((T, MX), F32), A((T, D), F32), A((T // 8, NH, D), F32), A((T, VD), F32), A((8, 128), F32),
        A((4, T, G * T), F32), A((4, T, ZD), BF), A((G, T, ZD), BF), A((G * T, VD), BF), A((G * T, VD), BF), A((G, T, D), BF),
    )
    vm = pl.BlockSpec(memory_space=pltpu.VMEM)
    anys = pl.BlockSpec(memory_space=pl.ANY)
    S = pltpu.SemaphoreType.DMA
    return pl.pallas_call(
        functools.partial(fwd_kernel, G, (rm, rw, rn)),
        out_shape=out_shape,
        in_specs=[vm] * 7,
        out_specs=[anys] * 5 + [vm] * 11,
        scratch_shapes=[
            pltpu.VMEM((G, 2, 2, rw, D), BF), pltpu.VMEM((G, 2, 2, rm, D), BF), pltpu.VMEM((G, 2, 2, rn, VD), BF),
            pltpu.VMEM((G, 2, 2, rw, D), BF), pltpu.VMEM((G, 2, 2, rn, FF), BF), pltpu.VMEM((MX, D), BF),
            pltpu.VMEM((4, NH, D), F32), pltpu.VMEM((G, NH, D), F32),
            pltpu.VMEM((4, T, VD), BF), pltpu.VMEM((4, T, VD), BF), pltpu.VMEM((4, 8, 128), F32), pltpu.VMEM((4, 8, 128), F32),
            pltpu.VMEM((G, T, D), BF), pltpu.VMEM((4, T, ZD), BF), pltpu.VMEM((G, T, ZD), BF), pltpu.VMEM((4 * G + 8, 128), F32),
            S((5, slots)), S((5, slots)), S((G,)), S((G,)), S((2, max(4, G))), S((2, max(4, G))), S((2, max(4, G))), S((2, max(4, G))), S((8,)), S((8,)),
            S((5,)),
        ],
        compiler_params=pltpu.CompilerParams(collective_id=1, has_side_effects=True, vmem_limit_bytes=60 * 2**20),
    )(x, wid, mix, nar, avg, vec, bias)


def padded(v, axis):
    extra = -v.shape[axis] % 16
    if extra == 0:
        return v
    pads = [(0, 0)] * v.ndim
    pads[axis] = (0, extra)
    return jnp.pad(v, pads)


class Link:
    def __init__(self, me, ssem, rsem):
        self.me, self.ssem, self.rsem = me, ssem, rsem
        self.used = 0
        self.started = []

    def slot(self):
        self.used += 1
        return self.used - 1

    def go(self, src, dst, slot, dev):
        cp = rcopy(src, dst, self.ssem.at[slot], self.rsem.at[slot], dev)
        cp.start()
        self.started.append(cp)

    def got(self, ref, slot):
        rcopy(ref, ref, self.ssem.at[slot], self.rsem.at[slot], self.me.sib()).wait_recv()

    def drain(self):
        for cp in self.started:
            cp.wait_send()

    def swap(self, src, dst):
        s = self.slot()
        self.go(src, dst, s, self.me.sib())
        return lambda: self.got(dst, s)

    def plane(self, src, dst):
        me = self.me
        slots = [self.slot() for _ in range(3)]
        for k in range(1, 4):
            q = (me.p + k) % 4
            self.go(src(q), dst(me.p), slots[k - 1], me.at(me.g, q // 2, q % 2))

        def wait():
            for k in range(1, 4):
                self.got(dst((me.p + 4 - k) % 4), slots[k - 1])

        return wait

    def line(self, src, dst):
        me, G = self.me, self.me.lines
        slots = [self.slot() for _ in range(G - 1)]
        for k in range(1, G):
            h = (me.g + k) % G
            self.go(src(h), dst(me.g), slots[k - 1], me.at(h, me.b, me.a))

        def wait():
            for k in range(1, G):
                self.got(dst((me.g + G - k) % G), slots[k - 1])

        return wait

    def pairs(self, src, dst, count):
        me = self.me
        slots = [self.slot() for _ in range(count - 1)]
        for k in range(1, count):
            d = (me.dp // 2 + k) % count
            self.go(src, dst(me.dp // 2), slots[k - 1], (2 * d + me.c, me.blk))

        def wait():
            for k in range(1, count):
                self.got(dst((me.dp // 2 + count - k) % count), slots[k - 1])

        return wait


class Reduce:
    def __init__(self, me, link, H, R, RL):
        self.me, self.link, self.H, self.R, self.RL = me, link, H, R, RL
        self.slots = [link.slot() for _ in range(3)]

    def bundle(self, b, a):
        return self.H.at[:, b, a]

    def first(self):
        me = self.me
        b, a = me.pick(me.nb, me.b), me.pick(me.a, me.na)
        dev = me.at(me.g, b, a)
        self.link.go(self.bundle(me.nb, me.na), self.R.at[0], self.slots[0], dev)
        self.link.go(self.bundle(b, a), self.R.at[1], self.slots[1], dev)

    def second(self):
        me, H = self.me, self.H
        self.link.got(self.R.at[0], self.slots[0])
        b, a = me.pick(me.b, me.nb), me.pick(me.na, me.a)
        for g in range(me.lines):
            H[g, b, a] = (H[g, b, a].astype(F32) + self.R[0, g].astype(F32)).astype(BF)
        self.link.go(self.bundle(b, a), self.R.at[2], self.slots[2], me.at(me.g, b, a))

    def third(self):
        me, H, R = self.me, self.H, self.R
        self.link.got(R.at[1], self.slots[1])
        self.link.got(R.at[2], self.slots[2])
        for g in range(me.lines):
            H[g, me.b, me.a] = (
                H[g, me.b, me.a].astype(F32) + R[1, g].astype(F32) + R[2, g].astype(F32)
            ).astype(BF)
        self.wait = self.link.line(lambda h: H.at[h, me.b, me.a], lambda h: self.RL.at[h])

    def fourth(self):
        me = self.me
        self.wait()
        self.RL[me.g] = self.H[me.g, me.b, me.a]
        total = self.RL[0].astype(F32)
        for g in range(1, me.lines):
            total = total + self.RL[g].astype(F32)
        return total


def into_blocks(H, value, first, rows):
    n = 4 * H.shape[0]
    count = value.shape[0]
    value = value.astype(BF)
    if H.shape[3] == rows and first == 0 and count == n * rows:
        H[...] = value.reshape(H.shape)
        return
    for i in range(n):
        lo, hi = max(first, i * rows), min(first + count, (i + 1) * rows)
        if lo < hi:
            H[i // 4, (i // 2) % 2, i % 2, lo - i * rows : hi - i * rows] = value[lo - first : hi - first]


def norm(v):
    centered = v - jnp.mean(v, axis=-1, keepdims=True)
    inverse = lax.rsqrt(jnp.mean(centered * centered, axis=-1, keepdims=True) + EPS_NORM)
    return centered * inverse, inverse


def norm_back(incoming, normed, inverse, gain):
    scaled = incoming * gain
    return inverse * (
        scaled
        - jnp.mean(scaled, axis=-1, keepdims=True)
        - normed * jnp.mean(scaled * normed, axis=-1, keepdims=True)
    )


def down(v):
    return jnp.sum(v.astype(F32), axis=0, keepdims=True)


def put(ref, off, row):
    width, at = row.shape[1], 0
    while at < width:
        r, lane = (off + at) // D, (off + at) % D
        take = min(width - at, D - lane)
        ref[r : r + 1, lane : lane + take] = row[:, at : at + take]
        at += take


def bwd_kernel(
    G, count, sizes,
    x_ref, cot_ref, w0_h, mx_h, n0_h, w1_h, n1_h, mixed_ref, pre_ref, keep_ref, att_ref, lse_ref,
    s_ref, q_ref, k_ref, v_ref, vp_h, xb_ref, avg_ref, vec_ref, index_ref,
    block_o, tok_o, gm_o, gw_o, gn_o, sum_o, ma_o,
    GD, EX, GU, LL, GH, GT, GV, XB, GM, PB, full, W0, WM, HM, WN0, W1, WN1, R0, RM, RN0, R1, RN1, L0, LM, LN0, L1, LN1,
    F0, FM, FN0, F1, FN1, GA, ST, P16, GS, QP, KS, KP, DX, DP, BP, fin, ftot, pairbuf,
    AV, AS, AW, AT, AP, AL, prof, PA, P0, PM, PN0, P1, PN1, ssem, rsem, lsem,
):
    me = Place(G)
    T = x_ref.shape[0]
    loads = {}
    for i, (name, src, dst) in enumerate(
        (("n0", n0_h, WN0), ("w1", w1_h, W1), ("n1", n1_h, WN1), ("sgv", vp_h, GV.at[0]), ("w0", w0_h, W0), ("mx", mx_h, WM))
    ):
        loads[name] = pltpu.make_async_copy(src, dst, lsem.at[i])
        loads[name].start()
    link = Link(me, ssem, rsem)
    others = close_peers(me)
    for k in range(1, count):
        others.append((2 * ((me.dp // 2 + k) % count) + me.c, me.blk))
    greet(me, others)
    o = 1 - me.c

    def cols(c, half):
        return pl.ds(pl.multiple_of(c * half, 128), half)

    def share_half(ref, own, dst):
        half = dst.shape[-1]
        idx = (slice(None),) * (len(own.shape) - 1)
        dst[0] = own[idx + (cols(me.c, half),)]
        return link.swap(own.at[idx + (cols(o, half),)], dst.at[1])

    AV[...] = jnp.zeros_like(AV)
    H0, HN0, H1, HN1 = (W.at[:, :, :, :, 0 : W.shape[-1] // 2] for W in (W0, WN0, W1, WN1))

    def flat(W):
        return W[...].reshape(4 * G * W.shape[3], W.shape[4])

    for i in range(4 * G):
        extra = HM.shape[3] - MX // (4 * G)
        if extra:
            HM[i // 4, (i // 2) % 2, i % 2, MX // (4 * G) :] = jnp.zeros((extra, HM.shape[4]), BF)
    got_xb = share_half(None, xb_ref, XB)
    full[1, :, :D] = silu(pre_ref[...]).astype(BF)
    PB[0] = full[1, :, cols(me.c, D // 2)]
    got_pb = link.swap(full.at[1, :, cols(o, D // 2)], PB.at[1])

    x = x_ref[...]
    mixed = lambda off, w: mixed_ref[:, off : off + w]
    reset = silu(mixed(D + ZD, VD))
    full[0] = (reset * att_ref[...]).astype(BF)
    GT[0] = full[0, :, cols(me.c, VD // 2)]
    got_gt = link.swap(full.at[0, :, cols(o, VD // 2)], GT.at[1])
    loads["n0"].wait()
    hidden_pre = mixed(D + ZD + VD, D) + dot(full[0], flat(WN0), NT) + vec(vec_ref, OFF_H, D)
    upd = sigmoid(mixed(0, D))
    act = silu(hidden_pre)
    one = x + upd * (act - x)
    gain_one = vec(vec_ref, OFF_G1, D)
    gain_two = vec(vec_ref, OFF_G2, D)
    n_one, r_one = norm(one)
    layer = n_one * gain_one + vec(vec_ref, OFF_S1, D)
    full[2, :, :D] = layer.astype(BF)
    LL[0] = full[2, :, cols(me.c, D // 2)]
    got_ll = link.swap(full.at[2, :, cols(o, D // 2)], LL.at[1])
    loads["w1"].wait()
    expand_pre = dot(full[2, :, :D], flat(W1), NT) + vec(vec_ref, OFF_UP, FF)
    full[3] = silu(expand_pre).astype(BF)
    EX[0] = full[3, :, cols(me.c, FF // 2)]
    got_ex = link.swap(full.at[3, :, cols(o, FF // 2)], EX.at[1])
    loads["n1"].wait()
    two = layer + dot(full[3], flat(WN1), NT) + vec(vec_ref, OFF_DOWN, D)
    n_two, r_two = norm(two)
    block_o[...] = n_two * gain_two + vec(vec_ref, OFF_S2, D)
    cot = cot_ref[...]
    back_two = norm_back(cot, n_two, r_two, gain_two)
    put(AV, OFF_G2, down(cot * n_two))
    put(AV, OFF_S2, down(cot))
    GD[0] = back_two.astype(BF)
    got_gd = link.swap(GD.at[0], GD.at[1])
    put(AV, OFF_DOWN, down(GD[0]))
    GU[0] = (dot(GD[0], flat(WN1)) * silu_grad(expand_pre)).astype(BF)
    got_gu = link.swap(GU.at[0], GU.at[1])
    put(AV, OFF_UP, down(GU[0]))
    into_one = back_two + dot(GU[0], flat(W1))
    put(AV, OFF_G1, down(into_one * n_one))
    put(AV, OFF_S1, down(into_one))
    back_one = norm_back(into_one, n_one, r_one, gain_one)
    GH[0] = (back_one * upd * silu_grad(hidden_pre)).astype(BF)
    got_gh = link.swap(GH.at[0], GH.at[1])
    put(AV, OFF_H, down(GH[0]))
    back_gated = dot(GH[0], flat(WN0))
    GA[me.p] = (back_gated * reset).astype(BF)
    inner = jnp.sum(GA[me.p].astype(F32) * att_ref[...], axis=1, keepdims=True)
    ST[me.p, 0] = lse_ref[...]
    ST[me.p, 1] = as_rows(inner)
    got_ga = link.plane(lambda q: GA.at[me.p], lambda q: GA.at[q])
    got_st = link.plane(lambda q: ST.at[me.p], lambda q: ST.at[q])
    GM[0, :, 0:D] = (back_one * (act - x) * upd * (1.0 - upd)).astype(BF)
    GM[0, :, D + ZD : D + ZD + VD] = (
        back_gated * att_ref[...] * silu_grad(mixed(D + ZD, VD))
    ).astype(BF)
    GM[0, :, D + ZD + VD :] = GH[0]
    tok_o[...] = back_one * (1.0 - upd)
    red = [
        Reduce(me, link, H, R, L)
        for H, R, L in ((HN1, RN1, LN1), (H1, R1, L1), (HN0, RN0, LN0), (H0, R0, L0), (HM, RM, LM))
    ]
    rn1, r1, rn0, r0, rmx = red

    def both(ref):
        return ref[...].reshape(2 * T, ref.shape[-1])

    def grads(H, out, into):
        rhs = both(into)
        for j in range(0, out.shape[-1], 384):
            lhs = out[:, :, j : j + 384].reshape(2 * T, 384)
            into_blocks(H, dot(lhs, rhs, TN), j, out.shape[-1] // (4 * G))

    got_gd()
    got_ex()
    grads(HN1, GD, EX)
    rn1.first()
    got_gu()
    got_ll()
    grads(H1, GU, LL)
    r1.first()
    got_gh()
    got_gt()
    grads(HN0, GH, GT)
    rn1.second()
    rn0.first()
    got_ga()
    got_st()
    kall = k_ref[...].reshape(G * T, ZD)
    for kk in (1, 2, 3, 0):
        i = (me.p + kk) % 4
        probs = jnp.exp(s_ref[i] - as_col(ST[i, 0]))
        back = dot(GA[i], v_ref[...], NT)
        gs = (probs * (back - as_col(ST[i, 1]))).astype(BF)
        P16[i] = probs.astype(BF)
        GS[i] = gs
        QP[i] = dot(gs, kall)
    got_q = link.plane(lambda q: QP.at[q], lambda q: KS.at[q])
    r1.second()
    rn1.third()
    gsall = GS[...].reshape(4 * T, G * T)
    KP[...] = dot(gsall, q_ref[...].reshape(4 * T, ZD), TN).reshape(G, T, ZD)
    got_k = link.line(lambda h: KP.at[h], lambda h: DP.at[h])
    pall = P16[...].reshape(4 * T, G * T)
    gall = GA[...].reshape(4 * T, VD)
    loads["sgv"].wait()
    wide = 512
    for j in range(VD // wide):
        sl = slice(j * wide, (j + 1) * wide)
        dv = dot(pall, gall[:, sl], TN)
        gv = (dv * GV[0, :, sl].astype(F32)).astype(BF)
        GV[0, :, sl] = gv
        put(AV, OFF_V + j * wide, down(gv))
    got_gv = link.swap(GV.at[0], GV.at[1])
    rn0.second()
    loads["w0"].wait()
    for g in range(G):
        DX[g] = dot(GV[0, g * T : (g + 1) * T], flat(W0)).astype(BF)
    got_dx = link.line(lambda h: DX.at[h], lambda h: BP.at[h])
    r1.third()
    got_gv()
    got_xb()
    xball = XB[...].reshape(2 * G * T, D // 2)
    wide = VD // 4
    for j in range(4):
        gvall = GV[:, :, j * wide : (j + 1) * wide].reshape(2 * G * T, wide)
        into_blocks(H0, dot(gvall, xball, TN), j * wide, VD // (4 * G))
    r0.first()
    rn0.third()
    got_q()
    KS[me.p] = QP[me.p]
    DP[me.g] = KP[me.g]
    scaling = ZD ** (-0.5)
    back_q = (KS[0] + KS[1] + KS[2] + KS[3]) * scaling
    got_k()
    back_k = DP[0]
    for g in range(1, G):
        back_k = back_k + DP[g]
    sp = mixed(D, ZD)
    shared = silu(sp)
    put(AV, OFF_QG, down(back_q * shared))
    put(AV, OFF_QG + ZD, down(back_k * shared))
    put(AV, OFF_QS, down(back_q))
    put(AV, OFF_QS + ZD, down(back_k))
    back_shared = back_q * vec(vec_ref, OFF_QG, ZD) + back_k * vec(vec_ref, OFF_QG + ZD, ZD)
    GM[0, :, D : D + ZD] = (back_shared * silu_grad(sp)).astype(BF)
    got_gm = link.swap(GM.at[0], GM.at[1])
    put(AV, OFF_MX, down(GM[0]))
    loads["mx"].wait()
    back_pre = dot(GM[0], WM[...]) * silu_grad(pre_ref[...])
    tok_o[...] += vec(vec_ref, OFF_OM, D) * back_pre
    put(AV, OFF_OM, down(back_pre * x))
    pre_buf = pairbuf
    pre_buf[...] = back_pre
    got_gm()
    got_pb()
    gmall = both(GM)
    pball = both(PB)
    step = MX // 5
    for j in range(5):
        into_blocks(
            HM, dot(gmall[:, j * step : (j + 1) * step], pball, TN), j * step, MX // (4 * G)
        )
    rmx.first()
    r0.second()
    damp, mix, dec, inf, outf = decays_of(avg_ref)
    zero = jnp.zeros((NH, D), F32)
    fin[me.p] = ma_back_first(pre_buf, dec, outf, zero)
    got_fin = link.plane(lambda q: fin.at[me.p], lambda q: fin.at[q])
    diagonals(G, T, GS, prof)
    got_fin()
    whole = power(dec, T)
    tot = fin[3]
    for q in (2, 1, 0):
        tot = whole * tot + fin[q]
    ftot[me.g] = tot
    got_tot = link.line(lambda h: ftot.at[me.g], lambda h: ftot.at[h])
    rmx.second()
    r0.third()
    got_tot()
    whole4 = power(whole, 4)
    leave = zero
    for i in range(G - 1, 0, -1):
        leave = jnp.where(i > me.g, whole4 * leave + ftot[i], leave)
    for q in (3, 2, 1):
        leave = jnp.where(q > me.p, whole * leave + fin[q], leave)
    ma_back(x_ref, pre_buf, keep_ref, leave, dec, inf, outf, tok_o, AV)
    table_rows(G, me, prof, index_ref, AV)
    rmx.third()
    got_av = link.swap(AV, AS)
    got_dx()
    BP[me.g] = DX[me.g]
    for g in range(G):
        tok_o[...] += BP[g].astype(F32)
    finish = []

    def pair_sum(value, buf):
        buf[me.dp // 2] = value
        link.pairs(buf.at[me.dp // 2], lambda d: buf.at[d], count)()
        value = buf[0]
        for d in range(1, count):
            value = value + buf[d]
        return value

    def close(r, F, buf):
        total = r.fourth()
        half = total.shape[-1]
        if count > 1:
            total = pair_sum(total, buf)
        F[:, cols(me.c, half)] = total
        part = F.at[:, cols(me.c, half)]
        s = link.slot()
        link.go(part, part, s, me.sib())
        finish.append(lambda: link.got(F.at[:, cols(o, half)], s))

    close(rn1, FN1, PN1)
    close(r1, F1, P1)
    close(rn0, FN0, PN0)
    got_av()
    AW[...] = AV[...] + AS[...]
    hr = AV.shape[0] // 2
    qr = hr // 4

    def part(ref, q):
        return ref.at[pl.ds(pl.multiple_of(me.c * hr + q * qr, 8), qr), :]

    got_ap = link.plane(lambda q: part(AW, q), lambda q: AP.at[q])
    close(r0, F0, P0)
    got_ap()
    AP[me.p] = AW[pl.ds(pl.multiple_of(me.c * hr + me.p * qr, 8), qr), :]
    AL[me.g] = AP[0] + AP[1] + AP[2] + AP[3]
    got_al = link.line(lambda h: AL.at[me.g], lambda h: AL.at[h])
    close(rmx, FM, PM)
    got_al()
    tot = AL[0]
    for g in range(1, G):
        tot = tot + AL[g]
    if count > 1:
        tot = pair_sum(tot, PA)
    AT[pl.ds(pl.multiple_of(me.c * hr + me.p * qr, 8), qr), :] = tot
    got_as = link.plane(lambda q: part(AT, me.p), lambda q: part(AT, q))
    got_as()
    mine = AT.at[pl.ds(pl.multiple_of(me.c * hr, 8), hr), :]
    theirs = AT.at[pl.ds(pl.multiple_of(o * hr, 8), hr), :]
    s = link.slot()
    link.go(mine, mine, s, me.sib())
    link.got(theirs, s)
    for f in finish:
        f()
    gm_o[...] = FM[...]
    gw_o[0] = F0[...]
    gw_o[1] = F1[...]
    gn_o[0] = FN0[...]
    gn_o[1] = FN1[...]
    sum_o[...] = AT[0:16]
    ma_o[...] = AT[16:64].reshape(3, NH, D)
    link.drain()


def ma_back_first(bp_ref, dec, outf, h):
    n8 = bp_ref.shape[0] // 8

    def step(i, h):
        bs = bp_ref[pl.ds((n8 - 1 - i) * 8, 8), :]
        for r in range(7, -1, -1):
            h = dec * (outf * bs[r : r + 1] + h)
        return h

    return lax.fori_loop(0, n8, step, h)


def ma_back(x_ref, bp_ref, keep_ref, leave, dec, inf, outf, tok_o, AV):
    n8 = x_ref.shape[0] // 8
    wide = 256
    for j in range(D // wide):
        sl = slice(j * wide, (j + 1) * wide)
        d, f, u = dec[:, sl], inf[:, sl], outf[:, sl]

        def step(i, carry):
            h, dd, di, du = carry
            at = n8 - 1 - i
            xs = x_ref[pl.ds(at * 8, 8), sl]
            bs = bp_ref[pl.ds(at * 8, 8), sl]
            states = [keep_ref[at, :, sl]]
            for r in range(8):
                states.append(d * states[-1] + f * xs[r : r + 1])
            rows = [None] * 8
            for r in range(7, -1, -1):
                adj = u * bs[r : r + 1] + h
                dd = dd + adj * states[r]
                di = di + adj * xs[r : r + 1]
                du = du + bs[r : r + 1] * states[r + 1]
                rows[r] = jnp.sum(f * adj, axis=0, keepdims=True)
                h = d * adj
            tok_o[pl.ds(at * 8, 8), sl] += jnp.concatenate(rows, axis=0)
            return h, dd, di, du

        zero = jnp.zeros((NH, wide), F32)
        _, dd, di, du = lax.fori_loop(0, n8, step, (leave[:, sl], zero, zero, zero))
        AV[16 : 16 + NH, sl] = dd
        AV[16 + NH : 16 + 2 * NH, sl] = di
        AV[16 + 2 * NH : 16 + 3 * NH, sl] = du


def diagonals(G, T, GS, prof):
    flip = (
        lax.broadcasted_iota(jnp.int32, (T, T), 0) + lax.broadcasted_iota(jnp.int32, (T, T), 1) == T - 1
    ).astype(F32).astype(BF)
    for i in range(4):
        turned = dot(flip, GS[i])
        for kk in range(G):
            m = 4 * kk - i + 3
            block = jnp.concatenate([turned[:, kk * T : (kk + 1) * T], jnp.zeros((T, T), F32)], axis=1)
            s = jnp.sum(pltpu.roll(block, 0, 1, stride=1, stride_axis=0), axis=0, keepdims=True)
            prof[m : m + 1] += s[:, :T]
            prof[m + 1 : m + 2] += s[:, T:]


def table_rows(G, me, prof, index_ref, AV):
    first_row = me.p - 4 * me.g - 4 + 4 * G
    total = jnp.zeros((NB, 128), F32)
    for r in range(4 * G + 1):
        hit = index_ref[pl.ds(first_row + r, 1), :] == lax.broadcasted_iota(jnp.int32, (NB, 128), 0)
        total = total + jnp.where(hit, prof[r : r + 1], 0.0)
    col = jnp.sum(total, axis=1, keepdims=True)
    put(AV, OFF_TB, as_rows(col)[0:1])


def backward_call(G, count, sizes, x, cot, weights, saved, avg, vv, index):
    T = x.shape[0]
    rm, rw, rn = sizes
    A = jax.ShapeDtypeStruct
    V = pltpu.VMEM
    half = D // 2
    hv = VD // 2
    vm = pl.BlockSpec(memory_space=pltpu.VMEM)
    hbm = pl.BlockSpec(memory_space=pl.ANY)
    S = pltpu.SemaphoreType.DMA
    out_shape = (
        A((T, D), F32), A((T, D), F32), A((rm, D), F32), A((2, rw, D), F32), A((2, rn, VD), F32),
        A((16, D), F32), A((3, NH, D), F32),
    )
    scratch = [
        V((2, T, D), BF), V((2, T, hv), BF), V((2, T, FF), BF), V((2, T, half), BF), V((2, T, D), BF), V((2, T, hv), BF),
        V((2, G * T, VD), BF), V((2, G, T, half), BF), V((2, T, MX), BF), V((2, T, half), BF), V((4, T, VD), BF),
        V((G, 2, 2, rw, D), BF), V((MX, D), BF), V((G, 2, 2, rm, half), BF), V((G, 2, 2, rn, VD), BF), V((G, 2, 2, rw, D), BF), V((G, 2, 2, rn, VD), BF),
        V((3, G, rw, half), BF), V((3, G, rm, half), BF), V((3, G, rn, hv), BF), V((3, G, rw, half), BF), V((3, G, rn, hv), BF),
        V((G, rw, half), BF), V((G, rm, half), BF), V((G, rn, hv), BF), V((G, rw, half), BF), V((G, rn, hv), BF),
        V((rw, D), F32), V((rm, D), F32), V((rn, VD), F32), V((rw, D), F32), V((rn, VD), F32),
        V((4, T, VD), BF), V((4, 2, 8, 128), F32), V((4, T, G * T), BF), V((4, T, G * T), BF),
        V((4, T, ZD), F32), V((4, T, ZD), F32), V((G, T, ZD), F32), V((G, T, D), BF), V((G, T, ZD), F32), V((G, T, D), BF),
        V((4, NH, D), F32), V((G, NH, D), F32), V((T, D), F32),
        V((64, D), F32), V((64, D), F32), V((64, D), F32), V((64, D), F32), V((4, 8, D), F32), V((G, 8, D), F32), V((4 * G + 8, 128), F32),
    ]
    if count > 1:
        scratch += [V((count, r, w), F32) for r, w in ((8, D), (rw, half), (rm, half), (rn, hv), (rw, half), (rn, hv))]
    else:
        scratch += [V((8, 128), F32)] * 6
    slots = 80 + 6 * G + 6 * count
    scratch += [S((slots,)), S((slots,)), S((6,))]
    return pl.pallas_call(
        functools.partial(bwd_kernel, G, count, sizes),
        out_shape=out_shape,
        in_specs=[vm] * 2 + [hbm] * 5 + [vm] * 9 + [hbm] + [vm] * 4,
        out_specs=[vm] * 7,
        scratch_shapes=scratch,
        compiler_params=pltpu.CompilerParams(collective_id=2, has_side_effects=True, vmem_limit_bytes=58 * 2**20),
    )(x, cot, *weights, *saved, avg, vv, index)


def prologue(mixer_weight, widen_weight, narrow_weight, vectors, averager, bias_index):
    n = lax.axis_size("blk")
    mix = padded(mixer_weight.T, 0)
    wid = padded(jnp.swapaxes(widen_weight, 1, 2), 1)
    nar = padded(jnp.swapaxes(narrow_weight, 1, 2), 1)
    avg = jnp.swapaxes(averager, 1, 2)
    index = jnp.pad(bias_index, (0, 1)).reshape(2 * n, 128)
    return mix, wid, nar, avg, vectors.reshape(NVEC // D, D), index


def carried_in(part, axis, combine, identity, reverse):
    count = lax.axis_size(axis)
    place = lax.axis_index(axis)
    ahead = count - 1 - place if reverse else place
    gathered = jax.tree.map(lambda a: lax.all_gather(a, axis), part)
    state = jax.tree.map(lambda a, e: jnp.zeros_like(a) + jnp.asarray(e, a.dtype), part, identity)

    def one(turn, state):
        source = count - 1 - turn if reverse else turn
        return combine(
            state, jax.tree.map(lambda a: lax.dynamic_index_in_dim(a, source, 0, False), gathered)
        )

    return lax.fori_loop(0, ahead, one, state)


def pieces(vectors):
    widths = (MX, VD, D, FF, D, D, D, D, D, D, 2 * ZD, 2 * ZD, NB)
    collected = []
    offset = 0
    for width in widths:
        collected.append(vectors[offset : offset + width])
        offset = offset + width
    return collected


def product(left_side, right_side, pattern):
    return jnp.einsum(pattern, left_side, right_side, preferred_element_type=jnp.float32)


def layer_norm(values, norm_gain, norm_shift):
    centered = values - jnp.mean(values, axis=-1, keepdims=True)
    inverse = lax.rsqrt(jnp.mean(centered * centered, axis=-1, keepdims=True) + EPS_NORM)
    normed = centered * inverse
    return (normed * norm_gain + norm_shift, normed, inverse)


def norm_back_sums(incoming, normed, inverse, norm_gain):
    scaled = incoming * norm_gain
    result = inverse * (
        scaled
        - jnp.mean(scaled, axis=-1, keepdims=True)
        - normed * jnp.mean(scaled * normed, axis=-1, keepdims=True)
    )
    return (result, jnp.sum(incoming * normed, axis=0), jnp.sum(incoming, axis=0))


def running(drive, decays, backward):
    result = drive
    factor = decays
    stride = 1
    total_rows = drive.shape[0]
    while stride < total_rows:
        padding = jnp.zeros((stride,) + drive.shape[1:], jnp.float32)
        if backward:
            shifted = jnp.concatenate([result[stride:], padding], axis=0)
        else:
            shifted = jnp.concatenate([padding, result[:-stride]], axis=0)
        result = result + factor * shifted
        factor = factor * factor
        stride = stride * 2
    return result


def compose(earlier, latter):
    return (earlier[0] * latter[0], latter[0] * earlier[1] + latter[1])


def toeplitz(profile, row_count, column_count):
    width_all = row_count + column_count
    tiled = jnp.tile(profile, row_count)[: row_count * (width_all - 1)]
    return tiled.reshape(row_count, width_all - 1)[:, row_count - 1 :]


def diagonal_sums(matrix):
    row_count, column_count = matrix.shape
    width_all = row_count + column_count
    padded = jnp.pad(matrix, ((0, 0), (row_count - 1, 0)))
    flattened = jnp.pad(padded.reshape(-1), (0, row_count))
    return jnp.sum(flattened.reshape(row_count, width_all), axis=0, dtype=jnp.float32)


def plain_update(weight, gradient, moment, decay_rate):
    moment_new = decay_rate * moment + (1.0 - decay_rate) * (gradient * gradient + EPS_ONE)
    update = gradient * lax.rsqrt(moment_new)
    rms_update = jnp.sqrt(jnp.mean(update * update))
    update = update / jnp.maximum(1.0, rms_update / CLIP_UPDATE)
    rms_weight = jnp.sqrt(jnp.mean(weight * weight))
    return (weight - RATE * jnp.maximum(EPS_TWO, rms_weight) * update, moment_new)


def with_collectives(
    tokens,
    cotangent,
    mixer_weight,
    widen_weight,
    narrow_weight,
    vectors,
    averager,
    bias_index,
    mixer_rows,
    mixer_cols,
    widen_rows,
    widen_cols,
    narrow_rows,
    narrow_cols,
    vector_moment,
    averager_moment,
):
    blocks = lax.axis_size("blk")
    position = lax.axis_index("blk")
    length = tokens.shape[1]
    full_length = length * blocks
    shards = (
        mixer_weight.astype(jnp.bfloat16),
        widen_weight.astype(jnp.bfloat16),
        narrow_weight.astype(jnp.bfloat16),
    )
    mixer_low, widen_low, narrow_low = (
        lax.all_gather(shards[0], "blk", axis=1, tiled=True),
        lax.all_gather(shards[1], "blk", axis=2, tiled=True),
        lax.all_gather(shards[2], "blk", axis=2, tiled=True),
    )
    (
        bias_mixer,
        bias_value,
        bias_hidden,
        bias_expand,
        bias_project,
        gain_one,
        shift_one,
        gain_two,
        shift_two,
        omega_scale,
        qk_gain,
        qk_shift,
        bias_table,
    ) = pieces(vectors)
    damping = jax.nn.sigmoid(averager[0])
    mixing = jax.nn.sigmoid(averager[1])
    decays = 1.0 - damping * mixing
    log_decay = jnp.log(decays)
    inflow = damping * averager[2]
    outflow = averager[3] * NH ** (-0.5)
    inputs = tokens[0]
    drive = inflow[None] * inputs[:, :, None]
    local_states = running(drive, decays, False)
    whole_decay = jnp.exp(log_decay * length)
    identity = (jnp.ones_like(decays), jnp.zeros_like(decays))
    entering = carried_in((whole_decay, local_states[-1]), "blk", compose, identity, False)[1]
    steps_ahead = (jnp.arange(length, dtype=jnp.int32) + 1).astype(jnp.float32)
    states = local_states + jnp.exp(log_decay[None] * steps_ahead[:, None, None]) * entering[None]
    pre_act = jnp.sum(states * outflow[None], axis=2) + omega_scale * inputs
    prime_low = jax.nn.silu(pre_act).astype(jnp.bfloat16)
    mixed_out = jnp.dot(prime_low, mixer_low, preferred_element_type=jnp.float32) + bias_mixer
    update_gate = jax.nn.sigmoid(mixed_out[:, :D])
    shared_pre = mixed_out[:, D : D + ZD]
    reset_pre = mixed_out[:, D + ZD : D + ZD + VD]
    hidden_x = mixed_out[:, D + ZD + VD :]
    shared = jax.nn.silu(shared_pre)
    reset_gate = jax.nn.silu(reset_pre)
    scaling = ZD ** (-0.5)
    queries = ((shared * qk_gain[:ZD] + qk_shift[:ZD]) * scaling).astype(jnp.bfloat16)
    key_rows = (shared * qk_gain[ZD:] + qk_shift[ZD:]).astype(jnp.bfloat16)
    inputs_low = inputs.astype(jnp.bfloat16)
    value_pre = jnp.dot(inputs_low, widen_low[0], preferred_element_type=jnp.float32) + bias_value
    value_rows = jax.nn.silu(value_pre).astype(jnp.bfloat16)
    key_all, value_all = (
        lax.all_gather(key_rows, "blk", axis=0, tiled=True),
        lax.all_gather(value_rows, "blk", axis=0, tiled=True),
    )
    buckets = jnp.arange(NB, dtype=jnp.int32)
    selector = (bias_index[:, None] == buckets[None, :]).astype(jnp.float32)
    bias_row = jnp.concatenate(
        [
            jnp.dot(selector, bias_table, precision=lax.Precision.HIGHEST),
            jnp.zeros((1,), jnp.float32),
        ]
    )
    begin = (blocks - 1 - position) * length
    profile = lax.dynamic_slice_in_dim(bias_row, begin, length + full_length)
    scores = product(queries, key_all, "qc,kc->qk") + toeplitz(profile, length, full_length)
    row_peak = jnp.max(scores, axis=1, keepdims=True)
    log_total = row_peak + jnp.log(jnp.sum(jnp.exp(scores - row_peak), axis=1, keepdims=True))
    softened = jnp.exp(scores - log_total)
    softened_low = softened.astype(jnp.bfloat16)
    attended = jnp.dot(softened_low, value_all, preferred_element_type=jnp.float32)
    gated_low = (reset_gate * attended).astype(jnp.bfloat16)
    hidden_pre = (
        hidden_x
        + jnp.dot(gated_low, narrow_low[0], preferred_element_type=jnp.float32)
        + bias_hidden
    )
    hidden_act = jax.nn.silu(hidden_pre)
    residual_one = inputs + update_gate * (hidden_act - inputs)
    layer_one, normed_one, inverse_one = layer_norm(residual_one, gain_one, shift_one)
    layer_low = layer_one.astype(jnp.bfloat16)
    expand_pre = jnp.dot(layer_low, widen_low[1], preferred_element_type=jnp.float32) + bias_expand
    expand_low = jax.nn.silu(expand_pre).astype(jnp.bfloat16)
    project_two = (
        jnp.dot(expand_low, narrow_low[1], preferred_element_type=jnp.float32) + bias_project
    )
    block_out, normed_two, inverse_two = layer_norm(layer_one + project_two, gain_two, shift_two)
    grad_second, gain_two_grad, shift_two_grad = norm_back_sums(
        cotangent[0], normed_two, inverse_two, gain_two
    )
    project_low = grad_second.astype(jnp.bfloat16)
    grad_down = product(expand_low, project_low, "tf,td->fd")
    expand_grad_low = (
        product(project_low, narrow_low[1], "td,fd->tf") * silu_grad(expand_pre)
    ).astype(jnp.bfloat16)
    grad_up = product(layer_low, expand_grad_low, "td,tf->df")
    grad_layer = grad_second + product(expand_grad_low, widen_low[1], "tf,df->td")
    grad_first, gain_one_grad, shift_one_grad = norm_back_sums(
        grad_layer, normed_one, inverse_one, gain_one
    )
    grad_update = grad_first * (hidden_act - inputs)
    hidden_grad_low = (grad_first * update_gate * silu_grad(hidden_pre)).astype(jnp.bfloat16)
    grad_hidden_weight = product(gated_low, hidden_grad_low, "tv,td->vd")
    grad_gated = product(hidden_grad_low, narrow_low[0], "td,vd->tv")
    grad_reset = grad_gated * attended
    attend_grad_low = (grad_gated * reset_gate).astype(jnp.bfloat16)
    grad_softened = product(attend_grad_low, value_all, "tv,kv->tk")
    row_inner = jnp.sum(softened * grad_softened, axis=1, keepdims=True)
    score_grad_low = (softened * (grad_softened - row_inner)).astype(jnp.bfloat16)
    grad_queries = product(score_grad_low, key_all, "tk,kc->tc")
    profile_grad = diagonal_sums(score_grad_low)
    partial_keys = product(score_grad_low, queries, "tk,tc->kc")
    partial_values = product(softened_low, attend_grad_low, "tk,tv->kv")
    grad_keys, grad_values = (
        lax.psum_scatter(partial_keys, "blk", scatter_dimension=0, tiled=True),
        lax.psum_scatter(partial_values, "blk", scatter_dimension=0, tiled=True),
    )
    grad_shared = grad_queries * scaling * qk_gain[:ZD] + grad_keys * qk_gain[ZD:]
    qk_gain_grad = jnp.concatenate(
        [jnp.sum(grad_queries * scaling * shared, axis=0), jnp.sum(grad_keys * shared, axis=0)]
    )
    qk_shift_grad = jnp.concatenate(
        [jnp.sum(grad_queries * scaling, axis=0), jnp.sum(grad_keys, axis=0)]
    )
    value_grad_low = (grad_values * silu_grad(value_pre)).astype(jnp.bfloat16)
    grad_value_weight = product(inputs_low, value_grad_low, "td,tv->dv")
    mixed_grad_low = jnp.concatenate(
        [
            grad_update * update_gate * (1.0 - update_gate),
            grad_shared * silu_grad(shared_pre),
            grad_reset * silu_grad(reset_pre),
            hidden_grad_low.astype(jnp.float32),
        ],
        axis=1,
    ).astype(jnp.bfloat16)
    grad_mixer_weight = product(prime_low, mixed_grad_low, "td,tm->dm")
    grad_pre = product(mixed_grad_low, mixer_low, "tm,dm->td") * silu_grad(pre_act)
    local_adjoint = running(outflow[None] * grad_pre[:, :, None], decays, True)
    leaving = carried_in((whole_decay, decays * local_adjoint[0]), "blk", compose, identity, True)[
        1
    ]
    steps_behind = (length - 1 - jnp.arange(length, dtype=jnp.int32)).astype(jnp.float32)
    adjoint = local_adjoint + jnp.exp(log_decay[None] * steps_behind[:, None, None]) * leaving[None]
    previous = jnp.concatenate([entering[None], states[:-1]], axis=0)
    grad_decay = jnp.sum(adjoint * previous, axis=0)
    grad_inflow = jnp.sum(adjoint * inputs[:, :, None], axis=0)
    grad_outflow = jnp.sum(grad_pre[:, :, None] * states, axis=0)
    tokens_grad = (
        grad_first * (1.0 - update_gate)
        + product(value_grad_low, widen_low[0], "tv,dv->td")
        + grad_pre * omega_scale
        + jnp.sum(adjoint * inflow[None], axis=2)
    )
    grad_damping = -mixing * grad_decay + averager[2] * grad_inflow
    average_grad = jnp.stack(
        [
            grad_damping * damping * (1.0 - damping),
            -damping * grad_decay * mixing * (1.0 - mixing),
            damping * grad_inflow,
            grad_outflow * NH ** (-0.5),
        ]
    )
    row_grad = lax.dynamic_update_slice(
        jnp.zeros((2 * full_length,), jnp.float32), profile_grad, (begin,)
    )
    table_grad = jnp.dot(row_grad[:-1], selector, precision=lax.Precision.HIGHEST)
    vector_local = jnp.concatenate(
        [
            jnp.sum(mixed_grad_low, axis=0, dtype=jnp.float32),
            jnp.sum(value_grad_low, axis=0, dtype=jnp.float32),
            jnp.sum(hidden_grad_low, axis=0, dtype=jnp.float32),
            jnp.sum(expand_grad_low, axis=0, dtype=jnp.float32),
            jnp.sum(project_low, axis=0, dtype=jnp.float32),
            gain_one_grad,
            shift_one_grad,
            gain_two_grad,
            shift_two_grad,
            jnp.sum(grad_pre * inputs, axis=0),
            qk_gain_grad,
            qk_shift_grad,
            table_grad,
        ]
    )
    full_grads = (
        grad_mixer_weight,
        jnp.stack([grad_value_weight, grad_up]),
        jnp.stack([grad_hidden_weight, grad_down]),
    )
    column_grads = (
        lax.psum_scatter(
            full_grads[0].astype(jnp.bfloat16), "blk", scatter_dimension=1, tiled=True
        ).astype(jnp.float32),
        lax.psum_scatter(
            full_grads[1].astype(jnp.bfloat16), "blk", scatter_dimension=2, tiled=True
        ).astype(jnp.float32),
        lax.psum_scatter(
            full_grads[2].astype(jnp.bfloat16), "blk", scatter_dimension=2, tiled=True
        ).astype(jnp.float32),
    )
    mixer_part, widen_part, narrow_part = (
        lax.psum(column_grads[0].astype(jnp.bfloat16), "dp").astype(jnp.float32),
        lax.psum(column_grads[1].astype(jnp.bfloat16), "dp").astype(jnp.float32),
        lax.psum(column_grads[2].astype(jnp.bfloat16), "dp").astype(jnp.float32),
    )
    vector_sum, average_sum = lax.psum((vector_local, average_grad), ("dp", "blk"))
    stacks = (mixer_part[None], widen_part, narrow_part)
    masters = (mixer_weight[None], widen_weight, narrow_weight)
    rows_old = (mixer_rows[None], widen_rows, narrow_rows)
    columns_old = (mixer_cols[None], widen_cols, narrow_cols)
    column_total = (MX, VD, D)
    local_square = jnp.sum(vector_sum * vector_sum) + jnp.sum(average_sum * average_sum)
    grad_squares = tuple((jnp.sum(matrix * matrix, axis=(1, 2)) for matrix in stacks))
    weight_squares = tuple((jnp.sum(matrix * matrix, axis=(1, 2)) for matrix in masters))
    decay_rate = 1.0 - STEP ** (-0.8)
    summed = lax.psum(grad_squares + weight_squares, "blk")
    clip_norm = jnp.sqrt(
        jnp.sum(summed[0]) + jnp.sum(summed[1]) + jnp.sum(summed[2]) + local_square
    )
    factor = jnp.minimum(1.0, CLIP_NORM / clip_norm)
    clipped = tuple((matrix * factor for matrix in stacks))
    squares = tuple((matrix * matrix + EPS_ONE for matrix in clipped))
    row_sums = lax.psum(tuple((jnp.sum(square_part, axis=2) for square_part in squares)), "blk")
    column_means = tuple((jnp.mean(square_part, axis=1) for square_part in squares))
    weight_total = summed[3:6]
    rows_new = tuple(
        (
            decay_rate * rows_old[member]
            + (1.0 - decay_rate) * row_sums[member] / column_total[member]
            for member in range(3)
        )
    )
    columns_new = tuple(
        (
            decay_rate * columns_old[member] + (1.0 - decay_rate) * column_means[member]
            for member in range(3)
        )
    )
    updates = tuple(
        (
            clipped[member]
            * lax.rsqrt(
                rows_new[member][:, :, None]
                * columns_new[member][:, None, :]
                / jnp.mean(rows_new[member], axis=1)[:, None, None]
            )
            for member in range(3)
        )
    )
    update_squares = lax.psum(
        tuple((jnp.sum(update * update, axis=(1, 2)) for update in updates)), "blk"
    )
    new_list = []
    for member in range(3):
        entries = rows_old[member].shape[1] * column_total[member]
        rms_update = jnp.sqrt(update_squares[member] / entries)
        bounded = updates[member] / jnp.maximum(1.0, rms_update / CLIP_UPDATE)[:, None, None]
        rms_weight = jnp.sqrt(weight_total[member] / entries)
        new_list.append(
            masters[member] - RATE * jnp.maximum(EPS_TWO, rms_weight)[:, None, None] * bounded
        )
    vector_grad = vector_sum * factor
    averager_grad = average_sum * factor
    vector_new, moment_vector = plain_update(vectors, vector_grad, vector_moment, decay_rate)
    averager_new, moment_averager = plain_update(
        averager, averager_grad, averager_moment, decay_rate
    )
    return (
        block_out[None],
        tokens_grad[None],
        clipped[0][0],
        clipped[1],
        clipped[2],
        vector_grad,
        averager_grad,
        new_list[0][0],
        new_list[1],
        new_list[2],
        vector_new,
        averager_new,
        rows_new[0][0],
        columns_new[0][0],
        rows_new[1],
        columns_new[1],
        rows_new[2],
        columns_new[2],
        moment_vector,
        moment_averager,
        clip_norm,
    )


def matrices(G, gm_ref, gw_ref, gn_ref, wm_ref, ww_ref, wn_ref):
    r0, r1, r2 = (t // (4 * G) for t in (MX, VD, D))
    return [
        (lambda: gm_ref[0:r0], lambda: wm_ref[0:r0], MX, D),
        (lambda: gw_ref[0, 0:r1], lambda: ww_ref[0, 0:r1], VD, D),
        (lambda: gw_ref[1, 0:r1], lambda: ww_ref[1, 0:r1], VD, D),
        (lambda: gn_ref[0, 0:r2], lambda: wn_ref[0, 0:r2], D, VD),
        (lambda: gn_ref[1, 0:r2], lambda: wn_ref[1, 0:r2], D, VD),
    ]


def raw_averager(avg, ma_ref):
    damp = sigmoid(avg[0])
    mix = sigmoid(avg[1])
    d_dec, d_inf, d_out = ma_ref[0], ma_ref[1], ma_ref[2]
    return [
        (-mix * d_dec + avg[2] * d_inf) * damp * (1.0 - damp),
        -damp * d_dec * mix * (1.0 - mix),
        damp * d_inf,
        d_out * NH ** (-0.5),
    ]


def stat_kernel(
    G,
    gm_ref, gw_ref, gn_ref, sum_ref, ma_ref, wm_ref, ww_ref, wn_ref, rm_ref, rw_ref, rn_ref, cm_ref, cw_ref, cn_ref, avg_ref,
    rm_o, rw_o, rn_o, cm_o, cw_o, cn_o, scal_o,
    rp, rl, up, ul, ssem, rsem,
):
    me = Place(G)
    link = Link(me, ssem, rsem)
    peers = []
    for k in range(1, G):
        peers.append(me.at(me.line(k), me.b, me.a))
    for k in range(1, 4):
        q = me.plane(k)
        peers.append(me.at(me.g, q // 2, q % 2))
    greet(me, peers)

    def allsum(value, pb, lb):
        pb[me.p] = value
        link.plane(lambda q: pb.at[me.p], lambda q: pb.at[q])()
        lb[me.g] = pb[0] + pb[1] + pb[2] + pb[3]
        link.line(lambda h: lb.at[me.g], lambda h: lb.at[h])()
        out = lb[0]
        for g in range(1, G):
            out = out + lb[g]
        return out

    rate = 1.0 - STEP ** (-0.8)
    mats = matrices(G, gm_ref, gw_ref, gn_ref, wm_ref, ww_ref, wn_ref)
    olds = [
        (rm_ref[0:1], cm_ref[...].T), (rw_ref[0:1], cw_ref[0:1].T), (rw_ref[1:2], cw_ref[1:2].T),
        (rn_ref[0:1], cn_ref[0:1].T), (rn_ref[1:2], cn_ref[1:2].T),
    ]
    lanes = lax.broadcasted_iota(jnp.int32, (1, D), 1)
    rows, cs, extra = [], [], jnp.zeros((1, D), F32)
    for i, (g, w, _, width) in enumerate(mats):
        sq = g()
        sq = sq * sq
        s = jnp.sum(sq, axis=0, keepdims=True)
        for j in range(width // D):
            rows.append(s[:, j * D : (j + 1) * D])
        cs.append(jnp.sum(sq, axis=1, keepdims=True))
        wv = w()
        extra = jnp.where(lanes == i, jnp.sum(wv * wv), extra)
    rows.append(extra)
    small = jnp.sum(sum_ref[...] * sum_ref[...])
    for v in raw_averager([avg_ref[i] for i in range(4)], ma_ref):
        small = small + jnp.sum(v * v)
    tot = allsum(jnp.concatenate(rows, axis=0), rp, rl)
    norm = jnp.sqrt(jnp.sum(tot[0:7]) + small)
    factor = jnp.minimum(1.0, CLIP_NORM / norm)
    at = 0
    squares = jnp.zeros((1, 128), F32)
    means = jnp.zeros((1, 128), F32)
    lane = lanes[:, :128]
    for i, (g, w, total, width) in enumerate(mats):
        ro, co = olds[i]
        row = jnp.concatenate([tot[at + j : at + j + 1] for j in range(width // D)], axis=1)
        at += width // D
        rnew = rate * ro + (1.0 - rate) * (factor * factor * row / total + EPS_ONE)
        cnew = rate * co + (1.0 - rate) * (factor * factor * cs[i] / width + EPS_ONE)
        mean = jnp.sum(rnew) / width
        u = factor * g() * lax.rsqrt(rnew * cnew / mean)
        squares = jnp.where(lane == i, jnp.sum(u * u), squares)
        means = jnp.where(lane == i, mean, means)
        ref, k = ((rm_o, 0), (rw_o, 0), (rw_o, 1), (rn_o, 0), (rn_o, 1))[i]
        ref[k : k + 1] = rnew
        ref, k = ((cm_o, 0), (cw_o, 0), (cw_o, 1), (cn_o, 0), (cn_o, 1))[i]
        ref[k : k + 1] = cnew.T
    sums = allsum(jnp.broadcast_to(squares, (8, 128)), up, ul)
    scal_o[0:1] = sums[0:1]
    scal_o[1:2] = tot[7:8, :128]
    scal_o[2:3] = means
    scal_o[3:4] = jnp.full((1, 128), norm, F32)
    scal_o[4:5] = jnp.full((1, 128), factor, F32)
    scal_o[5:8] = jnp.zeros((3, 128), F32)
    link.drain()


def step_kernel(
    G,
    gm_ref, gw_ref, gn_ref, sum_ref, ma_ref, wm_ref, ww_ref, wn_ref, rm_ref, rw_ref, rn_ref, cm_ref, cw_ref, cn_ref, scal_ref,
    vec_ref, vmom_ref, avg_ref, amom_ref, block_ref, tok_ref,
    gm_o, gw_o, gn_o, vg_o, ag_o, nm_o, nw_o, nn_o, nv_o, na_o, rm_o, cm_o, rw_o, cw_o, rn_o, cn_o, vmom_o, amom_o, clip_o,
    block_o, tok_o,
    s96, sems,
):
    cps = [pltpu.make_async_copy(block_ref, block_o, sems.at[0]), pltpu.make_async_copy(tok_ref, tok_o, sems.at[1])]
    for cp in cps:
        cp.start()
    rate = 1.0 - STEP ** (-0.8)
    lane = lax.broadcasted_iota(jnp.int32, (1, 128), 1)

    def scalar(row, i):
        return jnp.sum(jnp.where(lane == i, scal_ref[row : row + 1], 0.0))

    factor = scalar(4, 0)
    clip_o[...] = scal_ref[3:4, 0:1]
    rm_o[...] = rm_ref[...]
    rw_o[...] = rw_ref[...]
    rn_o[...] = rn_ref[...]
    cm_o[...] = cm_ref[...]
    cw_o[...] = cw_ref[...]
    cn_o[...] = cn_ref[...]
    mats = matrices(G, gm_ref, gw_ref, gn_ref, wm_ref, ww_ref, wn_ref)
    stats = [
        (rm_ref[0:1], cm_ref[...].T, gm_o, nm_o, None), (rw_ref[0:1], cw_ref[0:1].T, gw_o, nw_o, 0),
        (rw_ref[1:2], cw_ref[1:2].T, gw_o, nw_o, 1), (rn_ref[0:1], cn_ref[0:1].T, gn_o, nn_o, 0),
        (rn_ref[1:2], cn_ref[1:2].T, gn_o, nn_o, 1),
    ]
    for i, (g, w, total, width) in enumerate(mats):
        rnew, cnew, go, no, k = stats[i]
        entries = total * width
        rms_u = jnp.sqrt(scalar(0, i) / entries)
        rms_w = jnp.sqrt(scalar(1, i) / entries)
        scale = RATE * jnp.maximum(EPS_TWO, rms_w) / jnp.maximum(1.0, rms_u / CLIP_UPDATE)
        gv = factor * g()
        new = w() - scale * (gv * lax.rsqrt(rnew * cnew / scalar(2, i)))
        if k is None:
            go[...] = gv
            no[...] = new
        else:
            go[k] = gv
            no[k] = new
    for r in range(16):
        for j in range(D // 128):
            s96[r * (D // 128) + j : r * (D // 128) + j + 1] = sum_ref[r : r + 1, j * 128 : (j + 1) * 128]
    gv = factor * s96[...]
    vg_o[...] = gv
    mom = rate * vmom_ref[...] + (1.0 - rate) * (gv * gv + EPS_ONE)
    vmom_o[...] = mom
    u = gv * lax.rsqrt(mom)
    rms_u = jnp.sqrt(jnp.sum(u * u) / NVEC)
    wv = vec_ref[...]
    rms_w = jnp.sqrt(jnp.sum(wv * wv) / NVEC)
    nv_o[...] = wv - RATE * jnp.maximum(EPS_TWO, rms_w) * (u / jnp.maximum(1.0, rms_u / CLIP_UPDATE))
    avg = [avg_ref[i] for i in range(4)]
    raw = raw_averager(avg, ma_ref)
    us, su, sw = [], 0.0, 0.0
    for i in range(4):
        gv = factor * raw[i]
        ag_o[i] = gv
        mom = rate * amom_ref[i] + (1.0 - rate) * (gv * gv + EPS_ONE)
        amom_o[i] = mom
        u = gv * lax.rsqrt(mom)
        us.append(u)
        su = su + jnp.sum(u * u)
        sw = sw + jnp.sum(avg[i] * avg[i])
    count = 4 * D * NH
    scale = RATE * jnp.maximum(EPS_TWO, jnp.sqrt(sw / count)) / jnp.maximum(1.0, jnp.sqrt(su / count) / CLIP_UPDATE)
    for i in range(4):
        na_o[i] = avg[i] - scale * us[i]
    for cp in cps:
        cp.wait()


def stat_call(G, grads, masters, rows, cols, avg):
    A = jax.ShapeDtypeStruct
    V = pltpu.VMEM
    S = pltpu.SemaphoreType.DMA
    vm = pl.BlockSpec(memory_space=pltpu.VMEM)
    r0, r1, r2 = (t // (4 * G) for t in (MX, VD, D))
    slots = 4 * (3 + G)
    return pl.pallas_call(
        functools.partial(stat_kernel, G),
        out_shape=(
            A((1, D), F32), A((2, D), F32), A((2, VD), F32), A((1, r0), F32), A((2, r1), F32), A((2, r2), F32), A((8, 128), F32),
        ),
        in_specs=[vm] * 15,
        out_specs=[vm] * 7,
        scratch_shapes=[
            V((4, 8, D), F32), V((G, 8, D), F32), V((4, 8, 128), F32), V((G, 8, 128), F32), S((slots,)), S((slots,)),
        ],
        compiler_params=pltpu.CompilerParams(collective_id=3, has_side_effects=True, vmem_limit_bytes=56 * 2**20),
    )(*grads, *masters, *rows, *cols, avg)


def step_call(G, grads, masters, stats, vectors, vmom, avg, amom, block, tok):
    A = jax.ShapeDtypeStruct
    V = pltpu.VMEM
    vm = pl.BlockSpec(memory_space=pltpu.VMEM)
    hbm = pl.BlockSpec(memory_space=pl.ANY)
    r0, r1, r2 = (t // (4 * G) for t in (MX, VD, D))
    avgs, vecs = A((4, NH, D), F32), A((NVEC // 128, 128), F32)
    out_shape = (
        A((r0, D), F32), A((2, r1, D), F32), A((2, r2, VD), F32), vecs, avgs,
        A((r0, D), F32), A((2, r1, D), F32), A((2, r2, VD), F32), vecs, avgs,
        A((1, D), F32), A((1, r0), F32), A((2, D), F32), A((2, r1), F32), A((2, VD), F32), A((2, r2), F32),
        vecs, avgs, A((1, 1), F32), A(block.shape, F32), A(tok.shape, F32),
    )
    return pl.pallas_call(
        functools.partial(step_kernel, G),
        out_shape=out_shape,
        in_specs=[vm] * 19 + [hbm] * 2,
        out_specs=[vm] * 19 + [hbm] * 2,
        scratch_shapes=[V((NVEC // 128, 128), F32), pltpu.SemaphoreType.DMA((2,))],
        compiler_params=pltpu.CompilerParams(vmem_limit_bytes=56 * 2**20),
    )(*grads, *masters, *stats, vectors, vmom, avg, amom, block, tok)


def on_device(
    tokens, cotangent, mixer_weight, widen_weight, narrow_weight, vectors, averager, bias_index,
    mixer_rows, mixer_cols, widen_rows, widen_cols, narrow_rows, narrow_cols, vector_moment, averager_moment,
):
    G = lax.axis_size("blk") // 4
    count = lax.axis_size("dp") // 2
    mix, wid, nar, avg, vv, index = prologue(
        mixer_weight, widen_weight, narrow_weight, vectors, averager, bias_index
    )
    w0, mx, n0, w1, n1, *saved = forward_call(G, tokens[0], wid, mix, nar, avg, vv, index)
    sizes = (mix.shape[0], wid.shape[1], nar.shape[1])
    whole = (w0, mx, n0, w1, n1)
    block, tok, *grads = backward_call(
        G, count, sizes, tokens[0], cotangent[0], whole, saved, avg, vv, index
    )
    stats = stat_call(
        G, grads, (mix, wid, nar), (mixer_rows[None], widen_rows, narrow_rows),
        (mixer_cols[None], widen_cols, narrow_cols), avg,
    )
    out = step_call(
        G, grads, (mix, wid, nar), stats, vectors.reshape(NVEC // 128, 128),
        vector_moment.reshape(NVEC // 128, 128), avg, jnp.swapaxes(averager_moment, 1, 2), block, tok,
    )
    gm, gw, gn, vg, ag, nm, nw, nn, nv, na, rm, cm, rw, cw, rn, cn, vmom, amom, clip, block, tok = out
    ag, na, amom, gw, gn, nw, nn = (jnp.swapaxes(v, 1, 2) for v in (ag, na, amom, gw, gn, nw, nn))
    gm, nm = gm.T, nm.T
    return (
        block[None], tok[None], gm, gw, gn, vg.reshape(NVEC), ag, nm, nw, nn, nv.reshape(NVEC), na,
        rm[0], cm[0], rw, cw, rn, cn, vmom.reshape(NVEC), amom, clip[0, 0],
    )


def solution(mesh):
    in_specs = (
        P("dp", "blk", None), P("dp", "blk", None), P(None, "blk"), P(None, None, "blk"), P(None, None, "blk"),
        P(), P(), P(), P(), P("blk"), P(), P(None, "blk"), P(), P(None, "blk"), P(), P(),
    )
    out_specs = (
        P("dp", "blk", None), P("dp", "blk", None), P(None, "blk"), P(None, None, "blk"), P(None, None, "blk"),
        P(), P(), P(None, "blk"), P(None, None, "blk"), P(None, None, "blk"), P(), P(), P(), P("blk"), P(),
        P(None, "blk"), P(), P(None, "blk"), P(), P(), P(),
    )
    small = mesh.shape["dp"] % 2 == 0 and mesh.shape["blk"] in (8, 16)
    body = on_device if small else with_collectives
    return jax.shard_map(
        body, mesh=mesh, in_specs=in_specs, out_specs=out_specs, check_vma=False
    )
```

```python
import functools
import jax
import jax.numpy as jnp
from jax import lax
from jax.experimental import pallas as pl
from jax.experimental.pallas import tpu as pltpu
from jax.sharding import PartitionSpec as P

D = 768
ZD = 128
VD = 1536
FF = 1536
NH = 16
NB = 128
STEP = 10
MX = 3200
EPS_NORM = 1e-05
EPS_ONE = 1e-30
EPS_TWO = 0.001
CLIP_NORM = 1.0
CLIP_UPDATE = 1.0
RATE = 0.5

OFF_MX = 0
OFF_V = MX
OFF_H = OFF_V + VD
OFF_UP = OFF_H + D
OFF_DOWN = OFF_UP + FF
OFF_G1 = OFF_DOWN + D
OFF_S1 = OFF_G1 + D
OFF_G2 = OFF_S1 + D
OFF_S2 = OFF_G2 + D
OFF_OM = OFF_S2 + D
OFF_QG = OFF_OM + D
OFF_QS = OFF_QG + 2 * ZD
OFF_TB = OFF_QS + 2 * ZD
NVEC = OFF_TB + NB

MESH = pl.DeviceIdType.MESH
BF = jnp.bfloat16
F32 = jnp.float32
NN = (((1,), (0,)), ((), ()))
NT = (((1,), (1,)), ((), ()))
TN = (((0,), (0,)), ((), ()))


def dot(a, b, dims=NN):
    return lax.dot_general(a, b, dims, preferred_element_type=F32)


def sigmoid(v):
    return jax.nn.sigmoid(v)


def silu(v):
    return v * sigmoid(v)


def silu_grad(v):
    s = sigmoid(v)
    return s * (1.0 + v * (1.0 - s))


class Place:
    def __init__(self, lines):
        self.lines = lines
        self.dp = lax.axis_index("dp")
        blk = lax.axis_index("blk")
        self.blk = blk
        self.c = self.dp % 2
        self.g = blk // 4
        self.p = blk % 4
        self.b = self.p // 2
        self.a = self.p % 2
        self.na = 1 - self.a
        self.nb = 1 - self.b

    def sib(self):
        return (self.dp + 1 - 2 * self.c, self.blk)

    def at(self, g, b, a):
        return (self.dp, g * 4 + b * 2 + a)

    def line(self, k):
        return (self.g + k) % self.lines

    def plane(self, k):
        return (self.p + k) % 4

    def pick(self, first, second):
        return first + self.c * (second - first)


def vec(ref, off, width):
    rows = range(off // 128, (off + width) // 128)
    return jnp.concatenate([ref[r : r + 1] for r in rows], axis=1)


def greet(others):
    bar = pltpu.get_barrier_semaphore()
    for dev in others:
        pl.semaphore_signal(bar, inc=1, device_id=dev, device_id_type=MESH)


def greeted(others):
    pl.semaphore_wait(pltpu.get_barrier_semaphore(), len(others))


def close_peers(me):
    out = [me.sib()]
    for k in range(1, me.lines):
        out.append(me.at(me.line(k), me.b, me.a))
    for k in range(1, 4):
        q = me.plane(k)
        out.append(me.at(me.g, q // 2, q % 2))
    return out


def rcopy(src, dst, ssem, rsem, dev):
    return pltpu.make_async_remote_copy(
        src_ref=src, dst_ref=dst, send_sem=ssem, recv_sem=rsem, device_id=dev, device_id_type=MESH
    )


class Gather:
    def __init__(self, me, W, ssem, rsem):
        self.me, self.W, self.ssem, self.rsem = me, W, ssem, rsem
        self.half = W.shape[-1] // 2
        self.G = me.lines
        self.started = []
        self.maybe = []
        self.chained = set()
        self.by_plane = False

    def one(self, g, b, a, c):
        return self.W.at[g, b, a, :, pl.ds(pl.multiple_of(c * self.half, 128), self.half)]

    def go(self, src, slot, dev):
        cp = rcopy(src, src, self.ssem.at[slot], self.rsem.at[slot], dev)
        cp.start()
        self.started.append(cp)

    def await_in(self, ref, slot):
        rcopy(ref, ref, self.ssem.at[slot], self.rsem.at[slot], self.me.sib()).wait_recv()

    def near(self, j):
        me, G = self.me, self.G
        if j == 0:
            return me.g
        up = j - 1 + (me.g <= j - 1).astype(jnp.int32)
        down = G - j - (me.g >= G - j).astype(jnp.int32)
        low = (me.g < G // 2).astype(jnp.int32)
        return low * up + (1 - low) * down

    def along(self, h, way):
        me = self.me
        to = me.g + way
        up = jnp.asarray(way > 0, jnp.int32)
        ok = jnp.logical_and(to >= 0, to < self.G)
        src = self.one(h, me.b, me.a, me.c)
        cp = rcopy(
            src, src, self.ssem.at[8 * self.G + h + self.G * up], self.rsem.at[h], me.at(jnp.clip(to, 0, self.G - 1), me.b, me.a)
        )
        pl.when(ok)(cp.start)
        self.maybe.append((ok, cp))

    def z(self):
        self.along(self.me.g, 1)
        self.along(self.me.g, -1)

    def chain(self, j):
        if j > 0 and j not in self.chained:
            h = self.near(j)
            self.await_in(self.one(h, self.me.b, self.me.a, self.me.c), h)
            self.along(h, 2 * (h < self.me.g).astype(jnp.int32) - 1)
            self.chained.add(j)

    def first(self, j):
        me, G = self.me, self.G
        h = self.near(j)
        src = self.one(h, me.b, me.a, me.c)
        self.chain(j)
        self.go(src, G + h, me.at(me.g, me.b, me.na))
        self.go(src, 2 * G + h, me.at(me.g, me.nb, me.a))
        if j > 0:
            self.go(src, 4 * G + h, me.sib())

    def second(self, j):
        me, G = self.me, self.G
        h = self.near(j)
        x = self.one(h, me.b, me.na, me.c)
        y = self.one(h, me.nb, me.a, me.c)
        self.await_in(x, G + h)
        self.await_in(y, 2 * G + h)
        fwd = self.one(h, me.pick(me.b, me.nb), me.pick(me.na, me.a), me.c)
        self.go(fwd, 3 * G + h, me.at(me.g, me.pick(me.nb, me.b), me.pick(me.a, me.na)))
        self.go(x, 5 * G + h, me.sib())
        self.go(y, 6 * G + h, me.sib())

    def third(self, j):
        me, G = self.me, self.G
        h = self.near(j)
        d = self.one(h, me.nb, me.na, me.c)
        self.await_in(d, 3 * G + h)
        self.go(d, 7 * G + h, me.sib())

    def done(self):
        me, G = self.me, self.G
        o = 1 - me.c
        for j in range(G):
            h = self.near(j)
            if j > 0 and self.by_plane:
                self.await_in(self.bundle(h, o), 4 * G + h)
                continue
            if j > 0:
                self.await_in(self.one(h, me.b, me.a, o), 4 * G + h)
            self.await_in(self.one(h, me.b, me.na, o), 5 * G + h)
            self.await_in(self.one(h, me.nb, me.a, o), 6 * G + h)
            self.await_in(self.one(h, me.nb, me.na, o), 7 * G + h)

    def bundle(self, h, c):
        return self.W.at[h, :, :, :, pl.ds(pl.multiple_of(c * self.half, 128), self.half)]

    def bundle_along(self, h, way):
        me = self.me
        to = me.g + way
        up = jnp.asarray(way > 0, jnp.int32)
        ok = jnp.logical_and(to >= 0, to < self.G)
        src = self.bundle(h, me.c)
        cp = rcopy(
            src, src, self.ssem.at[8 * self.G + h + self.G * up], self.rsem.at[h], me.at(jnp.clip(to, 0, self.G - 1), me.b, me.a)
        )
        pl.when(ok)(cp.start)
        self.maybe.append((ok, cp))

    def bundle_out(self):
        self.by_plane = True
        self.bundle_along(self.me.g, 1)
        self.bundle_along(self.me.g, -1)

    def bundle_in(self, j):
        me, G = self.me, self.G
        h = self.near(j)
        src = self.bundle(h, me.c)
        self.await_in(src, h)
        self.bundle_along(h, 2 * (h < me.g).astype(jnp.int32) - 1)
        self.go(src, 4 * G + h, me.sib())

    def drain(self):
        for cp in self.started:
            cp.wait_send()
        for ok, cp in self.maybe:
            pl.when(ok)(cp.wait_send)
        self.started, self.maybe = [], []


def gather_slots(G):
    return 10 * G


def decays_of(avg_ref):
    damp = sigmoid(avg_ref[0])
    mix = sigmoid(avg_ref[1])
    dec = 1.0 - damp * mix
    return damp, mix, dec, damp * avg_ref[2], avg_ref[3] * NH ** (-0.5)


def power(v, n):
    while n > 1:
        v = v * v
        n = n // 2
    return v


def ma_pass(x_ref, h, dec, inf, outf, pre_ref, keep=None):
    def step(i, h):
        if keep is not None:
            keep[i] = h
        xs = x_ref[pl.ds(i * 8, 8), :]
        rows = []
        for r in range(8):
            h = dec * h + inf * xs[r : r + 1]
            if pre_ref is not None:
                rows.append(jnp.sum(outf * h, axis=0, keepdims=True))
        if pre_ref is not None:
            pre_ref[pl.ds(i * 8, 8), :] = jnp.concatenate(rows, axis=0)
        return h

    return lax.fori_loop(0, x_ref.shape[0] // 8, step, h)


def toeplitz_block(bias_ref, m):
    w = jnp.concatenate([bias_ref[pl.ds(m, 1), :], bias_ref[pl.ds(m + 1, 1), :]], axis=1)
    return pltpu.roll(jnp.broadcast_to(w, (128, 256)), 1, 1, stride=1, stride_axis=0)[:, 128:]


def as_rows(col):
    return jnp.broadcast_to(col, (128, 128)).T[0:8]


def as_col(rows):
    return jnp.broadcast_to(rows[0:1], (128, 128)).T[:, 0:1]


def attend_block(G, T, me, i, q_o, kall, v_o, brow, s_o, ob, lout, att_o):
    s = dot(q_o[i], kall, NT)
    tops = []
    for kk in range(G):
        m = 4 * kk - i + 3
        tops.append(toeplitz_block(brow, m))
    s = s + jnp.concatenate(tops, axis=1)
    s_o[i] = s
    top = jnp.max(s, axis=1, keepdims=True)
    e = jnp.exp(s - top)
    tot = jnp.sum(e, axis=1, keepdims=True)
    o = dot(e.astype(BF), v_o[...]) / tot
    if att_o is None:
        ob[i] = o.astype(BF)
    else:
        att_o[...] = o
    lout[i] = as_rows(top + jnp.log(tot))


class Link:
    def __init__(self, me, ssem, rsem):
        self.me, self.ssem, self.rsem = me, ssem, rsem
        self.used = 0
        self.started = []

    def slot(self, count=1):
        self.used += count
        return self.used - count

    def go(self, src, dst, slot, dev, sent=None):
        cp = rcopy(src, dst, self.ssem.at[slot if sent is None else sent], self.rsem.at[slot], dev)
        cp.start()
        self.started.append(cp)

    def got(self, ref, slot):
        rcopy(ref, ref, self.ssem.at[slot], self.rsem.at[slot], self.me.sib()).wait_recv()

    def drain(self):
        for cp in self.started:
            cp.wait_send()
        self.started = []

    def swap(self, src, dst):
        s = self.slot()
        self.go(src, dst, s, self.me.sib())
        return lambda: self.got(dst, s)

    def plane(self, src, dst):
        me = self.me
        slots = [self.slot() for _ in range(3)]
        for k in range(1, 4):
            q = (me.p + k) % 4
            self.go(src(q), dst(me.p), slots[k - 1], me.at(me.g, q // 2, q % 2))

        def wait():
            for k in range(1, 4):
                self.got(dst((me.p + 4 - k) % 4), slots[k - 1])

        return wait

    def line(self, src, dst):
        me, G = self.me, self.me.lines
        slots = [self.slot() for _ in range(G - 1)]
        for k in range(1, G):
            h = (me.g + k) % G
            self.go(src(h), dst(me.g), slots[k - 1], me.at(h, me.b, me.a))

        def wait():
            for k in range(1, G):
                self.got(dst((me.g + G - k) % G), slots[k - 1])

        return wait

    def pairs(self, src, dst, count):
        me = self.me
        slots = [self.slot() for _ in range(count - 1)]
        for k in range(1, count):
            d = (me.dp // 2 + k) % count
            self.go(src, dst(me.dp // 2), slots[k - 1], (2 * d + me.c, me.blk))

        def wait():
            for k in range(1, count):
                self.got(dst((me.dp // 2 + count - k) % count), slots[k - 1])

        return wait


class Reduce:
    def __init__(self, me, link, near, H, R, RL):
        self.me, self.link, self.near, self.H, self.R, self.RL = me, link, near, H, R, RL
        self.base = link.slot(6 * me.lines)
        self.by_plane = False
        self.s = (me.pick(me.nb, me.b), me.pick(me.a, me.na))
        self.m = (me.pick(me.b, me.nb), me.pick(me.na, me.a))

    def at(self, h):
        return 0 if self.by_plane else h

    def send(self, h, place, kind, to):
        self.link.go(
            self.H.at[h, place[0], place[1]], self.R.at[kind, self.at(h)], self.base + kind * self.me.lines + h,
            self.me.at(self.me.g, to[0], to[1]),
        )

    def got(self, h, kind):
        self.link.got(self.R.at[kind, self.at(h)], self.base + kind * self.me.lines + h)

    def add(self, h, place, kinds):
        total = self.H[h, place[0], place[1]].astype(F32)
        for kind in kinds:
            total = total + self.R[kind, self.at(h)].astype(F32)
        self.H[h, place[0], place[1]] = total.astype(BF)

    def behind(self, j):
        self.send(self.near(j), (self.me.nb, self.me.na), 0, self.s)

    def theirs(self, j):
        self.send(self.near(j), self.s, 1, self.s)

    def passed(self, j):
        h = self.near(j)
        self.got(h, 0)
        self.add(h, self.m, (0,))
        self.send(h, self.m, 2, self.m)

    def mine(self, j):
        me, h = self.me, self.near(j)
        self.got(h, 1)
        self.got(h, 2)
        self.add(h, (me.b, me.a), (1, 2))
        if j > 0 and not self.by_plane:
            self.link.go(
                self.H.at[h, me.b, me.a], self.RL.at[me.g], self.base + 3 * me.lines + me.g, me.at(h, me.b, me.a),
                self.base + 3 * me.lines + h,
            )

    def flow(self, j):
        me, G = self.me, self.me.lines
        h = self.near(j)
        self.by_plane = True
        base = self.base + 3 * G
        if j == 0:
            for slot, ok in ((h, me.g > 0), (G, me.g < G - 1)):
                pl.when(ok)(functools.partial(self.flow_in, h, slot))
            return
        up = (h > me.g).astype(jnp.int32)
        pl.when(jnp.where(up == 1, me.g > 0, me.g < G - 1))(functools.partial(self.flow_in, h, h))
        slot = jnp.where(h == me.g - 1, G, h)
        self.link.go(self.H.at[h], self.RL.at[slot], base + slot, me.at(me.g + 2 * up - 1, me.b, me.a), base + 2 * G + h)

    def flow_in(self, h, slot):
        self.link.got(self.RL.at[slot], self.base + 3 * self.me.lines + slot)
        self.H[h] = (self.H[h].astype(F32) + self.RL[slot].astype(F32)).astype(BF)

    def total(self):
        me = self.me
        if self.by_plane:
            return self.H[me.g, me.b, me.a].astype(F32)
        for k in range(1, me.lines):
            h = (me.g + k) % me.lines
            self.link.got(self.RL.at[h], self.base + 3 * me.lines + h)
        self.RL[me.g] = self.H[me.g, me.b, me.a]
        total = self.RL[0].astype(F32)
        for g in range(1, me.lines):
            total = total + self.RL[g].astype(F32)
        return total


def into_blocks(H, value, first, rows):
    n = 4 * H.shape[0]
    count = value.shape[0]
    value = value.astype(BF)
    if H.shape[3] == rows and first == 0 and count == n * rows:
        H[...] = value.reshape(H.shape)
        return
    for i in range(n):
        lo, hi = max(first, i * rows), min(first + count, (i + 1) * rows)
        if lo < hi:
            H[i // 4, (i // 2) % 2, i % 2, lo - i * rows : hi - i * rows] = value[lo - first : hi - first]


def norm(v):
    centered = v - jnp.mean(v, axis=-1, keepdims=True)
    inverse = lax.rsqrt(jnp.mean(centered * centered, axis=-1, keepdims=True) + EPS_NORM)
    return centered * inverse, inverse


def norm_back(incoming, normed, inverse, gain):
    scaled = incoming * gain
    return inverse * (
        scaled
        - jnp.mean(scaled, axis=-1, keepdims=True)
        - normed * jnp.mean(scaled * normed, axis=-1, keepdims=True)
    )


def down(v):
    return jnp.sum(v.astype(F32), axis=0, keepdims=True)


def put(ref, off, row):
    width, at = row.shape[1], 0
    while at < width:
        r, lane = (off + at) // D, (off + at) % D
        take = min(width - at, D - lane)
        ref[r : r + 1, lane : lane + take] = row[:, at : at + take]
        at += take


def ma_back_first(bp_ref, dec, outf, h):
    n8 = bp_ref.shape[0] // 8

    def step(i, h):
        bs = bp_ref[pl.ds((n8 - 1 - i) * 8, 8), :]
        for r in range(7, -1, -1):
            h = dec * (outf * bs[r : r + 1] + h)
        return h

    return lax.fori_loop(0, n8, step, h)


def ma_back(x_ref, bp_ref, keep_ref, leave, dec, inf, outf, tok_o, AV):
    n8 = x_ref.shape[0] // 8
    wide = 256
    for j in range(D // wide):
        sl = slice(j * wide, (j + 1) * wide)
        d, f, u = dec[:, sl], inf[:, sl], outf[:, sl]

        def step(i, carry):
            h, dd, di, du = carry
            at = n8 - 1 - i
            xs = x_ref[pl.ds(at * 8, 8), sl]
            bs = bp_ref[pl.ds(at * 8, 8), sl]
            states = [keep_ref[at, :, sl]]
            for r in range(8):
                states.append(d * states[-1] + f * xs[r : r + 1])
            rows = [None] * 8
            for r in range(7, -1, -1):
                adj = u * bs[r : r + 1] + h
                dd = dd + adj * states[r]
                di = di + adj * xs[r : r + 1]
                du = du + bs[r : r + 1] * states[r + 1]
                rows[r] = jnp.sum(f * adj, axis=0, keepdims=True)
                h = d * adj
            tok_o[pl.ds(at * 8, 8), sl] += jnp.concatenate(rows, axis=0)
            return h, dd, di, du

        zero = jnp.zeros((NH, wide), F32)
        _, dd, di, du = lax.fori_loop(0, n8, step, (leave[:, sl], zero, zero, zero))
        AV[16 : 16 + NH, sl] = dd
        AV[16 + NH : 16 + 2 * NH, sl] = di
        AV[16 + 2 * NH : 16 + 3 * NH, sl] = du


def diagonals(G, T, GS, prof):
    flip = (
        lax.broadcasted_iota(jnp.int32, (T, T), 0) + lax.broadcasted_iota(jnp.int32, (T, T), 1) == T - 1
    ).astype(F32).astype(BF)
    for i in range(4):
        turned = dot(flip, GS[i])
        for kk in range(G):
            m = 4 * kk - i + 3
            block = jnp.concatenate([turned[:, kk * T : (kk + 1) * T], jnp.zeros((T, T), F32)], axis=1)
            s = jnp.sum(pltpu.roll(block, 0, 1, stride=1, stride_axis=0), axis=0, keepdims=True)
            prof[m : m + 1] += s[:, :T]
            prof[m + 1 : m + 2] += s[:, T:]


def table_rows(G, me, prof, index_ref, AV):
    first_row = me.p - 4 * me.g - 4 + 4 * G
    total = jnp.zeros((NB, 128), F32)
    for r in range(4 * G + 1):
        hit = index_ref[pl.ds(first_row + r, 1), :] == lax.broadcasted_iota(jnp.int32, (NB, 128), 0)
        total = total + jnp.where(hit, prof[r : r + 1], 0.0)
    col = jnp.sum(total, axis=1, keepdims=True)
    put(AV, OFF_TB, as_rows(col)[0:1])


(
    SEND_X, AVERAGE_PLANE, AVERAGE, VALUES_0, VALUES_1, MIXING, BIAS_ROWS, MERGE, HIDDEN, FEED, FEED_OUT,
    BACK_UP, BACK_ONE, BACK_GATE, BACK_QUERIES, BACK_KEYS, SWAP_VALUES, VALUES_TO_TOKENS, GRADS_VALUES,
    BACK_SHARED, BACK_PRE, GRADS_MIXER, ADJOINT_FIRST, ADJOINT_PLANE, ADJOINT, DIAGONALS, TABLE_ROWS,
    SUMS_CORE, SUMS_PLANE, SUMS_LINE, SUMS_BACK, SUMS_ALL, ADD_VALUES, STATS, GRADS_DOWN, GRADS_UP,
    GRADS_HIDDEN,
) = range(37)
(
    FIRST, SECOND, THIRD, CHAIN, BUNDLE_IN, BEHIND, THEIRS, PASSED, MINE, FLOW, ALONG, BUNDLE_OUT, READY,
    CLOSE, ATTEND, ATTEND_BACK, VALUES_BACK,
) = range(100, 1800, 100)
ORDER = (
    ALONG + 0, FIRST + 40, FIRST + 10, ALONG + 1, CHAIN + 2, FIRST + 2, ALONG + 2, CHAIN + 1, SECOND + 40, CHAIN + 11,
    FIRST + 30, CHAIN + 22, FIRST + 1, FIRST + 11, FIRST + 0, ALONG + 3, SECOND + 2, BIAS_ROWS, CHAIN + 12,
    CHAIN + 31, FIRST + 12, THIRD + 40, AVERAGE_PLANE, FIRST + 31, FIRST + 20, SECOND + 10, CHAIN + 3, SECOND + 30,
    CHAIN + 13, CHAIN + 21, CHAIN + 23, FIRST + 13, FIRST + 3, AVERAGE, CHAIN + 33, SECOND + 31, SECOND + 0,
    CHAIN + 32, SECOND + 12, SEND_X, SECOND + 3, FIRST + 22, THIRD + 31, THIRD + 10, SECOND + 13, THIRD + 0,
    FIRST + 21, SECOND + 11, THIRD + 12, SECOND + 21, THIRD + 3, SECOND + 20, THIRD + 13, THIRD + 11, SECOND + 1,
    SECOND + 22, THIRD + 2, READY + 1, THIRD + 20, BUNDLE_OUT + 4, FIRST + 32, FIRST + 33, THIRD + 1, MIXING,
    READY + 0, FIRST + 23, VALUES_0, SECOND + 32, VALUES_1, SECOND + 23, SECOND + 33, ATTEND + 2, ATTEND + 1,
    BUNDLE_IN + 41, THIRD + 30, ATTEND + 0, BUNDLE_IN + 42, THIRD + 22, THIRD + 21, THIRD + 32, ATTEND + 3,
    THIRD + 23, READY + 2, THIRD + 33, BUNDLE_IN + 43, READY + 3, READY + 4, MERGE, HIDDEN, FEED, FEED_OUT, BACK_UP,
    BACK_ONE, BACK_GATE, GRADS_DOWN, FLOW + 43, GRADS_HIDDEN, BEHIND + 22, GRADS_UP, PASSED + 22, FLOW + 42,
    ATTEND_BACK + 2, THEIRS + 20, BEHIND + 30, ATTEND_BACK + 3, BEHIND + 31, THEIRS + 22, FLOW + 41, THEIRS + 31,
    ATTEND_BACK + 1, BEHIND + 23, BEHIND + 21, ATTEND_BACK + 0, BACK_KEYS, THEIRS + 23, VALUES_BACK + 0,
    VALUES_BACK + 2, VALUES_BACK + 1, SWAP_VALUES, BEHIND + 33, PASSED + 30, BEHIND + 32, BACK_QUERIES,
    VALUES_TO_TOKENS, PASSED + 23, THEIRS + 32, THEIRS + 30, PASSED + 21, GRADS_VALUES, PASSED + 33, BEHIND + 0,
    THEIRS + 33, THEIRS + 1, BACK_SHARED, BEHIND + 1, BACK_PRE, ADJOINT_FIRST, PASSED + 0, DIAGONALS, PASSED + 31,
    PASSED + 1, THEIRS + 21, THEIRS + 3, BEHIND + 2, PASSED + 32, GRADS_MIXER, BEHIND + 12, ADJOINT_PLANE,
    THEIRS + 11, MINE + 1, MINE + 22, MINE + 31, MINE + 30, BEHIND + 3, MINE + 33, BEHIND + 13, THEIRS + 13,
    PASSED + 12, MINE + 23, TABLE_ROWS, FLOW + 40, THEIRS + 12, BEHIND + 40, THEIRS + 0, MINE + 32, ADJOINT,
    PASSED + 3, BEHIND + 20, ADD_VALUES, SUMS_CORE, PASSED + 13, THEIRS + 40, MINE + 3, SUMS_PLANE, PASSED + 20,
    BEHIND + 11, MINE + 12, PASSED + 40, SUMS_LINE, MINE + 13, THEIRS + 2, BEHIND + 10, MINE + 21, MINE + 40,
    PASSED + 11, MINE + 11, SUMS_BACK, PASSED + 2, CLOSE + 3, CLOSE + 4, MINE + 0, MINE + 20, THEIRS + 10,
    PASSED + 10, SUMS_ALL, CLOSE + 2, MINE + 10, MINE + 2, CLOSE + 1, CLOSE + 0, STATS,
)


class Refs:
    def __init__(self, names, refs):
        self.__dict__.update(zip(names, refs))


def main_kernel(G, count, in_names, out_names, scratch_names, *refs):
    a, b = len(in_names), len(in_names) + len(out_names)
    I, O, S = Refs(in_names, refs[:a]), Refs(out_names, refs[a:b]), Refs(scratch_names, refs[b:])
    me = Place(G)
    T = I.x.shape[0]
    o = 1 - me.c
    others = close_peers(me)
    for k in range(1, count):
        others.append((2 * ((me.dp // 2 + k) % count) + me.c, me.blk))
    greet(others)
    Ws = (S.w0, S.mx, S.n0, S.w1, S.n1)
    for W, src in zip(Ws, (I.wid.at[0], I.mix, I.nar.at[0], I.wid.at[1], I.nar.at[1])):
        r = src.shape[0]
        W[me.g, me.b, me.a, 0:r] = src[...].astype(BF)
        if r < W.shape[3]:
            W[me.g, me.b, me.a, r:] = jnp.zeros((W.shape[3] - r, W.shape[4]), BF)
    S.xb[me.g] = I.x[...].astype(BF)
    damp, mix, dec, inf, outf = decays_of(I.avg)
    zero = jnp.zeros((NH, D), F32)
    whole = power(dec, T)
    S.fin[me.p] = ma_pass(I.x, zero, dec, inf, outf, None)
    S.AV[...] = jnp.zeros_like(S.AV)
    S.prof[...] = jnp.zeros_like(S.prof)
    greeted(others)
    link = Link(me, S.ssem, S.rsem)
    got = {}
    val = {}
    ga = [Gather(me, W, S.agss.at[i], S.agrs.at[i]) for i, W in enumerate(Ws)]
    got["fin"] = link.plane(lambda q: S.fin.at[me.p], lambda q: S.fin.at[q])
    mixed = lambda off, w: S.mixed[:, off : off + w]
    vector = lambda off, w: vec(I.vec, off, w)
    scaling = ZD ** (-0.5)

    def cols(c, half):
        return pl.ds(pl.multiple_of(c * half, 128), half)

    def flat(W):
        return W[...].reshape(4 * G * W.shape[3], W.shape[4])

    def send_x():
        got["x"] = link.line(lambda h: S.xb.at[me.g], lambda h: S.xb.at[h])

    def average_plane():
        got.pop("fin")()
        tot = S.fin[0]
        for q in range(1, 4):
            tot = whole * tot + S.fin[q]
        S.ftot[me.g] = tot
        got["ftot"] = link.line(lambda h: S.ftot.at[me.g], lambda h: S.ftot.at[h])

    def average_second():
        got.pop("ftot")()
        ent = zero
        whole4 = power(whole, 4)
        for i in range(G - 1):
            ent = jnp.where(i < me.g, whole4 * ent + S.ftot[i], ent)
        for q in range(3):
            ent = jnp.where(q < me.p, whole * ent + S.fin[q], ent)
        ma_pass(I.x, ent, dec, inf, outf, S.pre, S.keep)
        S.pre[...] = S.pre[...] + vector(OFF_OM, D) * I.x[...]

    def values(i):
        if i == 0:
            got.pop("x")()
            got["xb"] = link.swap(S.xb.at[:, :, cols(o, D // 2)], S.XB)
        step = max(1, G // 2)
        wide = step * 4 * S.w0.shape[3]
        wblk = S.w0[i * step : (i + 1) * step].reshape(wide, D)
        sl = slice(i * wide, (i + 1) * wide)
        for gg in range(G):
            vp = dot(S.xb[gg], wblk, NT) + vector(OFF_V + i * wide, wide)
            S.GV[0, gg * T : (gg + 1) * T, sl] = silu_grad(vp).astype(BF)
            S.v[gg * T : (gg + 1) * T, sl] = silu(vp).astype(BF)

    chunk = MX // 5

    def mixer_rows(i):
        r = MX // (4 * G)
        at = 0
        for k in range(4 * G):
            lo, hi = max(i * chunk, k * r), min((i + 1) * chunk, (k + 1) * r)
            if lo < hi:
                S.mc[at : at + hi - lo] = S.mx[k // 4, (k // 2) % 2, k % 2, lo - k * r : hi - k * r]
                at += hi - lo
        return S.mc[...]

    def mixing():
        prime = silu(S.pre[...]).astype(BF)
        for i in (1, 0, 2, 3, 4):
            sl = slice(i * chunk, (i + 1) * chunk)
            S.mixed[:, sl] = dot(prime, mixer_rows(i), NT) + vector(OFF_MX + i * chunk, chunk)
            if i == 0:
                shared = silu(mixed(D, ZD))
                S.qb[me.p] = ((shared * vector(OFF_QG, ZD) + vector(OFF_QS, ZD)) * scaling).astype(BF)
                S.kb[me.g] = (shared * vector(OFF_QG + ZD, ZD) + vector(OFF_QS + ZD, ZD)).astype(BF)
                got["q"] = link.plane(lambda q: S.qb.at[me.p], lambda q: S.qb.at[q])
                got["k"] = link.line(lambda h: S.kb.at[me.g], lambda h: S.kb.at[h])

    def bias_rows():
        first_row = me.p - 4 * me.g - 4 + 4 * G
        table = jnp.broadcast_to(vector(OFF_TB, NB), (128, NB)).T
        for r in range(4 * G + 1):
            hit = I.index[pl.ds(first_row + r, 1), :] == lax.broadcasted_iota(jnp.int32, (NB, 128), 0)
            S.brow[r : r + 1] = jnp.sum(jnp.where(hit, table, 0.0), axis=0, keepdims=True)

    def attend(kk):
        if kk == 2:
            got.pop("q")()
            got.pop("k")()
            val["o"] = [link.slot(4), link.slot(4)]
        i = (me.p + kk) % 4
        kall = S.kb[...].reshape(G * T, ZD)
        attend_block(G, T, me, i, S.qb, kall, S.v, S.brow, S.s, S.ob, S.lout, S.att if kk == 0 else None)
        if kk:
            to = me.at(me.g, i // 2, i % 2)
            link.go(S.ob.at[i], S.oin.at[me.p], val["o"][0] + kk, to)
            link.go(S.lout.at[i], S.lin.at[me.p], val["o"][1] + kk, to)
        else:
            S.lin[me.p] = S.lout[me.p]

    def merge():
        for k in range(1, 4):
            link.got(S.oin.at[(me.p + 4 - k) % 4], val["o"][0] + k)
            link.got(S.lin.at[(me.p + 4 - k) % 4], val["o"][1] + k)
        ls = [as_col(S.lin[j]) for j in range(4)]
        peak = functools.reduce(jnp.maximum, ls)
        lse = peak + jnp.log(functools.reduce(jnp.add, [jnp.exp(l - peak) for l in ls]))
        S.att[...] = S.att[...] * jnp.exp(as_col(S.lout[me.p]) - lse)
        for k in range(1, 4):
            j = (me.p + k) % 4
            S.att[...] += S.oin[j].astype(F32) * jnp.exp(as_col(S.lin[j]) - lse)
        S.ST[me.p, 0] = as_rows(lse)
        link.drain()

    full = S.ob

    def share_half(k, width, dst):
        half = width // 2
        dst[0] = full[k, :, cols(me.c, half)]
        return link.swap(full.at[k, :, cols(o, half)], dst.at[1])

    def hidden():
        x = I.x[...]
        full[1, :, :D] = silu(S.pre[...]).astype(BF)
        got["pb"] = share_half(1, D, S.PB)
        full[0] = (silu(mixed(D + ZD, VD)) * S.att[...]).astype(BF)
        got["gt"] = share_half(0, VD, S.GT)
        hidden_pre = mixed(D + ZD + VD, D) + dot(full[0], flat(S.n0), NT) + vector(OFF_H, D)
        upd = sigmoid(mixed(0, D))
        act = silu(hidden_pre)
        one = x + upd * (act - x)
        n_one, r_one = norm(one)
        layer = n_one * vector(OFF_G1, D) + vector(OFF_S1, D)
        full[2, :, :D] = layer.astype(BF)
        got["ll"] = share_half(2, D, S.LL)
        val.update(x=x, hidden_pre=hidden_pre, upd=upd, act=act, n_one=n_one, r_one=r_one, layer=layer)

    def feed():
        val["expand_pre"] = dot(full[2, :, :D], flat(S.w1), NT) + vector(OFF_UP, FF)
        full[3] = silu(val["expand_pre"]).astype(BF)
        got["ex"] = share_half(3, FF, S.EX)

    def feed_out():
        two = val["layer"] + dot(full[3], flat(S.n1), NT) + vector(OFF_DOWN, D)
        n_two, r_two = norm(two)
        gain_two = vector(OFF_G2, D)
        O.block[...] = n_two * gain_two + vector(OFF_S2, D)
        cot = I.cot[...]
        val["back_two"] = norm_back(cot, n_two, r_two, gain_two)
        put(S.AV, OFF_G2, down(cot * n_two))
        put(S.AV, OFF_S2, down(cot))
        S.GD[0] = val["back_two"].astype(BF)
        got["gd"] = link.swap(S.GD.at[0], S.GD.at[1])
        put(S.AV, OFF_DOWN, down(S.GD[0]))

    def back_up():
        S.GU[0] = (dot(S.GD[0], flat(S.n1)) * silu_grad(val["expand_pre"])).astype(BF)
        got["gu"] = link.swap(S.GU.at[0], S.GU.at[1])
        put(S.AV, OFF_UP, down(S.GU[0]))

    def back_first():
        into_one = val["back_two"] + dot(S.GU[0], flat(S.w1))
        put(S.AV, OFF_G1, down(into_one * val["n_one"]))
        put(S.AV, OFF_S1, down(into_one))
        back_one = norm_back(into_one, val["n_one"], val["r_one"], vector(OFF_G1, D))
        S.GH[0] = (back_one * val["upd"] * silu_grad(val["hidden_pre"])).astype(BF)
        got["gh"] = link.swap(S.GH.at[0], S.GH.at[1])
        put(S.AV, OFF_H, down(S.GH[0]))
        val["back_one"] = back_one

    def back_gate():
        upd, back_one = val["upd"], val["back_one"]
        back_gated = dot(S.GH[0], flat(S.n0))
        S.GA[me.p] = (back_gated * silu(mixed(D + ZD, VD))).astype(BF)
        S.ST[me.p, 1] = as_rows(jnp.sum(S.GA[me.p].astype(F32) * S.att[...], axis=1, keepdims=True))
        got["ga"] = link.plane(lambda q: S.GA.at[me.p], lambda q: S.GA.at[q])
        got["st"] = link.plane(lambda q: S.ST.at[me.p], lambda q: S.ST.at[q])
        S.GM[0, :, 0:D] = (back_one * (val["act"] - val["x"]) * upd * (1.0 - upd)).astype(BF)
        S.GM[0, :, D + ZD : D + ZD + VD] = (back_gated * S.att[...] * silu_grad(mixed(D + ZD, VD))).astype(BF)
        S.GM[0, :, D + ZD + VD :] = S.GH[0]
        O.tok[...] = back_one * (1.0 - upd)

    Hs = [W.at[:, :, :, :, 0 : W.shape[-1] // 2] for W in Ws]
    near = ga[0].near
    red = [Reduce(me, link, near, H, R, L) for H, R, L in zip(Hs, (S.R0, S.RM, S.RN0, S.R1, S.RN1), (S.L0, S.LM, S.LN0, S.L1, S.LN1))]

    def both(ref):
        return ref[...].reshape(2 * T, ref.shape[-1])

    def grads(i, out, into, names):
        for name in names:
            got.pop(name)()
        ga[i].drain()
        rhs = both(into)
        for j in range(0, out.shape[-1], 384):
            lhs = out[:, :, j : j + 384].reshape(2 * T, 384)
            into_blocks(Hs[i], dot(lhs, rhs, TN), j, out.shape[-1] // (4 * G))

    def attend_back(kk):
        if kk == 2:
            got.pop("ga")()
            got.pop("st")()
        i = (me.p + kk) % 4
        probs = jnp.exp(S.s[i] - as_col(S.ST[i, 0]))
        back = dot(S.GA[i], S.v[...], NT)
        gs = (probs * (back - as_col(S.ST[i, 1]))).astype(BF)
        S.P16[i] = probs.astype(BF)
        S.GS[i] = gs
        S.QP[i] = dot(gs, S.kb[...].reshape(G * T, ZD))

    def back_queries():
        got["dq"] = link.plane(lambda q: S.QP.at[q], lambda q: S.KS.at[q])

    def back_keys():
        S.KP[...] = dot(S.GS[...].reshape(4 * T, G * T), S.qb[...].reshape(4 * T, ZD), TN).reshape(G, T, ZD)
        got["dk"] = link.line(lambda h: S.KP.at[h], lambda h: S.DP.at[h])

    def back_values(j):
        wide = VD // 3
        sl = slice(j * wide, (j + 1) * wide)
        dv = dot(S.P16[...].reshape(4 * T, G * T), S.GA[:, :, sl].reshape(4 * T, wide), TN)
        gv = (dv * S.GV[0, :, sl].astype(F32)).astype(BF)
        S.GV[0, :, sl] = gv
        put(S.AV, OFF_V + j * wide, down(gv))

    def swap_values():
        got["gv"] = link.swap(S.GV.at[0], S.GV.at[1])

    def values_to_tokens():
        for g in range(G):
            S.DX[g] = dot(S.GV[0, g * T : (g + 1) * T], flat(S.w0)).astype(BF)
        got["dx"] = link.line(lambda h: S.DX.at[h], lambda h: S.BP.at[h])

    def grads_values():
        got.pop("gv")()
        got.pop("xb")()
        ga[0].drain()
        own = S.xb[:, :, cols(me.c, D // 2)].reshape(G * T, D // 2)
        their = S.XB[...].reshape(G * T, D // 2)
        wide = VD // 4
        for j in range(4):
            sl = slice(j * wide, (j + 1) * wide)
            total = dot(S.GV[0, :, sl], own, TN) + dot(S.GV[1, :, sl], their, TN)
            into_blocks(Hs[0], total, j * wide, VD // (4 * G))

    def back_shared():
        got.pop("dq")()
        S.KS[me.p] = S.QP[me.p]
        back_q = (S.KS[0] + S.KS[1] + S.KS[2] + S.KS[3]) * scaling
        got.pop("dk")()
        S.DP[me.g] = S.KP[me.g]
        back_k = S.DP[0]
        for g in range(1, G):
            back_k = back_k + S.DP[g]
        sp = mixed(D, ZD)
        shared = silu(sp)
        put(S.AV, OFF_QG, down(back_q * shared))
        put(S.AV, OFF_QG + ZD, down(back_k * shared))
        put(S.AV, OFF_QS, down(back_q))
        put(S.AV, OFF_QS + ZD, down(back_k))
        back = back_q * vector(OFF_QG, ZD) + back_k * vector(OFF_QG + ZD, ZD)
        S.GM[0, :, D : D + ZD] = (back * silu_grad(sp)).astype(BF)
        got["gm"] = link.swap(S.GM.at[0], S.GM.at[1])
        put(S.AV, OFF_MX, down(S.GM[0]))

    def back_pre():
        back = jnp.zeros((T, D), F32)
        for i in range(5):
            back = back + dot(S.GM[0, :, i * chunk : (i + 1) * chunk], mixer_rows(i))
        back = back * silu_grad(S.pre[...])
        O.tok[...] += vector(OFF_OM, D) * back
        put(S.AV, OFF_OM, down(back * I.x[...]))
        S.bp[...] = back

    def grads_mixer():
        got.pop("gm")()
        got.pop("pb")()
        ga[1].drain()
        rhs = both(S.PB)
        for j in range(5):
            sl = slice(j * chunk, (j + 1) * chunk)
            into_blocks(Hs[1], dot(S.GM[:, :, sl].reshape(2 * T, chunk), rhs, TN), j * chunk, MX // (4 * G))

    def average_back():
        S.fin2[me.p] = ma_back_first(S.bp, dec, outf, zero)
        got["fin2"] = link.plane(lambda q: S.fin2.at[me.p], lambda q: S.fin2.at[q])

    def average_back_plane():
        got.pop("fin2")()
        tot = S.fin2[3]
        for q in (2, 1, 0):
            tot = whole * tot + S.fin2[q]
        S.ftot2[me.g] = tot
        got["ftot2"] = link.line(lambda h: S.ftot2.at[me.g], lambda h: S.ftot2.at[h])

    def average_back_second():
        got.pop("ftot2")()
        whole4 = power(whole, 4)
        leave = zero
        for i in range(G - 1, 0, -1):
            leave = jnp.where(i > me.g, whole4 * leave + S.ftot2[i], leave)
        for q in (3, 2, 1):
            leave = jnp.where(q > me.p, whole * leave + S.fin2[q], leave)
        ma_back(I.x, S.bp, S.keep, leave, dec, inf, outf, O.tok, S.AV)

    def pair_sum(value, buf):
        buf[me.dp // 2] = value
        link.pairs(buf.at[me.dp // 2], lambda d: buf.at[d], count)()
        value = buf[0]
        for d in range(1, count):
            value = value + buf[d]
        return value

    Fs = (S.F0, S.FM, S.FN0, S.F1, S.FN1)
    Ps = (S.P0, S.PM, S.PN0, S.P1, S.PN1)
    finish = []

    def close(i):
        F = Fs[i]
        total = red[i].total()
        half = total.shape[-1]
        if count > 1:
            total = pair_sum(total, Ps[i])
        F[:, cols(me.c, half)] = total
        part = F.at[:, cols(me.c, half)]
        s = link.slot()
        link.go(part, part, s, me.sib())
        finish.append(lambda: link.got(F.at[:, cols(o, half)], s))

    hr = S.AV.shape[0] // 2
    qr = hr // 4

    def rows_of(core, q, n):
        return pl.ds(pl.multiple_of(core * hr + q * qr, 8), n)

    def sums_core():
        got["av"] = link.swap(S.AV, S.AS)

    def sums_plane():
        got.pop("av")()
        S.AW[...] = S.AV[...] + S.AS[...]
        got["ap"] = link.plane(lambda q: S.AW.at[rows_of(me.c, q, qr), :], lambda q: S.AP.at[q])

    def sums_line():
        got.pop("ap")()
        S.AP[me.p] = S.AW[rows_of(me.c, me.p, qr), :]
        S.AL[me.g] = S.AP[0] + S.AP[1] + S.AP[2] + S.AP[3]
        got["al"] = link.line(lambda h: S.AL.at[me.g], lambda h: S.AL.at[h])

    def sums_back():
        got.pop("al")()
        tot = S.AL[0]
        for g in range(1, G):
            tot = tot + S.AL[g]
        if count > 1:
            tot = pair_sum(tot, S.PA)
        S.AT[rows_of(me.c, me.p, qr), :] = tot
        got["at"] = link.plane(lambda q: S.AT.at[rows_of(me.c, me.p, qr), :], lambda q: S.AT.at[rows_of(me.c, q, qr), :])

    def sums_all():
        got.pop("at")()
        s = link.slot()
        mine = S.AT.at[rows_of(me.c, 0, hr), :]
        link.go(mine, mine, s, me.sib())
        finish.append(lambda: link.got(S.AT.at[rows_of(o, 0, hr), :], s))

    def add_values():
        got.pop("dx")()
        S.BP[me.g] = S.DX[me.g]
        for g in range(G):
            O.tok[...] += S.BP[g].astype(F32)

    def allsum(value, pb, lb):
        pb[me.p] = value
        link.plane(lambda q: pb.at[me.p], lambda q: pb.at[q])()
        lb[me.g] = pb[0] + pb[1] + pb[2] + pb[3]
        link.line(lambda h: lb.at[me.g], lambda h: lb.at[h])()
        out = lb[0]
        for g in range(1, G):
            out = out + lb[g]
        return out

    def stats():
        for f in finish:
            f()
        O.sums[...] = S.AT[0:16]
        O.ma[...] = S.AT[16:64].reshape(3, NH, D)
        for F, dst, i in zip(Fs, (O.gw.at[0], O.gm, O.gn.at[0], O.gw.at[1], O.gn.at[1]), range(5)):
            pltpu.make_async_copy(F, dst, S.outs.at[i]).start()
        adafactor_stats(G, I, O, S, allsum)
        for F, dst, i in zip(Fs, (O.gw.at[0], O.gm, O.gn.at[0], O.gw.at[1], O.gn.at[1]), range(5)):
            pltpu.make_async_copy(F, dst, S.outs.at[i]).wait()

    one = {
        SEND_X: send_x, AVERAGE_PLANE: average_plane, AVERAGE: average_second, VALUES_0: lambda: values(0),
        VALUES_1: lambda: values(1), MIXING: mixing, BIAS_ROWS: bias_rows, MERGE: merge, HIDDEN: hidden, FEED: feed,
        FEED_OUT: feed_out, BACK_UP: back_up, BACK_ONE: back_first, BACK_GATE: back_gate, BACK_QUERIES: back_queries,
        BACK_KEYS: back_keys, SWAP_VALUES: swap_values, VALUES_TO_TOKENS: values_to_tokens, GRADS_VALUES: grads_values,
        BACK_SHARED: back_shared, BACK_PRE: back_pre, GRADS_MIXER: grads_mixer, ADJOINT_FIRST: average_back,
        ADJOINT_PLANE: average_back_plane, ADJOINT: average_back_second,
        DIAGONALS: lambda: diagonals(G, T, S.GS, S.prof), TABLE_ROWS: lambda: table_rows(G, me, S.prof, I.index, S.AV),
        SUMS_CORE: sums_core, SUMS_PLANE: sums_plane, SUMS_LINE: sums_line, SUMS_BACK: sums_back, SUMS_ALL: sums_all,
        ADD_VALUES: add_values, STATS: stats,
        GRADS_DOWN: lambda: grads(4, S.GD, S.EX, ("gd", "ex")), GRADS_UP: lambda: grads(3, S.GU, S.LL, ("gu", "ll")),
        GRADS_HIDDEN: lambda: grads(2, S.GH, S.GT, ("gh", "gt")),
    }
    part = {
        CHAIN: lambda i, j: ga[i].chain(j), FIRST: lambda i, j: ga[i].first(j), SECOND: lambda i, j: ga[i].second(j),
        THIRD: lambda i, j: ga[i].third(j), BEHIND: lambda i, j: red[i].behind(j), THEIRS: lambda i, j: red[i].theirs(j),
        PASSED: lambda i, j: red[i].passed(j), MINE: lambda i, j: red[i].mine(j), BUNDLE_IN: lambda i, j: ga[i].bundle_in(j),
        FLOW: lambda i, j: red[i].flow(j),
    }
    single = {
        ATTEND: attend, ATTEND_BACK: attend_back, ALONG: lambda i: ga[i].z(), BUNDLE_OUT: lambda i: ga[i].bundle_out(),
        READY: lambda i: ga[i].done(), CLOSE: close, VALUES_BACK: back_values,
    }
    for step in ORDER:
        kind, rest = step - step % 100, step % 100
        if kind == 0:
            one[step]()
        elif kind in single:
            single[kind](rest)
        else:
            part[kind](rest // 10, rest % 10)
    for gather in ga:
        gather.drain()
    link.drain()


def adafactor_stats(G, I, O, S, allsum):
    rate = 1.0 - STEP ** (-0.8)
    mats = [
        (S.FM, I.rm[0:1], I.cm[...].T, MX, D, O.rm, O.cm, 0),
        (S.F0, I.rw[0:1], I.cw[0:1].T, VD, D, O.rw, O.cw, 0),
        (S.F1, I.rw[1:2], I.cw[1:2].T, VD, D, O.rw, O.cw, 1),
        (S.FN0, I.rn[0:1], I.cn[0:1].T, D, VD, O.rn, O.cn, 0),
        (S.FN1, I.rn[1:2], I.cn[1:2].T, D, VD, O.rn, O.cn, 1),
    ]
    masters = (I.mix, I.wid.at[0], I.wid.at[1], I.nar.at[0], I.nar.at[1])
    lanes = lax.broadcasted_iota(jnp.int32, (1, D), 1)
    rows, cs, extra = [], [], jnp.zeros((1, D), F32)
    for i, (F, _, _, total, width, _, _, _) in enumerate(mats):
        sq = F[0 : total // (4 * G)]
        sq = sq * sq
        s = jnp.sum(sq, axis=0, keepdims=True)
        for j in range(width // D):
            rows.append(s[:, j * D : (j + 1) * D])
        cs.append(jnp.sum(sq, axis=1, keepdims=True))
        wv = masters[i][...]
        extra = jnp.where(lanes == i, jnp.sum(wv * wv), extra)
    rows.append(extra)
    small = jnp.sum(O.sums[...] * O.sums[...])
    for v in raw_averager([I.avg[i] for i in range(4)], O.ma):
        small = small + jnp.sum(v * v)
    tot = allsum(jnp.concatenate(rows, axis=0), S.rp, S.rl)
    length = jnp.sqrt(jnp.sum(tot[0:7]) + small)
    factor = jnp.minimum(1.0, CLIP_NORM / length)
    at = 0
    squares = jnp.zeros((1, 128), F32)
    means = jnp.zeros((1, 128), F32)
    lane = lanes[:, :128]
    for i, (F, ro, co, total, width, rows_o, cols_o, k) in enumerate(mats):
        row = jnp.concatenate([tot[at + j : at + j + 1] for j in range(width // D)], axis=1)
        at += width // D
        rnew = rate * ro + (1.0 - rate) * (factor * factor * row / total + EPS_ONE)
        cnew = rate * co + (1.0 - rate) * (factor * factor * cs[i] / width + EPS_ONE)
        mean = jnp.sum(rnew) / width
        u = factor * F[0 : total // (4 * G)] * lax.rsqrt(rnew * cnew / mean)
        squares = jnp.where(lane == i, jnp.sum(u * u), squares)
        means = jnp.where(lane == i, mean, means)
        rows_o[k : k + 1] = rnew
        cols_o[k : k + 1] = cnew.T
    sums = allsum(jnp.broadcast_to(squares, (8, 128)), S.up, S.ul)
    O.scal[0:1] = sums[0:1]
    O.scal[1:2] = tot[7:8, :128]
    O.scal[2:3] = means
    O.scal[3:4] = jnp.full((1, 128), length, F32)
    O.scal[4:5] = jnp.full((1, 128), factor, F32)
    O.scal[5:8] = jnp.zeros((3, 128), F32)


def main_call(G, count, x, cot, mix, wid, nar, avg, vv, index, rows, cols):
    T = x.shape[0]
    r0, r1, r2 = (t // (4 * G) for t in (MX, VD, D))
    rm, rw, rn = (r + -r % 16 for r in (r0, r1, r2))
    A = jax.ShapeDtypeStruct
    V = pltpu.VMEM
    half, hv = D // 2, VD // 2
    vm = pl.BlockSpec(memory_space=pltpu.VMEM)
    hbm = pl.BlockSpec(memory_space=pl.ANY)
    S = pltpu.SemaphoreType.DMA
    ins = dict(
        x=x, cot=cot, mix=mix, wid=wid, nar=nar, avg=avg, vec=vv, index=index,
        rm=rows[0], rw=rows[1], rn=rows[2], cm=cols[0], cw=cols[1], cn=cols[2],
    )
    outs = dict(
        block=A((T, D), F32), tok=A((T, D), F32), gm=A((rm, D), F32), gw=A((2, rw, D), F32), gn=A((2, rn, VD), F32),
        sums=A((16, D), F32), ma=A((3, NH, D), F32), rm=A((1, D), F32), rw=A((2, D), F32), rn=A((2, VD), F32),
        cm=A((1, r0), F32), cw=A((2, r1), F32), cn=A((2, r2), F32), scal=A((8, 128), F32),
    )
    out_specs = [hbm if name in ("gm", "gw", "gn") else vm for name in outs]
    wide, narrow, mixer = (rw, half), (rn, hv), (rm, half)
    five = (wide, mixer, narrow, wide, narrow)
    scratch = dict(
        w0=V((G, 2, 2, rw, D), BF), mx=V((G, 2, 2, rm, D), BF), n0=V((G, 2, 2, rn, VD), BF),
        w1=V((G, 2, 2, rw, D), BF), n1=V((G, 2, 2, rn, FF), BF), mc=V((MX // 5, D), BF),
        fin=V((4, NH, D), F32), ftot=V((G, NH, D), F32), fin2=V((4, NH, D), F32), ftot2=V((G, NH, D), F32),
        ob=V((4, T, VD), BF), oin=V((4, T, VD), BF), lout=V((4, 8, 128), F32), lin=V((4, 8, 128), F32),
        xb=V((G, T, D), BF), qb=V((4, T, ZD), BF), kb=V((G, T, ZD), BF), brow=V((4 * G + 8, 128), F32),
        mixed=V((T, MX), F32), pre=V((T, D), F32), keep=V((T // 8, NH, D), F32), att=V((T, VD), F32),
        s=V((4, T, G * T), F32), v=V((G * T, VD), BF), GV=V((2, G * T, VD), BF), XB=V((G, T, half), BF),
        GD=V((2, T, D), BF), EX=V((2, T, hv), BF), GU=V((2, T, FF), BF), LL=V((2, T, half), BF),
        GH=V((2, T, D), BF), GT=V((2, T, hv), BF), GM=V((2, T, MX), BF), PB=V((2, T, half), BF),
        GA=V((4, T, VD), BF), ST=V((4, 2, 8, 128), F32), P16=V((4, T, G * T), BF), GS=V((4, T, G * T), BF),
        QP=V((4, T, ZD), F32), KS=V((4, T, ZD), F32), KP=V((G, T, ZD), F32), DP=V((G, T, ZD), F32),
        DX=V((G, T, D), BF), BP=V((G, T, D), BF), bp=V((T, D), F32),
        AV=V((64, D), F32), AS=V((64, D), F32), AW=V((64, D), F32), AT=V((64, D), F32),
        AP=V((4, 8, D), F32), AL=V((G, 8, D), F32), prof=V((4 * G + 8, 128), F32),
        rp=V((4, 8, D), F32), rl=V((G, 8, D), F32), up=V((4, 8, 128), F32), ul=V((G, 8, 128), F32),
    )
    for i, (r, w) in enumerate(five):
        name = ("0", "M", "N0", "1", "N1")[i]
        plane = FLOW + 10 * i in ORDER
        scratch["R" + name] = V((3, 1 if plane else G, r, w), BF)
        scratch["L" + name] = V((G + 1, 2, 2, r, w) if plane else (G, r, w), BF)
    for name, (r, w) in zip(("F0", "FM", "FN0", "F1", "FN1"), five):
        scratch[name] = V((r, 2 * w), F32)
    for name, (r, w) in zip(("PA", "P0", "PM", "PN0", "P1", "PN1"), ((8, D),) + five):
        scratch[name] = V((count, r, w) if count > 1 else (8, 128), F32)
    slots = 80 + 50 * G + 6 * count
    scratch.update(
        agss=S((5, gather_slots(G))), agrs=S((5, gather_slots(G))), ssem=S((slots,)), rsem=S((slots,)), outs=S((5,))
    )
    result = pl.pallas_call(
        functools.partial(main_kernel, G, count, tuple(ins), tuple(outs), tuple(scratch)),
        out_shape=tuple(outs.values()),
        in_specs=[vm] * len(ins),
        out_specs=out_specs,
        scratch_shapes=list(scratch.values()),
        compiler_params=pltpu.CompilerParams(collective_id=1, has_side_effects=True, vmem_limit_bytes=59 * 2**20),
    )(*ins.values())
    return dict(zip(outs, result))


def matrices(G, gm_ref, gw_ref, gn_ref, wm_ref, ww_ref, wn_ref):
    r0, r1, r2 = (t // (4 * G) for t in (MX, VD, D))
    return [
        (lambda: gm_ref[0:r0], lambda: wm_ref[0:r0], MX, D),
        (lambda: gw_ref[0, 0:r1], lambda: ww_ref[0, 0:r1], VD, D),
        (lambda: gw_ref[1, 0:r1], lambda: ww_ref[1, 0:r1], VD, D),
        (lambda: gn_ref[0, 0:r2], lambda: wn_ref[0, 0:r2], D, VD),
        (lambda: gn_ref[1, 0:r2], lambda: wn_ref[1, 0:r2], D, VD),
    ]


def raw_averager(avg, ma_ref):
    damp = sigmoid(avg[0])
    mix = sigmoid(avg[1])
    d_dec, d_inf, d_out = ma_ref[0], ma_ref[1], ma_ref[2]
    return [
        (-mix * d_dec + avg[2] * d_inf) * damp * (1.0 - damp),
        -damp * d_dec * mix * (1.0 - mix),
        damp * d_inf,
        d_out * NH ** (-0.5),
    ]


def step_kernel(
    G,
    gm_ref, gw_ref, gn_ref, sum_ref, ma_ref, wm_ref, ww_ref, wn_ref, rm_ref, rw_ref, rn_ref, cm_ref, cw_ref, cn_ref, scal_ref,
    vec_ref, vmom_ref, avg_ref, amom_ref, block_ref, tok_ref,
    gm_o, gw_o, gn_o, vg_o, ag_o, nm_o, nw_o, nn_o, nv_o, na_o, rm_o, cm_o, rw_o, cw_o, rn_o, cn_o, vmom_o, amom_o, clip_o,
    block_o, tok_o,
    s96,
):
    block_o[...] = block_ref[...]
    tok_o[...] = tok_ref[...]
    rate = 1.0 - STEP ** (-0.8)
    lane = lax.broadcasted_iota(jnp.int32, (1, 128), 1)

    def scalar(row, i):
        return jnp.sum(jnp.where(lane == i, scal_ref[row : row + 1], 0.0))

    factor = scalar(4, 0)
    clip_o[...] = scal_ref[3:4, 0:1]
    rm_o[...] = rm_ref[...]
    rw_o[...] = rw_ref[...]
    rn_o[...] = rn_ref[...]
    cm_o[...] = cm_ref[...]
    cw_o[...] = cw_ref[...]
    cn_o[...] = cn_ref[...]
    mats = matrices(G, gm_ref, gw_ref, gn_ref, wm_ref, ww_ref, wn_ref)
    stats = [
        (rm_ref[0:1], cm_ref[...].T, gm_o, nm_o, None), (rw_ref[0:1], cw_ref[0:1].T, gw_o, nw_o, 0),
        (rw_ref[1:2], cw_ref[1:2].T, gw_o, nw_o, 1), (rn_ref[0:1], cn_ref[0:1].T, gn_o, nn_o, 0),
        (rn_ref[1:2], cn_ref[1:2].T, gn_o, nn_o, 1),
    ]
    for i, (g, w, total, width) in enumerate(mats):
        rnew, cnew, go, no, k = stats[i]
        entries = total * width
        rms_u = jnp.sqrt(scalar(0, i) / entries)
        rms_w = jnp.sqrt(scalar(1, i) / entries)
        scale = RATE * jnp.maximum(EPS_TWO, rms_w) / jnp.maximum(1.0, rms_u / CLIP_UPDATE)
        gv = factor * g()
        new = w() - scale * (gv * lax.rsqrt(rnew * cnew / scalar(2, i)))
        if k is None:
            go[...] = gv
            no[...] = new
        else:
            go[k] = gv
            no[k] = new
    for r in range(16):
        for j in range(D // 128):
            s96[r * (D // 128) + j : r * (D // 128) + j + 1] = sum_ref[r : r + 1, j * 128 : (j + 1) * 128]
    gv = factor * s96[...]
    vg_o[...] = gv
    mom = rate * vmom_ref[...] + (1.0 - rate) * (gv * gv + EPS_ONE)
    vmom_o[...] = mom
    u = gv * lax.rsqrt(mom)
    rms_u = jnp.sqrt(jnp.sum(u * u) / NVEC)
    wv = vec_ref[...]
    rms_w = jnp.sqrt(jnp.sum(wv * wv) / NVEC)
    nv_o[...] = wv - RATE * jnp.maximum(EPS_TWO, rms_w) * (u / jnp.maximum(1.0, rms_u / CLIP_UPDATE))
    avg = [avg_ref[i] for i in range(4)]
    raw = raw_averager(avg, ma_ref)
    us, su, sw = [], 0.0, 0.0
    for i in range(4):
        gv = factor * raw[i]
        ag_o[i] = gv
        mom = rate * amom_ref[i] + (1.0 - rate) * (gv * gv + EPS_ONE)
        amom_o[i] = mom
        u = gv * lax.rsqrt(mom)
        us.append(u)
        su = su + jnp.sum(u * u)
        sw = sw + jnp.sum(avg[i] * avg[i])
    count = 4 * D * NH
    scale = RATE * jnp.maximum(EPS_TWO, jnp.sqrt(sw / count)) / jnp.maximum(1.0, jnp.sqrt(su / count) / CLIP_UPDATE)
    for i in range(4):
        na_o[i] = avg[i] - scale * us[i]


def step_call(G, grads, masters, stats, vectors, vmom, avg, amom, block, tok):
    A = jax.ShapeDtypeStruct
    V = pltpu.VMEM
    vm = pl.BlockSpec(memory_space=pltpu.VMEM)
    r0, r1, r2 = (t // (4 * G) for t in (MX, VD, D))
    avgs, vecs = A((4, NH, D), F32), A((NVEC // 128, 128), F32)
    out_shape = (
        A((r0, D), F32), A((2, r1, D), F32), A((2, r2, VD), F32), vecs, avgs,
        A((r0, D), F32), A((2, r1, D), F32), A((2, r2, VD), F32), vecs, avgs,
        A((1, D), F32), A((1, r0), F32), A((2, D), F32), A((2, r1), F32), A((2, VD), F32), A((2, r2), F32),
        vecs, avgs, A((1, 1), F32), A(block.shape, F32), A(tok.shape, F32),
    )
    return pl.pallas_call(
        functools.partial(step_kernel, G),
        out_shape=out_shape,
        in_specs=[vm] * 21,
        out_specs=[vm] * 21,
        scratch_shapes=[V((NVEC // 128, 128), F32)],
        compiler_params=pltpu.CompilerParams(vmem_limit_bytes=56 * 2**20),
    )(*grads, *masters, *stats, vectors, vmom, avg, amom, block, tok)


def prologue(mixer_weight, widen_weight, narrow_weight, vectors, averager, bias_index):
    n = lax.axis_size("blk")
    mix = mixer_weight.T
    wid = jnp.swapaxes(widen_weight, 1, 2)
    nar = jnp.swapaxes(narrow_weight, 1, 2)
    avg = jnp.swapaxes(averager, 1, 2)
    index = jnp.pad(bias_index, (0, 1)).reshape(2 * n, 128)
    return mix, wid, nar, avg, vectors.reshape(NVEC // 128, 128), index


def carried_in(part, axis, combine, identity, reverse):
    count = lax.axis_size(axis)
    place = lax.axis_index(axis)
    ahead = count - 1 - place if reverse else place
    gathered = jax.tree.map(lambda a: lax.all_gather(a, axis), part)
    state = jax.tree.map(lambda a, e: jnp.zeros_like(a) + jnp.asarray(e, a.dtype), part, identity)

    def one(turn, state):
        source = count - 1 - turn if reverse else turn
        return combine(
            state, jax.tree.map(lambda a: lax.dynamic_index_in_dim(a, source, 0, False), gathered)
        )

    return lax.fori_loop(0, ahead, one, state)


def pieces(vectors):
    widths = (MX, VD, D, FF, D, D, D, D, D, D, 2 * ZD, 2 * ZD, NB)
    collected = []
    offset = 0
    for width in widths:
        collected.append(vectors[offset : offset + width])
        offset = offset + width
    return collected


def product(left_side, right_side, pattern):
    return jnp.einsum(pattern, left_side, right_side, preferred_element_type=jnp.float32)


def layer_norm(values, norm_gain, norm_shift):
    centered = values - jnp.mean(values, axis=-1, keepdims=True)
    inverse = lax.rsqrt(jnp.mean(centered * centered, axis=-1, keepdims=True) + EPS_NORM)
    normed = centered * inverse
    return (normed * norm_gain + norm_shift, normed, inverse)


def norm_back_sums(incoming, normed, inverse, norm_gain):
    scaled = incoming * norm_gain
    result = inverse * (
        scaled
        - jnp.mean(scaled, axis=-1, keepdims=True)
        - normed * jnp.mean(scaled * normed, axis=-1, keepdims=True)
    )
    return (result, jnp.sum(incoming * normed, axis=0), jnp.sum(incoming, axis=0))


def running(drive, decays, backward):
    result = drive
    factor = decays
    stride = 1
    total_rows = drive.shape[0]
    while stride < total_rows:
        padding = jnp.zeros((stride,) + drive.shape[1:], jnp.float32)
        if backward:
            shifted = jnp.concatenate([result[stride:], padding], axis=0)
        else:
            shifted = jnp.concatenate([padding, result[:-stride]], axis=0)
        result = result + factor * shifted
        factor = factor * factor
        stride = stride * 2
    return result


def compose(earlier, latter):
    return (earlier[0] * latter[0], latter[0] * earlier[1] + latter[1])


def toeplitz(profile, row_count, column_count):
    width_all = row_count + column_count
    tiled = jnp.tile(profile, row_count)[: row_count * (width_all - 1)]
    return tiled.reshape(row_count, width_all - 1)[:, row_count - 1 :]


def diagonal_sums(matrix):
    row_count, column_count = matrix.shape
    width_all = row_count + column_count
    padded = jnp.pad(matrix, ((0, 0), (row_count - 1, 0)))
    flattened = jnp.pad(padded.reshape(-1), (0, row_count))
    return jnp.sum(flattened.reshape(row_count, width_all), axis=0, dtype=jnp.float32)


def plain_update(weight, gradient, moment, decay_rate):
    moment_new = decay_rate * moment + (1.0 - decay_rate) * (gradient * gradient + EPS_ONE)
    update = gradient * lax.rsqrt(moment_new)
    rms_update = jnp.sqrt(jnp.mean(update * update))
    update = update / jnp.maximum(1.0, rms_update / CLIP_UPDATE)
    rms_weight = jnp.sqrt(jnp.mean(weight * weight))
    return (weight - RATE * jnp.maximum(EPS_TWO, rms_weight) * update, moment_new)


def with_collectives(
    tokens,
    cotangent,
    mixer_weight,
    widen_weight,
    narrow_weight,
    vectors,
    averager,
    bias_index,
    mixer_rows,
    mixer_cols,
    widen_rows,
    widen_cols,
    narrow_rows,
    narrow_cols,
    vector_moment,
    averager_moment,
):
    blocks = lax.axis_size("blk")
    position = lax.axis_index("blk")
    length = tokens.shape[1]
    full_length = length * blocks
    shards = (
        mixer_weight.astype(jnp.bfloat16),
        widen_weight.astype(jnp.bfloat16),
        narrow_weight.astype(jnp.bfloat16),
    )
    mixer_low, widen_low, narrow_low = (
        lax.all_gather(shards[0], "blk", axis=1, tiled=True),
        lax.all_gather(shards[1], "blk", axis=2, tiled=True),
        lax.all_gather(shards[2], "blk", axis=2, tiled=True),
    )
    (
        bias_mixer,
        bias_value,
        bias_hidden,
        bias_expand,
        bias_project,
        gain_one,
        shift_one,
        gain_two,
        shift_two,
        omega_scale,
        qk_gain,
        qk_shift,
        bias_table,
    ) = pieces(vectors)
    damping = jax.nn.sigmoid(averager[0])
    mixing = jax.nn.sigmoid(averager[1])
    decays = 1.0 - damping * mixing
    log_decay = jnp.log(decays)
    inflow = damping * averager[2]
    outflow = averager[3] * NH ** (-0.5)
    inputs = tokens[0]
    drive = inflow[None] * inputs[:, :, None]
    local_states = running(drive, decays, False)
    whole_decay = jnp.exp(log_decay * length)
    identity = (jnp.ones_like(decays), jnp.zeros_like(decays))
    entering = carried_in((whole_decay, local_states[-1]), "blk", compose, identity, False)[1]
    steps_ahead = (jnp.arange(length, dtype=jnp.int32) + 1).astype(jnp.float32)
    states = local_states + jnp.exp(log_decay[None] * steps_ahead[:, None, None]) * entering[None]
    pre_act = jnp.sum(states * outflow[None], axis=2) + omega_scale * inputs
    prime_low = jax.nn.silu(pre_act).astype(jnp.bfloat16)
    mixed_out = jnp.dot(prime_low, mixer_low, preferred_element_type=jnp.float32) + bias_mixer
    update_gate = jax.nn.sigmoid(mixed_out[:, :D])
    shared_pre = mixed_out[:, D : D + ZD]
    reset_pre = mixed_out[:, D + ZD : D + ZD + VD]
    hidden_x = mixed_out[:, D + ZD + VD :]
    shared = jax.nn.silu(shared_pre)
    reset_gate = jax.nn.silu(reset_pre)
    scaling = ZD ** (-0.5)
    queries = ((shared * qk_gain[:ZD] + qk_shift[:ZD]) * scaling).astype(jnp.bfloat16)
    key_rows = (shared * qk_gain[ZD:] + qk_shift[ZD:]).astype(jnp.bfloat16)
    inputs_low = inputs.astype(jnp.bfloat16)
    value_pre = jnp.dot(inputs_low, widen_low[0], preferred_element_type=jnp.float32) + bias_value
    value_rows = jax.nn.silu(value_pre).astype(jnp.bfloat16)
    key_all, value_all = (
        lax.all_gather(key_rows, "blk", axis=0, tiled=True),
        lax.all_gather(value_rows, "blk", axis=0, tiled=True),
    )
    buckets = jnp.arange(NB, dtype=jnp.int32)
    selector = (bias_index[:, None] == buckets[None, :]).astype(jnp.float32)
    bias_row = jnp.concatenate(
        [
            jnp.dot(selector, bias_table, precision=lax.Precision.HIGHEST),
            jnp.zeros((1,), jnp.float32),
        ]
    )
    begin = (blocks - 1 - position) * length
    profile = lax.dynamic_slice_in_dim(bias_row, begin, length + full_length)
    scores = product(queries, key_all, "qc,kc->qk") + toeplitz(profile, length, full_length)
    row_peak = jnp.max(scores, axis=1, keepdims=True)
    log_total = row_peak + jnp.log(jnp.sum(jnp.exp(scores - row_peak), axis=1, keepdims=True))
    softened = jnp.exp(scores - log_total)
    softened_low = softened.astype(jnp.bfloat16)
    attended = jnp.dot(softened_low, value_all, preferred_element_type=jnp.float32)
    gated_low = (reset_gate * attended).astype(jnp.bfloat16)
    hidden_pre = (
        hidden_x
        + jnp.dot(gated_low, narrow_low[0], preferred_element_type=jnp.float32)
        + bias_hidden
    )
    hidden_act = jax.nn.silu(hidden_pre)
    residual_one = inputs + update_gate * (hidden_act - inputs)
    layer_one, normed_one, inverse_one = layer_norm(residual_one, gain_one, shift_one)
    layer_low = layer_one.astype(jnp.bfloat16)
    expand_pre = jnp.dot(layer_low, widen_low[1], preferred_element_type=jnp.float32) + bias_expand
    expand_low = jax.nn.silu(expand_pre).astype(jnp.bfloat16)
    project_two = (
        jnp.dot(expand_low, narrow_low[1], preferred_element_type=jnp.float32) + bias_project
    )
    block_out, normed_two, inverse_two = layer_norm(layer_one + project_two, gain_two, shift_two)
    grad_second, gain_two_grad, shift_two_grad = norm_back_sums(
        cotangent[0], normed_two, inverse_two, gain_two
    )
    project_low = grad_second.astype(jnp.bfloat16)
    grad_down = product(expand_low, project_low, "tf,td->fd")
    expand_grad_low = (
        product(project_low, narrow_low[1], "td,fd->tf") * silu_grad(expand_pre)
    ).astype(jnp.bfloat16)
    grad_up = product(layer_low, expand_grad_low, "td,tf->df")
    grad_layer = grad_second + product(expand_grad_low, widen_low[1], "tf,df->td")
    grad_first, gain_one_grad, shift_one_grad = norm_back_sums(
        grad_layer, normed_one, inverse_one, gain_one
    )
    grad_update = grad_first * (hidden_act - inputs)
    hidden_grad_low = (grad_first * update_gate * silu_grad(hidden_pre)).astype(jnp.bfloat16)
    grad_hidden_weight = product(gated_low, hidden_grad_low, "tv,td->vd")
    grad_gated = product(hidden_grad_low, narrow_low[0], "td,vd->tv")
    grad_reset = grad_gated * attended
    attend_grad_low = (grad_gated * reset_gate).astype(jnp.bfloat16)
    grad_softened = product(attend_grad_low, value_all, "tv,kv->tk")
    row_inner = jnp.sum(softened * grad_softened, axis=1, keepdims=True)
    score_grad_low = (softened * (grad_softened - row_inner)).astype(jnp.bfloat16)
    grad_queries = product(score_grad_low, key_all, "tk,kc->tc")
    profile_grad = diagonal_sums(score_grad_low)
    partial_keys = product(score_grad_low, queries, "tk,tc->kc")
    partial_values = product(softened_low, attend_grad_low, "tk,tv->kv")
    grad_keys, grad_values = (
        lax.psum_scatter(partial_keys, "blk", scatter_dimension=0, tiled=True),
        lax.psum_scatter(partial_values, "blk", scatter_dimension=0, tiled=True),
    )
    grad_shared = grad_queries * scaling * qk_gain[:ZD] + grad_keys * qk_gain[ZD:]
    qk_gain_grad = jnp.concatenate(
        [jnp.sum(grad_queries * scaling * shared, axis=0), jnp.sum(grad_keys * shared, axis=0)]
    )
    qk_shift_grad = jnp.concatenate(
        [jnp.sum(grad_queries * scaling, axis=0), jnp.sum(grad_keys, axis=0)]
    )
    value_grad_low = (grad_values * silu_grad(value_pre)).astype(jnp.bfloat16)
    grad_value_weight = product(inputs_low, value_grad_low, "td,tv->dv")
    mixed_grad_low = jnp.concatenate(
        [
            grad_update * update_gate * (1.0 - update_gate),
            grad_shared * silu_grad(shared_pre),
            grad_reset * silu_grad(reset_pre),
            hidden_grad_low.astype(jnp.float32),
        ],
        axis=1,
    ).astype(jnp.bfloat16)
    grad_mixer_weight = product(prime_low, mixed_grad_low, "td,tm->dm")
    grad_pre = product(mixed_grad_low, mixer_low, "tm,dm->td") * silu_grad(pre_act)
    local_adjoint = running(outflow[None] * grad_pre[:, :, None], decays, True)
    leaving = carried_in((whole_decay, decays * local_adjoint[0]), "blk", compose, identity, True)[
        1
    ]
    steps_behind = (length - 1 - jnp.arange(length, dtype=jnp.int32)).astype(jnp.float32)
    adjoint = local_adjoint + jnp.exp(log_decay[None] * steps_behind[:, None, None]) * leaving[None]
    previous = jnp.concatenate([entering[None], states[:-1]], axis=0)
    grad_decay = jnp.sum(adjoint * previous, axis=0)
    grad_inflow = jnp.sum(adjoint * inputs[:, :, None], axis=0)
    grad_outflow = jnp.sum(grad_pre[:, :, None] * states, axis=0)
    tokens_grad = (
        grad_first * (1.0 - update_gate)
        + product(value_grad_low, widen_low[0], "tv,dv->td")
        + grad_pre * omega_scale
        + jnp.sum(adjoint * inflow[None], axis=2)
    )
    grad_damping = -mixing * grad_decay + averager[2] * grad_inflow
    average_grad = jnp.stack(
        [
            grad_damping * damping * (1.0 - damping),
            -damping * grad_decay * mixing * (1.0 - mixing),
            damping * grad_inflow,
            grad_outflow * NH ** (-0.5),
        ]
    )
    row_grad = lax.dynamic_update_slice(
        jnp.zeros((2 * full_length,), jnp.float32), profile_grad, (begin,)
    )
    table_grad = jnp.dot(row_grad[:-1], selector, precision=lax.Precision.HIGHEST)
    vector_local = jnp.concatenate(
        [
            jnp.sum(mixed_grad_low, axis=0, dtype=jnp.float32),
            jnp.sum(value_grad_low, axis=0, dtype=jnp.float32),
            jnp.sum(hidden_grad_low, axis=0, dtype=jnp.float32),
            jnp.sum(expand_grad_low, axis=0, dtype=jnp.float32),
            jnp.sum(project_low, axis=0, dtype=jnp.float32),
            gain_one_grad,
            shift_one_grad,
            gain_two_grad,
            shift_two_grad,
            jnp.sum(grad_pre * inputs, axis=0),
            qk_gain_grad,
            qk_shift_grad,
            table_grad,
        ]
    )
    full_grads = (
        grad_mixer_weight,
        jnp.stack([grad_value_weight, grad_up]),
        jnp.stack([grad_hidden_weight, grad_down]),
    )
    column_grads = (
        lax.psum_scatter(
            full_grads[0].astype(jnp.bfloat16), "blk", scatter_dimension=1, tiled=True
        ).astype(jnp.float32),
        lax.psum_scatter(
            full_grads[1].astype(jnp.bfloat16), "blk", scatter_dimension=2, tiled=True
        ).astype(jnp.float32),
        lax.psum_scatter(
            full_grads[2].astype(jnp.bfloat16), "blk", scatter_dimension=2, tiled=True
        ).astype(jnp.float32),
    )
    mixer_part, widen_part, narrow_part = (
        lax.psum(column_grads[0].astype(jnp.bfloat16), "dp").astype(jnp.float32),
        lax.psum(column_grads[1].astype(jnp.bfloat16), "dp").astype(jnp.float32),
        lax.psum(column_grads[2].astype(jnp.bfloat16), "dp").astype(jnp.float32),
    )
    vector_sum, average_sum = lax.psum((vector_local, average_grad), ("dp", "blk"))
    stacks = (mixer_part[None], widen_part, narrow_part)
    masters = (mixer_weight[None], widen_weight, narrow_weight)
    rows_old = (mixer_rows[None], widen_rows, narrow_rows)
    columns_old = (mixer_cols[None], widen_cols, narrow_cols)
    column_total = (MX, VD, D)
    local_square = jnp.sum(vector_sum * vector_sum) + jnp.sum(average_sum * average_sum)
    grad_squares = tuple((jnp.sum(matrix * matrix, axis=(1, 2)) for matrix in stacks))
    weight_squares = tuple((jnp.sum(matrix * matrix, axis=(1, 2)) for matrix in masters))
    decay_rate = 1.0 - STEP ** (-0.8)
    summed = lax.psum(grad_squares + weight_squares, "blk")
    clip_norm = jnp.sqrt(
        jnp.sum(summed[0]) + jnp.sum(summed[1]) + jnp.sum(summed[2]) + local_square
    )
    factor = jnp.minimum(1.0, CLIP_NORM / clip_norm)
    clipped = tuple((matrix * factor for matrix in stacks))
    squares = tuple((matrix * matrix + EPS_ONE for matrix in clipped))
    row_sums = lax.psum(tuple((jnp.sum(square_part, axis=2) for square_part in squares)), "blk")
    column_means = tuple((jnp.mean(square_part, axis=1) for square_part in squares))
    weight_total = summed[3:6]
    rows_new = tuple(
        (
            decay_rate * rows_old[member]
            + (1.0 - decay_rate) * row_sums[member] / column_total[member]
            for member in range(3)
        )
    )
    columns_new = tuple(
        (
            decay_rate * columns_old[member] + (1.0 - decay_rate) * column_means[member]
            for member in range(3)
        )
    )
    updates = tuple(
        (
            clipped[member]
            * lax.rsqrt(
                rows_new[member][:, :, None]
                * columns_new[member][:, None, :]
                / jnp.mean(rows_new[member], axis=1)[:, None, None]
            )
            for member in range(3)
        )
    )
    update_squares = lax.psum(
        tuple((jnp.sum(update * update, axis=(1, 2)) for update in updates)), "blk"
    )
    new_list = []
    for member in range(3):
        entries = rows_old[member].shape[1] * column_total[member]
        rms_update = jnp.sqrt(update_squares[member] / entries)
        bounded = updates[member] / jnp.maximum(1.0, rms_update / CLIP_UPDATE)[:, None, None]
        rms_weight = jnp.sqrt(weight_total[member] / entries)
        new_list.append(
            masters[member] - RATE * jnp.maximum(EPS_TWO, rms_weight)[:, None, None] * bounded
        )
    vector_grad = vector_sum * factor
    averager_grad = average_sum * factor
    vector_new, moment_vector = plain_update(vectors, vector_grad, vector_moment, decay_rate)
    averager_new, moment_averager = plain_update(
        averager, averager_grad, averager_moment, decay_rate
    )
    return (
        block_out[None],
        tokens_grad[None],
        clipped[0][0],
        clipped[1],
        clipped[2],
        vector_grad,
        averager_grad,
        new_list[0][0],
        new_list[1],
        new_list[2],
        vector_new,
        averager_new,
        rows_new[0][0],
        columns_new[0][0],
        rows_new[1],
        columns_new[1],
        rows_new[2],
        columns_new[2],
        moment_vector,
        moment_averager,
        clip_norm,
    )


def on_device(
    tokens, cotangent, mixer_weight, widen_weight, narrow_weight, vectors, averager, bias_index,
    mixer_rows, mixer_cols, widen_rows, widen_cols, narrow_rows, narrow_cols, vector_moment, averager_moment,
):
    G = lax.axis_size("blk") // 4
    count = lax.axis_size("dp") // 2
    mix, wid, nar, avg, vv, index = prologue(
        mixer_weight, widen_weight, narrow_weight, vectors, averager, bias_index
    )
    r = main_call(
        G, count, tokens[0], cotangent[0], mix, wid, nar, avg, vv, index, (mixer_rows[None], widen_rows, narrow_rows),
        (mixer_cols[None], widen_cols, narrow_cols),
    )
    out = step_call(
        G, (r["gm"], r["gw"], r["gn"], r["sums"], r["ma"]), (mix, wid, nar),
        (r["rm"], r["rw"], r["rn"], r["cm"], r["cw"], r["cn"], r["scal"]), vectors.reshape(NVEC // 128, 128),
        vector_moment.reshape(NVEC // 128, 128), avg, jnp.swapaxes(averager_moment, 1, 2), r["block"], r["tok"],
    )
    gm, gw, gn, vg, ag, nm, nw, nn, nv, na, rm, cm, rw, cw, rn, cn, vmom, amom, clip, block, tok = out
    ag, na, amom, gw, gn, nw, nn = (jnp.swapaxes(v, 1, 2) for v in (ag, na, amom, gw, gn, nw, nn))
    gm, nm = gm.T, nm.T
    return (
        block[None], tok[None], gm, gw, gn, vg.reshape(NVEC), ag, nm, nw, nn, nv.reshape(NVEC), na,
        rm[0], cm[0], rw, cw, rn, cn, vmom.reshape(NVEC), amom, clip[0, 0],
    )


def solution(mesh):
    in_specs = (
        P("dp", "blk", None), P("dp", "blk", None), P(None, "blk"), P(None, None, "blk"), P(None, None, "blk"),
        P(), P(), P(), P(), P("blk"), P(), P(None, "blk"), P(), P(None, "blk"), P(), P(),
    )
    out_specs = (
        P("dp", "blk", None), P("dp", "blk", None), P(None, "blk"), P(None, None, "blk"), P(None, None, "blk"),
        P(), P(), P(None, "blk"), P(None, None, "blk"), P(None, None, "blk"), P(), P(), P(), P("blk"), P(),
        P(None, "blk"), P(), P(None, "blk"), P(), P(), P(),
    )
    small = mesh.shape["dp"] % 2 == 0 and mesh.shape["blk"] in (8, 16)
    body = on_device if small else with_collectives
    return jax.shard_map(
        body, mesh=mesh, in_specs=in_specs, out_specs=out_specs, check_vma=False
    )
```

```python
import functools
import jax
import jax.numpy as jnp
from jax import lax
from jax.experimental import pallas as pl
from jax.experimental.pallas import tpu as pltpu
from jax.sharding import PartitionSpec as P

D = 768
ZD = 128
VD = 1536
FF = 1536
NH = 16
NB = 128
STEP = 10
MX = 3200
EPS_NORM = 1e-05
EPS_ONE = 1e-30
EPS_TWO = 0.001
CLIP_NORM = 1.0
CLIP_UPDATE = 1.0
RATE = 0.5

OFF_MX = 0
OFF_V = MX
OFF_H = OFF_V + VD
OFF_UP = OFF_H + D
OFF_DOWN = OFF_UP + FF
OFF_G1 = OFF_DOWN + D
OFF_S1 = OFF_G1 + D
OFF_G2 = OFF_S1 + D
OFF_S2 = OFF_G2 + D
OFF_OM = OFF_S2 + D
OFF_QG = OFF_OM + D
OFF_QS = OFF_QG + 2 * ZD
OFF_TB = OFF_QS + 2 * ZD
NVEC = OFF_TB + NB

MESH = pl.DeviceIdType.MESH
BF = jnp.bfloat16
F32 = jnp.float32
NN = (((1,), (0,)), ((), ()))
NT = (((1,), (1,)), ((), ()))
TN = (((0,), (0,)), ((), ()))


def dot(a, b, dims=NN):
    return lax.dot_general(a, b, dims, preferred_element_type=F32)


def sigmoid(v):
    return jax.nn.sigmoid(v)


def silu(v):
    return v * sigmoid(v)


def silu_grad(v):
    s = sigmoid(v)
    return s * (1.0 + v * (1.0 - s))


class Place:
    def __init__(self, lines):
        self.lines = lines
        self.dp = lax.axis_index("dp")
        blk = lax.axis_index("blk")
        self.blk = blk
        self.c = self.dp % 2
        self.g = blk // 4
        self.p = blk % 4
        self.b = self.p // 2
        self.a = self.p % 2
        self.na = 1 - self.a
        self.nb = 1 - self.b

    def sib(self):
        return (self.dp + 1 - 2 * self.c, self.blk)

    def at(self, g, b, a):
        return (self.dp, g * 4 + b * 2 + a)

    def line(self, k):
        return (self.g + k) % self.lines

    def plane(self, k):
        return (self.p + k) % 4

    def pick(self, first, second):
        return first + self.c * (second - first)


def vec(ref, off, width):
    rows = range(off // 128, (off + width) // 128)
    return jnp.concatenate([ref[r : r + 1] for r in rows], axis=1)


def greet(others):
    bar = pltpu.get_barrier_semaphore()
    for dev in others:
        pl.semaphore_signal(bar, inc=1, device_id=dev, device_id_type=MESH)


def greeted(others):
    pl.semaphore_wait(pltpu.get_barrier_semaphore(), len(others))


def close_peers(me):
    out = [me.sib()]
    for k in range(1, me.lines):
        out.append(me.at(me.line(k), me.b, me.a))
    for k in range(1, 4):
        q = me.plane(k)
        out.append(me.at(me.g, q // 2, q % 2))
    return out


def rcopy(src, dst, ssem, rsem, dev):
    return pltpu.make_async_remote_copy(
        src_ref=src, dst_ref=dst, send_sem=ssem, recv_sem=rsem, device_id=dev, device_id_type=MESH
    )


class Gather:
    def __init__(self, me, W, ssem, rsem):
        self.me, self.W, self.ssem, self.rsem = me, W, ssem, rsem
        self.half = W.shape[-1] // 2
        self.G = me.lines
        self.started = []
        self.maybe = []
        self.chained = set()
        self.by_plane = False

    def one(self, g, b, a, c):
        return self.W.at[g, b, a, :, pl.ds(pl.multiple_of(c * self.half, 128), self.half)]

    def go(self, src, slot, dev):
        cp = rcopy(src, src, self.ssem.at[slot], self.rsem.at[slot], dev)
        cp.start()
        self.started.append(cp)

    def await_in(self, ref, slot):
        rcopy(ref, ref, self.ssem.at[slot], self.rsem.at[slot], self.me.sib()).wait_recv()

    def near(self, j):
        me, G = self.me, self.G
        if j == 0:
            return me.g
        up = j - 1 + (me.g <= j - 1).astype(jnp.int32)
        down = G - j - (me.g >= G - j).astype(jnp.int32)
        low = (me.g < G // 2).astype(jnp.int32)
        return low * up + (1 - low) * down

    def along(self, h, way):
        me = self.me
        to = me.g + way
        up = jnp.asarray(way > 0, jnp.int32)
        ok = jnp.logical_and(to >= 0, to < self.G)
        src = self.one(h, me.b, me.a, me.c)
        cp = rcopy(
            src, src, self.ssem.at[8 * self.G + h + self.G * up], self.rsem.at[h], me.at(jnp.clip(to, 0, self.G - 1), me.b, me.a)
        )
        pl.when(ok)(cp.start)
        self.maybe.append((ok, cp))

    def z(self):
        self.along(self.me.g, 1)
        self.along(self.me.g, -1)

    def chain(self, j):
        if j > 0 and j not in self.chained:
            h = self.near(j)
            self.await_in(self.one(h, self.me.b, self.me.a, self.me.c), h)
            self.along(h, 2 * (h < self.me.g).astype(jnp.int32) - 1)
            self.chained.add(j)

    def first(self, j):
        me, G = self.me, self.G
        h = self.near(j)
        src = self.one(h, me.b, me.a, me.c)
        self.chain(j)
        self.go(src, G + h, me.at(me.g, me.b, me.na))
        self.go(src, 2 * G + h, me.at(me.g, me.nb, me.a))
        if j > 0:
            self.go(src, 4 * G + h, me.sib())

    def second(self, j):
        me, G = self.me, self.G
        h = self.near(j)
        x = self.one(h, me.b, me.na, me.c)
        y = self.one(h, me.nb, me.a, me.c)
        self.await_in(x, G + h)
        self.await_in(y, 2 * G + h)
        fwd = self.one(h, me.pick(me.b, me.nb), me.pick(me.na, me.a), me.c)
        self.go(fwd, 3 * G + h, me.at(me.g, me.pick(me.nb, me.b), me.pick(me.a, me.na)))
        self.go(x, 5 * G + h, me.sib())
        self.go(y, 6 * G + h, me.sib())

    def third(self, j):
        me, G = self.me, self.G
        h = self.near(j)
        d = self.one(h, me.nb, me.na, me.c)
        self.await_in(d, 3 * G + h)
        self.go(d, 7 * G + h, me.sib())

    def done(self):
        me, G = self.me, self.G
        o = 1 - me.c
        for j in range(G):
            h = self.near(j)
            if j > 0 and self.by_plane:
                self.await_in(self.bundle(h, o), 4 * G + h)
                continue
            if j > 0:
                self.await_in(self.one(h, me.b, me.a, o), 4 * G + h)
            self.await_in(self.one(h, me.b, me.na, o), 5 * G + h)
            self.await_in(self.one(h, me.nb, me.a, o), 6 * G + h)
            self.await_in(self.one(h, me.nb, me.na, o), 7 * G + h)

    def bundle(self, h, c):
        return self.W.at[h, :, :, :, pl.ds(pl.multiple_of(c * self.half, 128), self.half)]

    def bundle_along(self, h, way):
        me = self.me
        to = me.g + way
        up = jnp.asarray(way > 0, jnp.int32)
        ok = jnp.logical_and(to >= 0, to < self.G)
        src = self.bundle(h, me.c)
        cp = rcopy(
            src, src, self.ssem.at[8 * self.G + h + self.G * up], self.rsem.at[h], me.at(jnp.clip(to, 0, self.G - 1), me.b, me.a)
        )
        pl.when(ok)(cp.start)
        self.maybe.append((ok, cp))

    def bundle_out(self):
        self.by_plane = True
        self.bundle_along(self.me.g, 1)
        self.bundle_along(self.me.g, -1)

    def bundle_in(self, j):
        me, G = self.me, self.G
        h = self.near(j)
        src = self.bundle(h, me.c)
        self.await_in(src, h)
        self.bundle_along(h, 2 * (h < me.g).astype(jnp.int32) - 1)
        self.go(src, 4 * G + h, me.sib())

    def drain(self):
        for cp in self.started:
            cp.wait_send()
        for ok, cp in self.maybe:
            pl.when(ok)(cp.wait_send)
        self.started, self.maybe = [], []


def gather_slots(G):
    return 10 * G


def decays_of(avg_ref):
    damp = sigmoid(avg_ref[0])
    mix = sigmoid(avg_ref[1])
    dec = 1.0 - damp * mix
    return damp, mix, dec, damp * avg_ref[2], avg_ref[3] * NH ** (-0.5)


def power(v, n):
    while n > 1:
        v = v * v
        n = n // 2
    return v


def ma_pass(x_ref, h, dec, inf, outf, pre_ref, keep=None):
    def step(i, h):
        if keep is not None:
            keep[i] = h
        xs = x_ref[pl.ds(i * 8, 8), :]
        rows = []
        for r in range(8):
            h = dec * h + inf * xs[r : r + 1]
            if pre_ref is not None:
                rows.append(jnp.sum(outf * h, axis=0, keepdims=True))
        if pre_ref is not None:
            pre_ref[pl.ds(i * 8, 8), :] = jnp.concatenate(rows, axis=0)
        return h

    return lax.fori_loop(0, x_ref.shape[0] // 8, step, h)


def toeplitz_block(bias_ref, m):
    w = jnp.concatenate([bias_ref[pl.ds(m, 1), :], bias_ref[pl.ds(m + 1, 1), :]], axis=1)
    return pltpu.roll(jnp.broadcast_to(w, (128, 256)), 1, 1, stride=1, stride_axis=0)[:, 128:]


def as_rows(col):
    return jnp.broadcast_to(col, (128, 128)).T[0:8]


def as_col(rows):
    return jnp.broadcast_to(rows[0:1], (128, 128)).T[:, 0:1]


def attend_block(G, T, me, i, q_o, kall, v_o, brow, s_o, ob, lout, att_o):
    s = dot(q_o[i], kall, NT)
    tops = []
    for kk in range(G):
        m = 4 * kk - i + 3
        tops.append(toeplitz_block(brow, m))
    s = s + jnp.concatenate(tops, axis=1)
    s_o[i] = s
    top = jnp.max(s, axis=1, keepdims=True)
    e = jnp.exp(s - top)
    tot = jnp.sum(e, axis=1, keepdims=True)
    o = dot(e.astype(BF), v_o[...]) / tot
    if att_o is None:
        ob[i] = o.astype(BF)
    else:
        att_o[...] = o
    lout[i] = as_rows(top + jnp.log(tot))


class Link:
    def __init__(self, me, ssem, rsem):
        self.me, self.ssem, self.rsem = me, ssem, rsem
        self.used = 0
        self.started = []

    def slot(self, count=1):
        self.used += count
        return self.used - count

    def go(self, src, dst, slot, dev, sent=None):
        cp = rcopy(src, dst, self.ssem.at[slot if sent is None else sent], self.rsem.at[slot], dev)
        cp.start()
        self.started.append(cp)

    def got(self, ref, slot):
        rcopy(ref, ref, self.ssem.at[slot], self.rsem.at[slot], self.me.sib()).wait_recv()

    def drain(self):
        for cp in self.started:
            cp.wait_send()
        self.started = []

    def swap(self, src, dst):
        s = self.slot()
        self.go(src, dst, s, self.me.sib())
        return lambda: self.got(dst, s)

    def plane(self, src, dst):
        me = self.me
        slots = [self.slot() for _ in range(3)]
        for k in range(1, 4):
            q = (me.p + k) % 4
            self.go(src(q), dst(me.p), slots[k - 1], me.at(me.g, q // 2, q % 2))

        def wait():
            for k in range(1, 4):
                self.got(dst((me.p + 4 - k) % 4), slots[k - 1])

        return wait

    def line(self, src, dst):
        me, G = self.me, self.me.lines
        slots = [self.slot() for _ in range(G - 1)]
        for k in range(1, G):
            h = (me.g + k) % G
            self.go(src(h), dst(me.g), slots[k - 1], me.at(h, me.b, me.a))

        def wait():
            for k in range(1, G):
                self.got(dst((me.g + G - k) % G), slots[k - 1])

        return wait

    def pairs(self, src, dst, count):
        me = self.me
        slots = [self.slot() for _ in range(count - 1)]
        for k in range(1, count):
            d = (me.dp // 2 + k) % count
            self.go(src, dst(me.dp // 2), slots[k - 1], (2 * d + me.c, me.blk))

        def wait():
            for k in range(1, count):
                self.got(dst((me.dp // 2 + count - k) % count), slots[k - 1])

        return wait


class Reduce:
    def __init__(self, me, link, near, H, R, RL):
        self.me, self.link, self.near, self.H, self.R, self.RL = me, link, near, H, R, RL
        self.base = link.slot(6 * me.lines)
        self.by_plane = False
        self.s = (me.pick(me.nb, me.b), me.pick(me.a, me.na))
        self.m = (me.pick(me.b, me.nb), me.pick(me.na, me.a))

    def at(self, h):
        return 0 if self.by_plane else h

    def send(self, h, place, kind, to):
        self.link.go(
            self.H.at[h, place[0], place[1]], self.R.at[kind, self.at(h)], self.base + kind * self.me.lines + h,
            self.me.at(self.me.g, to[0], to[1]),
        )

    def got(self, h, kind):
        self.link.got(self.R.at[kind, self.at(h)], self.base + kind * self.me.lines + h)

    def add(self, h, place, kinds):
        total = self.H[h, place[0], place[1]].astype(F32)
        for kind in kinds:
            total = total + self.R[kind, self.at(h)].astype(F32)
        self.H[h, place[0], place[1]] = total.astype(BF)

    def behind(self, j):
        self.send(self.near(j), (self.me.nb, self.me.na), 0, self.s)

    def theirs(self, j):
        self.send(self.near(j), self.s, 1, self.s)

    def passed(self, j):
        h = self.near(j)
        self.got(h, 0)
        self.add(h, self.m, (0,))
        self.send(h, self.m, 2, self.m)

    def mine(self, j):
        me, h = self.me, self.near(j)
        self.got(h, 1)
        self.got(h, 2)
        self.add(h, (me.b, me.a), (1, 2))
        if j > 0 and not self.by_plane:
            self.link.go(
                self.H.at[h, me.b, me.a], self.RL.at[me.g], self.base + 3 * me.lines + me.g, me.at(h, me.b, me.a),
                self.base + 3 * me.lines + h,
            )

    def flow(self, j):
        me, G = self.me, self.me.lines
        h = self.near(j)
        self.by_plane = True
        base = self.base + 3 * G
        if j == 0:
            for slot, ok in ((h, me.g > 0), (G, me.g < G - 1)):
                pl.when(ok)(functools.partial(self.flow_in, h, slot))
            return
        up = (h > me.g).astype(jnp.int32)
        pl.when(jnp.where(up == 1, me.g > 0, me.g < G - 1))(functools.partial(self.flow_in, h, h))
        slot = jnp.where(h == me.g - 1, G, h)
        self.link.go(self.H.at[h], self.RL.at[slot], base + slot, me.at(me.g + 2 * up - 1, me.b, me.a), base + 2 * G + h)

    def flow_in(self, h, slot):
        self.link.got(self.RL.at[slot], self.base + 3 * self.me.lines + slot)
        self.H[h] = (self.H[h].astype(F32) + self.RL[slot].astype(F32)).astype(BF)

    def total(self):
        me = self.me
        if self.by_plane:
            return self.H[me.g, me.b, me.a].astype(F32)
        for k in range(1, me.lines):
            h = (me.g + k) % me.lines
            self.link.got(self.RL.at[h], self.base + 3 * me.lines + h)
        self.RL[me.g] = self.H[me.g, me.b, me.a]
        total = self.RL[0].astype(F32)
        for g in range(1, me.lines):
            total = total + self.RL[g].astype(F32)
        return total


def into_blocks(H, value, first, rows):
    n = 4 * H.shape[0]
    count = value.shape[0]
    value = value.astype(BF)
    if H.shape[3] == rows and first == 0 and count == n * rows:
        H[...] = value.reshape(H.shape)
        return
    for i in range(n):
        lo, hi = max(first, i * rows), min(first + count, (i + 1) * rows)
        if lo < hi:
            H[i // 4, (i // 2) % 2, i % 2, lo - i * rows : hi - i * rows] = value[lo - first : hi - first]


def norm(v):
    centered = v - jnp.mean(v, axis=-1, keepdims=True)
    inverse = lax.rsqrt(jnp.mean(centered * centered, axis=-1, keepdims=True) + EPS_NORM)
    return centered * inverse, inverse


def norm_back(incoming, normed, inverse, gain):
    scaled = incoming * gain
    return inverse * (
        scaled
        - jnp.mean(scaled, axis=-1, keepdims=True)
        - normed * jnp.mean(scaled * normed, axis=-1, keepdims=True)
    )


def down(v):
    return jnp.sum(v.astype(F32), axis=0, keepdims=True)


def put(ref, off, row):
    width, at = row.shape[1], 0
    while at < width:
        r, lane = (off + at) // D, (off + at) % D
        take = min(width - at, D - lane)
        ref[r : r + 1, lane : lane + take] = row[:, at : at + take]
        at += take


def ma_back_first(bp_ref, dec, outf, h):
    n8 = bp_ref.shape[0] // 8

    def step(i, h):
        bs = bp_ref[pl.ds((n8 - 1 - i) * 8, 8), :]
        for r in range(7, -1, -1):
            h = dec * (outf * bs[r : r + 1] + h)
        return h

    return lax.fori_loop(0, n8, step, h)


def ma_back(x_ref, bp_ref, keep_ref, leave, dec, inf, outf, tok_o, AV):
    n8 = x_ref.shape[0] // 8
    wide = 256
    for j in range(D // wide):
        sl = slice(j * wide, (j + 1) * wide)
        d, f, u = dec[:, sl], inf[:, sl], outf[:, sl]

        def step(i, carry):
            h, dd, di, du = carry
            at = n8 - 1 - i
            xs = x_ref[pl.ds(at * 8, 8), sl]
            bs = bp_ref[pl.ds(at * 8, 8), sl]
            states = [keep_ref[at, :, sl]]
            for r in range(8):
                states.append(d * states[-1] + f * xs[r : r + 1])
            rows = [None] * 8
            for r in range(7, -1, -1):
                adj = u * bs[r : r + 1] + h
                dd = dd + adj * states[r]
                di = di + adj * xs[r : r + 1]
                du = du + bs[r : r + 1] * states[r + 1]
                rows[r] = jnp.sum(f * adj, axis=0, keepdims=True)
                h = d * adj
            tok_o[pl.ds(at * 8, 8), sl] += jnp.concatenate(rows, axis=0)
            return h, dd, di, du

        zero = jnp.zeros((NH, wide), F32)
        _, dd, di, du = lax.fori_loop(0, n8, step, (leave[:, sl], zero, zero, zero))
        AV[16 : 16 + NH, sl] = dd
        AV[16 + NH : 16 + 2 * NH, sl] = di
        AV[16 + 2 * NH : 16 + 3 * NH, sl] = du


def diagonals(G, T, GS, prof):
    flip = (
        lax.broadcasted_iota(jnp.int32, (T, T), 0) + lax.broadcasted_iota(jnp.int32, (T, T), 1) == T - 1
    ).astype(F32).astype(BF)
    for i in range(4):
        turned = dot(flip, GS[i])
        for kk in range(G):
            m = 4 * kk - i + 3
            block = jnp.concatenate([turned[:, kk * T : (kk + 1) * T], jnp.zeros((T, T), F32)], axis=1)
            s = jnp.sum(pltpu.roll(block, 0, 1, stride=1, stride_axis=0), axis=0, keepdims=True)
            prof[m : m + 1] += s[:, :T]
            prof[m + 1 : m + 2] += s[:, T:]


def table_rows(G, me, prof, index_ref, AV):
    first_row = me.p - 4 * me.g - 4 + 4 * G
    total = jnp.zeros((NB, 128), F32)
    for r in range(4 * G + 1):
        hit = index_ref[pl.ds(first_row + r, 1), :] == lax.broadcasted_iota(jnp.int32, (NB, 128), 0)
        total = total + jnp.where(hit, prof[r : r + 1], 0.0)
    col = jnp.sum(total, axis=1, keepdims=True)
    put(AV, OFF_TB, as_rows(col)[0:1])


(
    SEND_X, AVERAGE_PLANE, AVERAGE, VALUES_0, VALUES_1, MIXING, BIAS_ROWS, MERGE, HIDDEN, FEED, FEED_OUT,
    BACK_UP, BACK_ONE, BACK_GATE, BACK_QUERIES, BACK_KEYS, SWAP_VALUES, VALUES_TO_TOKENS, GRADS_VALUES,
    BACK_SHARED, BACK_PRE, GRADS_MIXER, ADJOINT_FIRST, ADJOINT_PLANE, ADJOINT, DIAGONALS, TABLE_ROWS,
    SUMS_CORE, SUMS_PLANE, SUMS_LINE, SUMS_BACK, SUMS_ALL, ADD_VALUES, STATS, GRADS_DOWN, GRADS_UP,
    GRADS_HIDDEN,
) = range(37)
(
    FIRST, SECOND, THIRD, CHAIN, BUNDLE_IN, BEHIND, THEIRS, PASSED, MINE, FLOW, ALONG, BUNDLE_OUT, READY,
    CLOSE, ATTEND, ATTEND_BACK, VALUES_BACK,
) = range(100, 1800, 100)
ORDER = (
    ALONG + 3, ALONG + 2, ALONG + 0, FIRST + 0, FIRST + 30, FIRST + 10, CHAIN + 31, CHAIN + 32, ALONG + 1,
    AVERAGE_PLANE, CHAIN + 1, FIRST + 31, FIRST + 40, SECOND + 0, SECOND + 10, FIRST + 1, CHAIN + 11, SECOND + 40,
    FIRST + 11, CHAIN + 12, FIRST + 20, SECOND + 31, SECOND + 1, FIRST + 12, CHAIN + 3, FIRST + 32, CHAIN + 21,
    CHAIN + 33, FIRST + 3, CHAIN + 2, FIRST + 2, FIRST + 33, BIAS_ROWS, CHAIN + 13, SECOND + 11, AVERAGE, CHAIN + 23,
    SEND_X, FIRST + 13, SECOND + 2, SECOND + 12, THIRD + 40, THIRD + 1, SECOND + 3, THIRD + 10, FIRST + 23,
    SECOND + 30, SECOND + 33, SECOND + 13, THIRD + 11, SECOND + 32, CHAIN + 22, THIRD + 30, THIRD + 12, THIRD + 2,
    FIRST + 21, BUNDLE_OUT + 4, SECOND + 20, THIRD + 33, THIRD + 0, THIRD + 31, SECOND + 23, FIRST + 22, THIRD + 13,
    THIRD + 3, READY + 1, MIXING, READY + 0, VALUES_0, SECOND + 22, VALUES_1, BUNDLE_IN + 41, SECOND + 21, THIRD + 20,
    ATTEND + 2, ATTEND + 1, THIRD + 32, BUNDLE_IN + 42, THIRD + 21, ATTEND + 3, THIRD + 22, THIRD + 23, READY + 3,
    ATTEND + 0, BUNDLE_IN + 43, READY + 2, MERGE, HIDDEN, FEED, READY + 4, FEED_OUT, BACK_UP, BACK_ONE, BACK_GATE,
    GRADS_DOWN, FLOW + 43, GRADS_HIDDEN, GRADS_UP, FLOW + 42, FLOW + 41, ATTEND_BACK + 2, THEIRS + 21, BEHIND + 22,
    ATTEND_BACK + 0, ATTEND_BACK + 1, THEIRS + 32, BEHIND + 21, ATTEND_BACK + 3, VALUES_BACK + 1, BACK_KEYS,
    VALUES_BACK + 2, THEIRS + 31, PASSED + 22, VALUES_BACK + 0, SWAP_VALUES, THEIRS + 30, BACK_QUERIES, BEHIND + 23,
    THEIRS + 22, THEIRS + 23, FLOW + 40, BEHIND + 20, BEHIND + 33, BEHIND + 32, DIAGONALS, VALUES_TO_TOKENS,
    BEHIND + 30, THEIRS + 40, PASSED + 23, BEHIND + 31, GRADS_VALUES, BEHIND + 2, PASSED + 33, THEIRS + 33,
    BACK_SHARED, PASSED + 21, PASSED + 32, THEIRS + 3, BACK_PRE, ADJOINT_FIRST, BEHIND + 3, BEHIND + 40, GRADS_MIXER,
    ADJOINT_PLANE, THEIRS + 2, PASSED + 3, THEIRS + 12, PASSED + 2, PASSED + 31, MINE + 22, MINE + 32, PASSED + 40,
    PASSED + 20, MINE + 21, PASSED + 30, BEHIND + 1, THEIRS + 11, MINE + 31, MINE + 40, MINE + 23, BEHIND + 12,
    MINE + 3, PASSED + 1, TABLE_ROWS, THEIRS + 1, MINE + 33, ADJOINT, BEHIND + 13, BEHIND + 11, ADD_VALUES, SUMS_CORE,
    THEIRS + 20, PASSED + 12, PASSED + 11, SUMS_PLANE, BEHIND + 10, BEHIND + 0, MINE + 12, MINE + 30, PASSED + 13,
    CLOSE + 4, MINE + 1, SUMS_LINE, THEIRS + 13, MINE + 2, MINE + 11, PASSED + 0, SUMS_BACK, MINE + 13, THEIRS + 10,
    PASSED + 10, CLOSE + 3, MINE + 20, SUMS_ALL, CLOSE + 2, THEIRS + 0, MINE + 10, MINE + 0, CLOSE + 0, CLOSE + 1,
    STATS,
)


class Refs:
    def __init__(self, names, refs):
        self.__dict__.update(zip(names, refs))


def main_kernel(G, count, in_names, out_names, scratch_names, *refs):
    a, b = len(in_names), len(in_names) + len(out_names)
    I, O, S = Refs(in_names, refs[:a]), Refs(out_names, refs[a:b]), Refs(scratch_names, refs[b:])
    me = Place(G)
    T = I.x.shape[0]
    o = 1 - me.c
    others = close_peers(me)
    for k in range(1, count):
        others.append((2 * ((me.dp // 2 + k) % count) + me.c, me.blk))
    greet(others)
    Ws = (S.w0, S.mx, S.n0, S.w1, S.n1)
    for W, src in zip(Ws, (I.wid.at[0], I.mix, I.nar.at[0], I.wid.at[1], I.nar.at[1])):
        r = src.shape[0]
        W[me.g, me.b, me.a, 0:r] = src[...].astype(BF)
        if r < W.shape[3]:
            W[me.g, me.b, me.a, r:] = jnp.zeros((W.shape[3] - r, W.shape[4]), BF)
    S.xb[me.g] = I.x[...].astype(BF)
    damp, mix, dec, inf, outf = decays_of(I.avg)
    zero = jnp.zeros((NH, D), F32)
    whole = power(dec, T)
    S.fin[me.p] = ma_pass(I.x, zero, dec, inf, outf, None)
    S.AV[...] = jnp.zeros_like(S.AV)
    S.prof[...] = jnp.zeros_like(S.prof)
    greeted(others)
    link = Link(me, S.ssem, S.rsem)
    got = {}
    val = {}
    ga = [Gather(me, W, S.agss.at[i], S.agrs.at[i]) for i, W in enumerate(Ws)]
    got["fin"] = link.plane(lambda q: S.fin.at[me.p], lambda q: S.fin.at[q])
    mixed = lambda off, w: S.mixed[:, off : off + w]
    vector = lambda off, w: vec(I.vec, off, w)
    scaling = ZD ** (-0.5)

    def cols(c, half):
        return pl.ds(pl.multiple_of(c * half, 128), half)

    def flat(W):
        return W[...].reshape(4 * G * W.shape[3], W.shape[4])

    def send_x():
        got["x"] = link.line(lambda h: S.xb.at[me.g], lambda h: S.xb.at[h])

    def average_plane():
        got.pop("fin")()
        tot = S.fin[0]
        for q in range(1, 4):
            tot = whole * tot + S.fin[q]
        S.ftot[me.g] = tot
        got["ftot"] = link.line(lambda h: S.ftot.at[me.g], lambda h: S.ftot.at[h])

    def average_second():
        got.pop("ftot")()
        ent = zero
        whole4 = power(whole, 4)
        for i in range(G - 1):
            ent = jnp.where(i < me.g, whole4 * ent + S.ftot[i], ent)
        for q in range(3):
            ent = jnp.where(q < me.p, whole * ent + S.fin[q], ent)
        ma_pass(I.x, ent, dec, inf, outf, S.pre, S.keep)
        S.pre[...] = S.pre[...] + vector(OFF_OM, D) * I.x[...]

    def values(i):
        if i == 0:
            got.pop("x")()
            got["xb"] = link.swap(S.xb.at[:, :, cols(o, D // 2)], S.XB)
        step = max(1, G // 2)
        wide = step * 4 * S.w0.shape[3]
        wblk = S.w0[i * step : (i + 1) * step].reshape(wide, D)
        sl = slice(i * wide, (i + 1) * wide)
        for gg in range(G):
            vp = dot(S.xb[gg], wblk, NT) + vector(OFF_V + i * wide, wide)
            S.GV[0, gg * T : (gg + 1) * T, sl] = silu_grad(vp).astype(BF)
            S.v[gg * T : (gg + 1) * T, sl] = silu(vp).astype(BF)

    chunk = MX // 5

    def mixer_rows(i):
        r = MX // (4 * G)
        at = 0
        for k in range(4 * G):
            lo, hi = max(i * chunk, k * r), min((i + 1) * chunk, (k + 1) * r)
            if lo < hi:
                S.mc[at : at + hi - lo] = S.mx[k // 4, (k // 2) % 2, k % 2, lo - k * r : hi - k * r]
                at += hi - lo
        return S.mc[...]

    def mixing():
        prime = silu(S.pre[...]).astype(BF)
        for i in (1, 0, 2, 3, 4):
            sl = slice(i * chunk, (i + 1) * chunk)
            S.mixed[:, sl] = dot(prime, mixer_rows(i), NT) + vector(OFF_MX + i * chunk, chunk)
            if i == 0:
                shared = silu(mixed(D, ZD))
                S.qb[me.p] = ((shared * vector(OFF_QG, ZD) + vector(OFF_QS, ZD)) * scaling).astype(BF)
                S.kb[me.g] = (shared * vector(OFF_QG + ZD, ZD) + vector(OFF_QS + ZD, ZD)).astype(BF)
                got["q"] = link.plane(lambda q: S.qb.at[me.p], lambda q: S.qb.at[q])
                got["k"] = link.line(lambda h: S.kb.at[me.g], lambda h: S.kb.at[h])

    def bias_rows():
        first_row = me.p - 4 * me.g - 4 + 4 * G
        table = jnp.broadcast_to(vector(OFF_TB, NB), (128, NB)).T
        for r in range(4 * G + 1):
            hit = I.index[pl.ds(first_row + r, 1), :] == lax.broadcasted_iota(jnp.int32, (NB, 128), 0)
            S.brow[r : r + 1] = jnp.sum(jnp.where(hit, table, 0.0), axis=0, keepdims=True)

    def attend(kk):
        if kk == 2:
            got.pop("q")()
            got.pop("k")()
            val["o"] = [link.slot(4), link.slot(4)]
        i = (me.p + kk) % 4
        kall = S.kb[...].reshape(G * T, ZD)
        attend_block(G, T, me, i, S.qb, kall, S.v, S.brow, S.s, S.ob, S.lout, S.att if kk == 0 else None)
        if kk:
            to = me.at(me.g, i // 2, i % 2)
            link.go(S.ob.at[i], S.oin.at[me.p], val["o"][0] + kk, to)
            link.go(S.lout.at[i], S.lin.at[me.p], val["o"][1] + kk, to)
        else:
            S.lin[me.p] = S.lout[me.p]

    def merge():
        for k in range(1, 4):
            link.got(S.oin.at[(me.p + 4 - k) % 4], val["o"][0] + k)
            link.got(S.lin.at[(me.p + 4 - k) % 4], val["o"][1] + k)
        ls = [as_col(S.lin[j]) for j in range(4)]
        peak = functools.reduce(jnp.maximum, ls)
        lse = peak + jnp.log(functools.reduce(jnp.add, [jnp.exp(l - peak) for l in ls]))
        S.att[...] = S.att[...] * jnp.exp(as_col(S.lout[me.p]) - lse)
        for k in range(1, 4):
            j = (me.p + k) % 4
            S.att[...] += S.oin[j].astype(F32) * jnp.exp(as_col(S.lin[j]) - lse)
        S.ST[me.p, 0] = as_rows(lse)
        link.drain()

    full = S.ob

    def share_half(k, width, dst):
        half = width // 2
        dst[0] = full[k, :, cols(me.c, half)]
        return link.swap(full.at[k, :, cols(o, half)], dst.at[1])

    def hidden():
        x = I.x[...]
        full[1, :, :D] = silu(S.pre[...]).astype(BF)
        got["pb"] = share_half(1, D, S.PB)
        full[0] = (silu(mixed(D + ZD, VD)) * S.att[...]).astype(BF)
        got["gt"] = share_half(0, VD, S.GT)
        hidden_pre = mixed(D + ZD + VD, D) + dot(full[0], flat(S.n0), NT) + vector(OFF_H, D)
        upd = sigmoid(mixed(0, D))
        act = silu(hidden_pre)
        one = x + upd * (act - x)
        n_one, r_one = norm(one)
        layer = n_one * vector(OFF_G1, D) + vector(OFF_S1, D)
        full[2, :, :D] = layer.astype(BF)
        got["ll"] = share_half(2, D, S.LL)
        val.update(x=x, hidden_pre=hidden_pre, upd=upd, act=act, n_one=n_one, r_one=r_one, layer=layer)

    def feed():
        val["expand_pre"] = dot(full[2, :, :D], flat(S.w1), NT) + vector(OFF_UP, FF)
        full[3] = silu(val["expand_pre"]).astype(BF)
        got["ex"] = share_half(3, FF, S.EX)

    def feed_out():
        two = val["layer"] + dot(full[3], flat(S.n1), NT) + vector(OFF_DOWN, D)
        n_two, r_two = norm(two)
        gain_two = vector(OFF_G2, D)
        O.block[...] = n_two * gain_two + vector(OFF_S2, D)
        cot = I.cot[...]
        val["back_two"] = norm_back(cot, n_two, r_two, gain_two)
        put(S.AV, OFF_G2, down(cot * n_two))
        put(S.AV, OFF_S2, down(cot))
        S.GD[0] = val["back_two"].astype(BF)
        got["gd"] = link.swap(S.GD.at[0], S.GD.at[1])
        put(S.AV, OFF_DOWN, down(S.GD[0]))

    def back_up():
        S.GU[0] = (dot(S.GD[0], flat(S.n1)) * silu_grad(val["expand_pre"])).astype(BF)
        got["gu"] = link.swap(S.GU.at[0], S.GU.at[1])
        put(S.AV, OFF_UP, down(S.GU[0]))

    def back_first():
        into_one = val["back_two"] + dot(S.GU[0], flat(S.w1))
        put(S.AV, OFF_G1, down(into_one * val["n_one"]))
        put(S.AV, OFF_S1, down(into_one))
        back_one = norm_back(into_one, val["n_one"], val["r_one"], vector(OFF_G1, D))
        S.GH[0] = (back_one * val["upd"] * silu_grad(val["hidden_pre"])).astype(BF)
        got["gh"] = link.swap(S.GH.at[0], S.GH.at[1])
        put(S.AV, OFF_H, down(S.GH[0]))
        val["back_one"] = back_one

    def back_gate():
        upd, back_one = val["upd"], val["back_one"]
        back_gated = dot(S.GH[0], flat(S.n0))
        S.GA[me.p] = (back_gated * silu(mixed(D + ZD, VD))).astype(BF)
        S.ST[me.p, 1] = as_rows(jnp.sum(S.GA[me.p].astype(F32) * S.att[...], axis=1, keepdims=True))
        got["ga"] = link.plane(lambda q: S.GA.at[me.p], lambda q: S.GA.at[q])
        got["st"] = link.plane(lambda q: S.ST.at[me.p], lambda q: S.ST.at[q])
        S.GM[0, :, 0:D] = (back_one * (val["act"] - val["x"]) * upd * (1.0 - upd)).astype(BF)
        S.GM[0, :, D + ZD : D + ZD + VD] = (back_gated * S.att[...] * silu_grad(mixed(D + ZD, VD))).astype(BF)
        S.GM[0, :, D + ZD + VD :] = S.GH[0]
        O.tok[...] = back_one * (1.0 - upd)

    Hs = [W.at[:, :, :, :, 0 : W.shape[-1] // 2] for W in Ws]
    near = ga[0].near
    red = [Reduce(me, link, near, H, R, L) for H, R, L in zip(Hs, (S.R0, S.RM, S.RN0, S.R1, S.RN1), (S.L0, S.LM, S.LN0, S.L1, S.LN1))]

    def both(ref):
        return ref[...].reshape(2 * T, ref.shape[-1])

    def grads(i, out, into, names):
        for name in names:
            got.pop(name)()
        ga[i].drain()
        rhs = both(into)
        for j in range(0, out.shape[-1], 384):
            lhs = out[:, :, j : j + 384].reshape(2 * T, 384)
            into_blocks(Hs[i], dot(lhs, rhs, TN), j, out.shape[-1] // (4 * G))

    def attend_back(kk):
        if kk == 2:
            got.pop("ga")()
            got.pop("st")()
        i = (me.p + kk) % 4
        probs = jnp.exp(S.s[i] - as_col(S.ST[i, 0]))
        back = dot(S.GA[i], S.v[...], NT)
        gs = (probs * (back - as_col(S.ST[i, 1]))).astype(BF)
        S.P16[i] = probs.astype(BF)
        S.GS[i] = gs
        S.QP[i] = dot(gs, S.kb[...].reshape(G * T, ZD))

    def back_queries():
        got["dq"] = link.plane(lambda q: S.QP.at[q], lambda q: S.KS.at[q])

    def back_keys():
        S.KP[...] = dot(S.GS[...].reshape(4 * T, G * T), S.qb[...].reshape(4 * T, ZD), TN).reshape(G, T, ZD)
        got["dk"] = link.line(lambda h: S.KP.at[h], lambda h: S.DP.at[h])

    def back_values(j):
        wide = VD // 3
        sl = slice(j * wide, (j + 1) * wide)
        dv = dot(S.P16[...].reshape(4 * T, G * T), S.GA[:, :, sl].reshape(4 * T, wide), TN)
        gv = (dv * S.GV[0, :, sl].astype(F32)).astype(BF)
        S.GV[0, :, sl] = gv
        put(S.AV, OFF_V + j * wide, down(gv))

    def swap_values():
        got["gv"] = link.swap(S.GV.at[0], S.GV.at[1])

    def values_to_tokens():
        for g in range(G):
            S.DX[g] = dot(S.GV[0, g * T : (g + 1) * T], flat(S.w0)).astype(BF)
        got["dx"] = link.line(lambda h: S.DX.at[h], lambda h: S.BP.at[h])

    def grads_values():
        got.pop("gv")()
        got.pop("xb")()
        ga[0].drain()
        own = S.xb[:, :, cols(me.c, D // 2)].reshape(G * T, D // 2)
        their = S.XB[...].reshape(G * T, D // 2)
        wide = VD // 4
        for j in range(4):
            sl = slice(j * wide, (j + 1) * wide)
            total = dot(S.GV[0, :, sl], own, TN) + dot(S.GV[1, :, sl], their, TN)
            into_blocks(Hs[0], total, j * wide, VD // (4 * G))

    def back_shared():
        got.pop("dq")()
        S.KS[me.p] = S.QP[me.p]
        back_q = (S.KS[0] + S.KS[1] + S.KS[2] + S.KS[3]) * scaling
        got.pop("dk")()
        S.DP[me.g] = S.KP[me.g]
        back_k = S.DP[0]
        for g in range(1, G):
            back_k = back_k + S.DP[g]
        sp = mixed(D, ZD)
        shared = silu(sp)
        put(S.AV, OFF_QG, down(back_q * shared))
        put(S.AV, OFF_QG + ZD, down(back_k * shared))
        put(S.AV, OFF_QS, down(back_q))
        put(S.AV, OFF_QS + ZD, down(back_k))
        back = back_q * vector(OFF_QG, ZD) + back_k * vector(OFF_QG + ZD, ZD)
        S.GM[0, :, D : D + ZD] = (back * silu_grad(sp)).astype(BF)
        got["gm"] = link.swap(S.GM.at[0], S.GM.at[1])
        put(S.AV, OFF_MX, down(S.GM[0]))

    def back_pre():
        back = jnp.zeros((T, D), F32)
        for i in range(5):
            back = back + dot(S.GM[0, :, i * chunk : (i + 1) * chunk], mixer_rows(i))
        back = back * silu_grad(S.pre[...])
        O.tok[...] += vector(OFF_OM, D) * back
        put(S.AV, OFF_OM, down(back * I.x[...]))
        S.bp[...] = back

    def grads_mixer():
        got.pop("gm")()
        got.pop("pb")()
        ga[1].drain()
        rhs = both(S.PB)
        for j in range(5):
            sl = slice(j * chunk, (j + 1) * chunk)
            into_blocks(Hs[1], dot(S.GM[:, :, sl].reshape(2 * T, chunk), rhs, TN), j * chunk, MX // (4 * G))

    def average_back():
        S.fin2[me.p] = ma_back_first(S.bp, dec, outf, zero)
        got["fin2"] = link.plane(lambda q: S.fin2.at[me.p], lambda q: S.fin2.at[q])

    def average_back_plane():
        got.pop("fin2")()
        tot = S.fin2[3]
        for q in (2, 1, 0):
            tot = whole * tot + S.fin2[q]
        S.ftot2[me.g] = tot
        got["ftot2"] = link.line(lambda h: S.ftot2.at[me.g], lambda h: S.ftot2.at[h])

    def average_back_second():
        got.pop("ftot2")()
        whole4 = power(whole, 4)
        leave = zero
        for i in range(G - 1, 0, -1):
            leave = jnp.where(i > me.g, whole4 * leave + S.ftot2[i], leave)
        for q in (3, 2, 1):
            leave = jnp.where(q > me.p, whole * leave + S.fin2[q], leave)
        ma_back(I.x, S.bp, S.keep, leave, dec, inf, outf, O.tok, S.AV)

    def pair_sum(value, buf):
        buf[me.dp // 2] = value
        link.pairs(buf.at[me.dp // 2], lambda d: buf.at[d], count)()
        value = buf[0]
        for d in range(1, count):
            value = value + buf[d]
        return value

    Fs = (S.F0, S.FM, S.FN0, S.F1, S.FN1)
    Ps = (S.P0, S.PM, S.PN0, S.P1, S.PN1)
    finish = []

    def close(i):
        F = Fs[i]
        total = red[i].total()
        half = total.shape[-1]
        if count > 1:
            total = pair_sum(total, Ps[i])
        F[:, cols(me.c, half)] = total
        part = F.at[:, cols(me.c, half)]
        s = link.slot()
        link.go(part, part, s, me.sib())
        finish.append(lambda: link.got(F.at[:, cols(o, half)], s))

    hr = S.AV.shape[0] // 2
    qr = hr // 4

    def rows_of(core, q, n):
        return pl.ds(pl.multiple_of(core * hr + q * qr, 8), n)

    def sums_core():
        got["av"] = link.swap(S.AV, S.AS)

    def sums_plane():
        got.pop("av")()
        S.AW[...] = S.AV[...] + S.AS[...]
        got["ap"] = link.plane(lambda q: S.AW.at[rows_of(me.c, q, qr), :], lambda q: S.AP.at[q])

    def sums_line():
        got.pop("ap")()
        S.AP[me.p] = S.AW[rows_of(me.c, me.p, qr), :]
        S.AL[me.g] = S.AP[0] + S.AP[1] + S.AP[2] + S.AP[3]
        got["al"] = link.line(lambda h: S.AL.at[me.g], lambda h: S.AL.at[h])

    def sums_back():
        got.pop("al")()
        tot = S.AL[0]
        for g in range(1, G):
            tot = tot + S.AL[g]
        if count > 1:
            tot = pair_sum(tot, S.PA)
        S.AT[rows_of(me.c, me.p, qr), :] = tot
        got["at"] = link.plane(lambda q: S.AT.at[rows_of(me.c, me.p, qr), :], lambda q: S.AT.at[rows_of(me.c, q, qr), :])

    def sums_all():
        got.pop("at")()
        s = link.slot()
        mine = S.AT.at[rows_of(me.c, 0, hr), :]
        link.go(mine, mine, s, me.sib())
        finish.append(lambda: link.got(S.AT.at[rows_of(o, 0, hr), :], s))

    def add_values():
        got.pop("dx")()
        S.BP[me.g] = S.DX[me.g]
        for g in range(G):
            O.tok[...] += S.BP[g].astype(F32)

    def allsum(value, pb, lb):
        pb[me.p] = value
        link.plane(lambda q: pb.at[me.p], lambda q: pb.at[q])()
        lb[me.g] = pb[0] + pb[1] + pb[2] + pb[3]
        link.line(lambda h: lb.at[me.g], lambda h: lb.at[h])()
        out = lb[0]
        for g in range(1, G):
            out = out + lb[g]
        return out

    def stats():
        for f in finish:
            f()
        O.sums[...] = S.AT[0:16]
        O.ma[...] = S.AT[16:64].reshape(3, NH, D)
        for F, dst, i in zip(Fs, (O.gw.at[0], O.gm, O.gn.at[0], O.gw.at[1], O.gn.at[1]), range(5)):
            pltpu.make_async_copy(F, dst, S.outs.at[i]).start()
        adafactor_stats(G, I, O, S, allsum)
        for F, dst, i in zip(Fs, (O.gw.at[0], O.gm, O.gn.at[0], O.gw.at[1], O.gn.at[1]), range(5)):
            pltpu.make_async_copy(F, dst, S.outs.at[i]).wait()

    one = {
        SEND_X: send_x, AVERAGE_PLANE: average_plane, AVERAGE: average_second, VALUES_0: lambda: values(0),
        VALUES_1: lambda: values(1), MIXING: mixing, BIAS_ROWS: bias_rows, MERGE: merge, HIDDEN: hidden, FEED: feed,
        FEED_OUT: feed_out, BACK_UP: back_up, BACK_ONE: back_first, BACK_GATE: back_gate, BACK_QUERIES: back_queries,
        BACK_KEYS: back_keys, SWAP_VALUES: swap_values, VALUES_TO_TOKENS: values_to_tokens, GRADS_VALUES: grads_values,
        BACK_SHARED: back_shared, BACK_PRE: back_pre, GRADS_MIXER: grads_mixer, ADJOINT_FIRST: average_back,
        ADJOINT_PLANE: average_back_plane, ADJOINT: average_back_second,
        DIAGONALS: lambda: diagonals(G, T, S.GS, S.prof), TABLE_ROWS: lambda: table_rows(G, me, S.prof, I.index, S.AV),
        SUMS_CORE: sums_core, SUMS_PLANE: sums_plane, SUMS_LINE: sums_line, SUMS_BACK: sums_back, SUMS_ALL: sums_all,
        ADD_VALUES: add_values, STATS: stats,
        GRADS_DOWN: lambda: grads(4, S.GD, S.EX, ("gd", "ex")), GRADS_UP: lambda: grads(3, S.GU, S.LL, ("gu", "ll")),
        GRADS_HIDDEN: lambda: grads(2, S.GH, S.GT, ("gh", "gt")),
    }
    part = {
        CHAIN: lambda i, j: ga[i].chain(j), FIRST: lambda i, j: ga[i].first(j), SECOND: lambda i, j: ga[i].second(j),
        THIRD: lambda i, j: ga[i].third(j), BEHIND: lambda i, j: red[i].behind(j), THEIRS: lambda i, j: red[i].theirs(j),
        PASSED: lambda i, j: red[i].passed(j), MINE: lambda i, j: red[i].mine(j), BUNDLE_IN: lambda i, j: ga[i].bundle_in(j),
        FLOW: lambda i, j: red[i].flow(j),
    }
    single = {
        ATTEND: attend, ATTEND_BACK: attend_back, ALONG: lambda i: ga[i].z(), BUNDLE_OUT: lambda i: ga[i].bundle_out(),
        READY: lambda i: ga[i].done(), CLOSE: close, VALUES_BACK: back_values,
    }
    for step in ORDER:
        kind, rest = step - step % 100, step % 100
        if kind == 0:
            one[step]()
        elif kind in single:
            single[kind](rest)
        else:
            part[kind](rest // 10, rest % 10)
    for gather in ga:
        gather.drain()
    link.drain()


def adafactor_stats(G, I, O, S, allsum):
    rate = 1.0 - STEP ** (-0.8)
    mats = [
        (S.FM, vec(I.rm, 0, D), I.cm[...].T, MX, D, O.rm, O.cm, 0),
        (S.F0, I.rw[0:1], I.cw[0:1].T, VD, D, O.rw, O.cw, 0),
        (S.F1, I.rw[1:2], I.cw[1:2].T, VD, D, O.rw, O.cw, 1),
        (S.FN0, I.rn[0:1], I.cn[0:1].T, D, VD, O.rn, O.cn, 0),
        (S.FN1, I.rn[1:2], I.cn[1:2].T, D, VD, O.rn, O.cn, 1),
    ]
    masters = (I.mix, I.wid.at[0], I.wid.at[1], I.nar.at[0], I.nar.at[1])
    lanes = lax.broadcasted_iota(jnp.int32, (1, D), 1)
    rows, cs, extra = [], [], jnp.zeros((1, D), F32)
    for i, (F, _, _, total, width, _, _, _) in enumerate(mats):
        sq = F[0 : total // (4 * G)]
        sq = sq * sq
        s = jnp.sum(sq, axis=0, keepdims=True)
        for j in range(width // D):
            rows.append(s[:, j * D : (j + 1) * D])
        cs.append(jnp.sum(sq, axis=1, keepdims=True))
        wv = masters[i][...]
        extra = jnp.where(lanes == i, jnp.sum(wv * wv), extra)
    rows.append(extra)
    small = jnp.sum(O.sums[...] * O.sums[...])
    for v in raw_averager([I.avg[i] for i in range(4)], O.ma):
        small = small + jnp.sum(v * v)
    tot = allsum(jnp.concatenate(rows, axis=0), S.rp, S.rl)
    length = jnp.sqrt(jnp.sum(tot[0:7]) + small)
    factor = jnp.minimum(1.0, CLIP_NORM / length)
    at = 0
    squares = jnp.zeros((1, 128), F32)
    means = jnp.zeros((1, 128), F32)
    lane = lanes[:, :128]
    for i, (F, ro, co, total, width, rows_o, cols_o, k) in enumerate(mats):
        row = jnp.concatenate([tot[at + j : at + j + 1] for j in range(width // D)], axis=1)
        at += width // D
        rnew = rate * ro + (1.0 - rate) * (factor * factor * row / total + EPS_ONE)
        cnew = rate * co + (1.0 - rate) * (factor * factor * cs[i] / width + EPS_ONE)
        mean = jnp.sum(rnew) / width
        u = factor * F[0 : total // (4 * G)] * lax.rsqrt(rnew * cnew / mean)
        squares = jnp.where(lane == i, jnp.sum(u * u), squares)
        means = jnp.where(lane == i, mean, means)
        rows_o[k : k + 1] = rnew
        cols_o[k : k + 1] = cnew.T
    sums = allsum(jnp.broadcast_to(squares, (8, 128)), S.up, S.ul)
    O.scal[0:1] = sums[0:1]
    O.scal[1:2] = tot[7:8, :128]
    O.scal[2:3] = means
    O.scal[3:4] = jnp.full((1, 128), length, F32)
    O.scal[4:5] = jnp.full((1, 128), factor, F32)
    O.scal[5:8] = jnp.zeros((3, 128), F32)


def main_call(G, count, x, cot, mix, wid, nar, avg, vv, index, rows, cols):
    T = x.shape[0]
    r0, r1, r2 = (t // (4 * G) for t in (MX, VD, D))
    rm, rw, rn = (r + -r % 16 for r in (r0, r1, r2))
    A = jax.ShapeDtypeStruct
    V = pltpu.VMEM
    half, hv = D // 2, VD // 2
    vm = pl.BlockSpec(memory_space=pltpu.VMEM)
    hbm = pl.BlockSpec(memory_space=pl.ANY)
    S = pltpu.SemaphoreType.DMA
    ins = dict(
        x=x, cot=cot, mix=mix, wid=wid, nar=nar, avg=avg, vec=vv, index=index,
        rm=rows[0], rw=rows[1], rn=rows[2], cm=cols[0], cw=cols[1], cn=cols[2],
    )
    outs = dict(
        block=A((T, D), F32), tok=A((T, D), F32), gm=A((rm, D), F32), gw=A((2, rw, D), F32), gn=A((2, rn, VD), F32),
        sums=A((16, D), F32), ma=A((3, NH, D), F32), rm=A((1, D), F32), rw=A((2, D), F32), rn=A((2, VD), F32),
        cm=A((1, r0), F32), cw=A((2, r1), F32), cn=A((2, r2), F32), scal=A((8, 128), F32),
    )
    out_specs = [hbm if name in ("gm", "gw", "gn") else vm for name in outs]
    wide, narrow, mixer = (rw, half), (rn, hv), (rm, half)
    five = (wide, mixer, narrow, wide, narrow)
    scratch = dict(
        w0=V((G, 2, 2, rw, D), BF), mx=V((G, 2, 2, rm, D), BF), n0=V((G, 2, 2, rn, VD), BF),
        w1=V((G, 2, 2, rw, D), BF), n1=V((G, 2, 2, rn, FF), BF), mc=V((MX // 5, D), BF),
        fin=V((4, NH, D), F32), ftot=V((G, NH, D), F32), fin2=V((4, NH, D), F32), ftot2=V((G, NH, D), F32),
        ob=V((4, T, VD), BF), oin=V((4, T, VD), BF), lout=V((4, 8, 128), F32), lin=V((4, 8, 128), F32),
        xb=V((G, T, D), BF), qb=V((4, T, ZD), BF), kb=V((G, T, ZD), BF), brow=V((4 * G + 8, 128), F32),
        mixed=V((T, MX), F32), pre=V((T, D), F32), keep=V((T // 8, NH, D), F32), att=V((T, VD), F32),
        s=V((4, T, G * T), F32), v=V((G * T, VD), BF), GV=V((2, G * T, VD), BF), XB=V((G, T, half), BF),
        GD=V((2, T, D), BF), EX=V((2, T, hv), BF), GU=V((2, T, FF), BF), LL=V((2, T, half), BF),
        GH=V((2, T, D), BF), GT=V((2, T, hv), BF), GM=V((2, T, MX), BF), PB=V((2, T, half), BF),
        GA=V((4, T, VD), BF), ST=V((4, 2, 8, 128), F32), P16=V((4, T, G * T), BF), GS=V((4, T, G * T), BF),
        QP=V((4, T, ZD), F32), KS=V((4, T, ZD), F32), KP=V((G, T, ZD), F32), DP=V((G, T, ZD), F32),
        DX=V((G, T, D), BF), BP=V((G, T, D), BF), bp=V((T, D), F32),
        AV=V((64, D), F32), AS=V((64, D), F32), AW=V((64, D), F32), AT=V((64, D), F32),
        AP=V((4, 8, D), F32), AL=V((G, 8, D), F32), prof=V((4 * G + 8, 128), F32),
        rp=V((4, 8, D), F32), rl=V((G, 8, D), F32), up=V((4, 8, 128), F32), ul=V((G, 8, 128), F32),
    )
    for i, (r, w) in enumerate(five):
        name = ("0", "M", "N0", "1", "N1")[i]
        plane = FLOW + 10 * i in ORDER
        scratch["R" + name] = V((3, 1 if plane else G, r, w), BF)
        scratch["L" + name] = V((G + 1, 2, 2, r, w) if plane else (G, r, w), BF)
    for name, (r, w) in zip(("F0", "FM", "FN0", "F1", "FN1"), five):
        scratch[name] = V((r, 2 * w), F32)
    for name, (r, w) in zip(("PA", "P0", "PM", "PN0", "P1", "PN1"), ((8, D),) + five):
        scratch[name] = V((count, r, w) if count > 1 else (8, 128), F32)
    slots = 80 + 50 * G + 6 * count
    scratch.update(
        agss=S((5, gather_slots(G))), agrs=S((5, gather_slots(G))), ssem=S((slots,)), rsem=S((slots,)), outs=S((5,))
    )
    result = pl.pallas_call(
        functools.partial(main_kernel, G, count, tuple(ins), tuple(outs), tuple(scratch)),
        out_shape=tuple(outs.values()),
        in_specs=[vm] * len(ins),
        out_specs=out_specs,
        scratch_shapes=list(scratch.values()),
        compiler_params=pltpu.CompilerParams(collective_id=1, has_side_effects=True, vmem_limit_bytes=59 * 2**20),
    )(*ins.values())
    return dict(zip(outs, result))


def matrices(G, gm_ref, gw_ref, gn_ref, wm_ref, ww_ref, wn_ref):
    r0, r1, r2 = (t // (4 * G) for t in (MX, VD, D))
    return [
        (lambda: gm_ref[0:r0], lambda: wm_ref[0:r0], MX, D),
        (lambda: gw_ref[0, 0:r1], lambda: ww_ref[0, 0:r1], VD, D),
        (lambda: gw_ref[1, 0:r1], lambda: ww_ref[1, 0:r1], VD, D),
        (lambda: gn_ref[0, 0:r2], lambda: wn_ref[0, 0:r2], D, VD),
        (lambda: gn_ref[1, 0:r2], lambda: wn_ref[1, 0:r2], D, VD),
    ]


def raw_averager(avg, ma_ref):
    damp = sigmoid(avg[0])
    mix = sigmoid(avg[1])
    d_dec, d_inf, d_out = ma_ref[0], ma_ref[1], ma_ref[2]
    return [
        (-mix * d_dec + avg[2] * d_inf) * damp * (1.0 - damp),
        -damp * d_dec * mix * (1.0 - mix),
        damp * d_inf,
        d_out * NH ** (-0.5),
    ]


def step_kernel(
    G,
    gm_ref, gw_ref, gn_ref, sum_ref, ma_ref, wm_ref, ww_ref, wn_ref, rm_ref, rw_ref, rn_ref, cm_ref, cw_ref, cn_ref, scal_ref,
    vec_ref, vmom_ref, avg_ref, amom_ref, block_ref, tok_ref,
    gm_o, gw_o, gn_o, vg_o, ag_o, nm_o, nw_o, nn_o, nv_o, na_o, rm_o, cm_o, rw_o, cw_o, rn_o, cn_o, vmom_o, amom_o, clip_o,
    block_o, tok_o,
    s96,
):
    block_o[...] = block_ref[...]
    tok_o[...] = tok_ref[...]
    rate = 1.0 - STEP ** (-0.8)
    lane = lax.broadcasted_iota(jnp.int32, (1, 128), 1)

    def scalar(row, i):
        return jnp.sum(jnp.where(lane == i, scal_ref[row : row + 1], 0.0))

    factor = scalar(4, 0)
    clip_o[...] = scal_ref[3:4, 0:1]
    for r in range(D // 128):
        rm_o[r : r + 1] = rm_ref[:, r * 128 : (r + 1) * 128]
    rw_o[...] = rw_ref[...]
    rn_o[...] = rn_ref[...]
    cm_o[...] = cm_ref[...]
    cw_o[...] = cw_ref[...]
    cn_o[...] = cn_ref[...]
    mats = matrices(G, gm_ref, gw_ref, gn_ref, wm_ref, ww_ref, wn_ref)
    stats = [
        (rm_ref[0:1], cm_ref[...].T, gm_o, nm_o, None), (rw_ref[0:1], cw_ref[0:1].T, gw_o, nw_o, 0),
        (rw_ref[1:2], cw_ref[1:2].T, gw_o, nw_o, 1), (rn_ref[0:1], cn_ref[0:1].T, gn_o, nn_o, 0),
        (rn_ref[1:2], cn_ref[1:2].T, gn_o, nn_o, 1),
    ]
    for i, (g, w, total, width) in enumerate(mats):
        rnew, cnew, go, no, k = stats[i]
        entries = total * width
        rms_u = jnp.sqrt(scalar(0, i) / entries)
        rms_w = jnp.sqrt(scalar(1, i) / entries)
        scale = RATE * jnp.maximum(EPS_TWO, rms_w) / jnp.maximum(1.0, rms_u / CLIP_UPDATE)
        gv = factor * g()
        new = w() - scale * (gv * lax.rsqrt(rnew * cnew / scalar(2, i)))
        if k is None:
            go[...] = gv
            no[...] = new
        else:
            go[k] = gv
            no[k] = new
    for r in range(16):
        for j in range(D // 128):
            s96[r * (D // 128) + j : r * (D // 128) + j + 1] = sum_ref[r : r + 1, j * 128 : (j + 1) * 128]
    gv = factor * s96[...]
    vg_o[...] = gv
    mom = rate * vmom_ref[...] + (1.0 - rate) * (gv * gv + EPS_ONE)
    vmom_o[...] = mom
    u = gv * lax.rsqrt(mom)
    rms_u = jnp.sqrt(jnp.sum(u * u) / NVEC)
    wv = vec_ref[...]
    rms_w = jnp.sqrt(jnp.sum(wv * wv) / NVEC)
    nv_o[...] = wv - RATE * jnp.maximum(EPS_TWO, rms_w) * (u / jnp.maximum(1.0, rms_u / CLIP_UPDATE))
    avg = [avg_ref[i] for i in range(4)]
    raw = raw_averager(avg, ma_ref)
    us, su, sw = [], 0.0, 0.0
    for i in range(4):
        gv = factor * raw[i]
        ag_o[i] = gv
        mom = rate * amom_ref[i] + (1.0 - rate) * (gv * gv + EPS_ONE)
        amom_o[i] = mom
        u = gv * lax.rsqrt(mom)
        us.append(u)
        su = su + jnp.sum(u * u)
        sw = sw + jnp.sum(avg[i] * avg[i])
    count = 4 * D * NH
    scale = RATE * jnp.maximum(EPS_TWO, jnp.sqrt(sw / count)) / jnp.maximum(1.0, jnp.sqrt(su / count) / CLIP_UPDATE)
    for i in range(4):
        na_o[i] = avg[i] - scale * us[i]


def step_call(G, grads, masters, stats, vectors, vmom, avg, amom, block, tok):
    A = jax.ShapeDtypeStruct
    V = pltpu.VMEM
    vm = pl.BlockSpec(memory_space=pltpu.VMEM)
    r0, r1, r2 = (t // (4 * G) for t in (MX, VD, D))
    avgs, vecs = A((4, NH, D), F32), A((NVEC // 128, 128), F32)
    out_shape = (
        A((r0, D), F32), A((2, r1, D), F32), A((2, r2, VD), F32), vecs, avgs,
        A((r0, D), F32), A((2, r1, D), F32), A((2, r2, VD), F32), vecs, avgs,
        A((D // 128, 128), F32), A((1, r0), F32), A((2, D), F32), A((2, r1), F32), A((2, VD), F32), A((2, r2), F32),
        vecs, avgs, A((1, 1), F32), A(block.shape, F32), A(tok.shape, F32),
    )
    return pl.pallas_call(
        functools.partial(step_kernel, G),
        out_shape=out_shape,
        in_specs=[vm] * 21,
        out_specs=[vm] * 21,
        scratch_shapes=[V((NVEC // 128, 128), F32)],
        compiler_params=pltpu.CompilerParams(vmem_limit_bytes=56 * 2**20),
    )(*grads, *masters, *stats, vectors, vmom, avg, amom, block, tok)


def prologue(mixer_weight, widen_weight, narrow_weight, vectors, averager, bias_index):
    n = lax.axis_size("blk")
    mix = mixer_weight.T
    wid = jnp.swapaxes(widen_weight, 1, 2)
    nar = jnp.swapaxes(narrow_weight, 1, 2)
    avg = jnp.swapaxes(averager, 1, 2)
    index = jnp.pad(bias_index, (0, 1)).reshape(2 * n, 128)
    return mix, wid, nar, avg, vectors.reshape(NVEC // 128, 128), index


def carried_in(part, axis, combine, identity, reverse):
    count = lax.axis_size(axis)
    place = lax.axis_index(axis)
    ahead = count - 1 - place if reverse else place
    gathered = jax.tree.map(lambda a: lax.all_gather(a, axis), part)
    state = jax.tree.map(lambda a, e: jnp.zeros_like(a) + jnp.asarray(e, a.dtype), part, identity)

    def one(turn, state):
        source = count - 1 - turn if reverse else turn
        return combine(
            state, jax.tree.map(lambda a: lax.dynamic_index_in_dim(a, source, 0, False), gathered)
        )

    return lax.fori_loop(0, ahead, one, state)


def pieces(vectors):
    widths = (MX, VD, D, FF, D, D, D, D, D, D, 2 * ZD, 2 * ZD, NB)
    collected = []
    offset = 0
    for width in widths:
        collected.append(vectors[offset : offset + width])
        offset = offset + width
    return collected


def product(left_side, right_side, pattern):
    return jnp.einsum(pattern, left_side, right_side, preferred_element_type=jnp.float32)


def layer_norm(values, norm_gain, norm_shift):
    centered = values - jnp.mean(values, axis=-1, keepdims=True)
    inverse = lax.rsqrt(jnp.mean(centered * centered, axis=-1, keepdims=True) + EPS_NORM)
    normed = centered * inverse
    return (normed * norm_gain + norm_shift, normed, inverse)


def norm_back_sums(incoming, normed, inverse, norm_gain):
    scaled = incoming * norm_gain
    result = inverse * (
        scaled
        - jnp.mean(scaled, axis=-1, keepdims=True)
        - normed * jnp.mean(scaled * normed, axis=-1, keepdims=True)
    )
    return (result, jnp.sum(incoming * normed, axis=0), jnp.sum(incoming, axis=0))


def running(drive, decays, backward):
    result = drive
    factor = decays
    stride = 1
    total_rows = drive.shape[0]
    while stride < total_rows:
        padding = jnp.zeros((stride,) + drive.shape[1:], jnp.float32)
        if backward:
            shifted = jnp.concatenate([result[stride:], padding], axis=0)
        else:
            shifted = jnp.concatenate([padding, result[:-stride]], axis=0)
        result = result + factor * shifted
        factor = factor * factor
        stride = stride * 2
    return result


def compose(earlier, latter):
    return (earlier[0] * latter[0], latter[0] * earlier[1] + latter[1])


def toeplitz(profile, row_count, column_count):
    width_all = row_count + column_count
    tiled = jnp.tile(profile, row_count)[: row_count * (width_all - 1)]
    return tiled.reshape(row_count, width_all - 1)[:, row_count - 1 :]


def diagonal_sums(matrix):
    row_count, column_count = matrix.shape
    width_all = row_count + column_count
    padded = jnp.pad(matrix, ((0, 0), (row_count - 1, 0)))
    flattened = jnp.pad(padded.reshape(-1), (0, row_count))
    return jnp.sum(flattened.reshape(row_count, width_all), axis=0, dtype=jnp.float32)


def plain_update(weight, gradient, moment, decay_rate):
    moment_new = decay_rate * moment + (1.0 - decay_rate) * (gradient * gradient + EPS_ONE)
    update = gradient * lax.rsqrt(moment_new)
    rms_update = jnp.sqrt(jnp.mean(update * update))
    update = update / jnp.maximum(1.0, rms_update / CLIP_UPDATE)
    rms_weight = jnp.sqrt(jnp.mean(weight * weight))
    return (weight - RATE * jnp.maximum(EPS_TWO, rms_weight) * update, moment_new)


def with_collectives(
    tokens,
    cotangent,
    mixer_weight,
    widen_weight,
    narrow_weight,
    vectors,
    averager,
    bias_index,
    mixer_rows,
    mixer_cols,
    widen_rows,
    widen_cols,
    narrow_rows,
    narrow_cols,
    vector_moment,
    averager_moment,
):
    blocks = lax.axis_size("blk")
    position = lax.axis_index("blk")
    length = tokens.shape[1]
    full_length = length * blocks
    shards = (
        mixer_weight.astype(jnp.bfloat16),
        widen_weight.astype(jnp.bfloat16),
        narrow_weight.astype(jnp.bfloat16),
    )
    mixer_low, widen_low, narrow_low = (
        lax.all_gather(shards[0], "blk", axis=1, tiled=True),
        lax.all_gather(shards[1], "blk", axis=2, tiled=True),
        lax.all_gather(shards[2], "blk", axis=2, tiled=True),
    )
    (
        bias_mixer,
        bias_value,
        bias_hidden,
        bias_expand,
        bias_project,
        gain_one,
        shift_one,
        gain_two,
        shift_two,
        omega_scale,
        qk_gain,
        qk_shift,
        bias_table,
    ) = pieces(vectors)
    damping = jax.nn.sigmoid(averager[0])
    mixing = jax.nn.sigmoid(averager[1])
    decays = 1.0 - damping * mixing
    log_decay = jnp.log(decays)
    inflow = damping * averager[2]
    outflow = averager[3] * NH ** (-0.5)
    inputs = tokens[0]
    drive = inflow[None] * inputs[:, :, None]
    local_states = running(drive, decays, False)
    whole_decay = jnp.exp(log_decay * length)
    identity = (jnp.ones_like(decays), jnp.zeros_like(decays))
    entering = carried_in((whole_decay, local_states[-1]), "blk", compose, identity, False)[1]
    steps_ahead = (jnp.arange(length, dtype=jnp.int32) + 1).astype(jnp.float32)
    states = local_states + jnp.exp(log_decay[None] * steps_ahead[:, None, None]) * entering[None]
    pre_act = jnp.sum(states * outflow[None], axis=2) + omega_scale * inputs
    prime_low = jax.nn.silu(pre_act).astype(jnp.bfloat16)
    mixed_out = jnp.dot(prime_low, mixer_low, preferred_element_type=jnp.float32) + bias_mixer
    update_gate = jax.nn.sigmoid(mixed_out[:, :D])
    shared_pre = mixed_out[:, D : D + ZD]
    reset_pre = mixed_out[:, D + ZD : D + ZD + VD]
    hidden_x = mixed_out[:, D + ZD + VD :]
    shared = jax.nn.silu(shared_pre)
    reset_gate = jax.nn.silu(reset_pre)
    scaling = ZD ** (-0.5)
    queries = ((shared * qk_gain[:ZD] + qk_shift[:ZD]) * scaling).astype(jnp.bfloat16)
    key_rows = (shared * qk_gain[ZD:] + qk_shift[ZD:]).astype(jnp.bfloat16)
    inputs_low = inputs.astype(jnp.bfloat16)
    value_pre = jnp.dot(inputs_low, widen_low[0], preferred_element_type=jnp.float32) + bias_value
    value_rows = jax.nn.silu(value_pre).astype(jnp.bfloat16)
    key_all, value_all = (
        lax.all_gather(key_rows, "blk", axis=0, tiled=True),
        lax.all_gather(value_rows, "blk", axis=0, tiled=True),
    )
    buckets = jnp.arange(NB, dtype=jnp.int32)
    selector = (bias_index[:, None] == buckets[None, :]).astype(jnp.float32)
    bias_row = jnp.concatenate(
        [
            jnp.dot(selector, bias_table, precision=lax.Precision.HIGHEST),
            jnp.zeros((1,), jnp.float32),
        ]
    )
    begin = (blocks - 1 - position) * length
    profile = lax.dynamic_slice_in_dim(bias_row, begin, length + full_length)
    scores = product(queries, key_all, "qc,kc->qk") + toeplitz(profile, length, full_length)
    row_peak = jnp.max(scores, axis=1, keepdims=True)
    log_total = row_peak + jnp.log(jnp.sum(jnp.exp(scores - row_peak), axis=1, keepdims=True))
    softened = jnp.exp(scores - log_total)
    softened_low = softened.astype(jnp.bfloat16)
    attended = jnp.dot(softened_low, value_all, preferred_element_type=jnp.float32)
    gated_low = (reset_gate * attended).astype(jnp.bfloat16)
    hidden_pre = (
        hidden_x
        + jnp.dot(gated_low, narrow_low[0], preferred_element_type=jnp.float32)
        + bias_hidden
    )
    hidden_act = jax.nn.silu(hidden_pre)
    residual_one = inputs + update_gate * (hidden_act - inputs)
    layer_one, normed_one, inverse_one = layer_norm(residual_one, gain_one, shift_one)
    layer_low = layer_one.astype(jnp.bfloat16)
    expand_pre = jnp.dot(layer_low, widen_low[1], preferred_element_type=jnp.float32) + bias_expand
    expand_low = jax.nn.silu(expand_pre).astype(jnp.bfloat16)
    project_two = (
        jnp.dot(expand_low, narrow_low[1], preferred_element_type=jnp.float32) + bias_project
    )
    block_out, normed_two, inverse_two = layer_norm(layer_one + project_two, gain_two, shift_two)
    grad_second, gain_two_grad, shift_two_grad = norm_back_sums(
        cotangent[0], normed_two, inverse_two, gain_two
    )
    project_low = grad_second.astype(jnp.bfloat16)
    grad_down = product(expand_low, project_low, "tf,td->fd")
    expand_grad_low = (
        product(project_low, narrow_low[1], "td,fd->tf") * silu_grad(expand_pre)
    ).astype(jnp.bfloat16)
    grad_up = product(layer_low, expand_grad_low, "td,tf->df")
    grad_layer = grad_second + product(expand_grad_low, widen_low[1], "tf,df->td")
    grad_first, gain_one_grad, shift_one_grad = norm_back_sums(
        grad_layer, normed_one, inverse_one, gain_one
    )
    grad_update = grad_first * (hidden_act - inputs)
    hidden_grad_low = (grad_first * update_gate * silu_grad(hidden_pre)).astype(jnp.bfloat16)
    grad_hidden_weight = product(gated_low, hidden_grad_low, "tv,td->vd")
    grad_gated = product(hidden_grad_low, narrow_low[0], "td,vd->tv")
    grad_reset = grad_gated * attended
    attend_grad_low = (grad_gated * reset_gate).astype(jnp.bfloat16)
    grad_softened = product(attend_grad_low, value_all, "tv,kv->tk")
    row_inner = jnp.sum(softened * grad_softened, axis=1, keepdims=True)
    score_grad_low = (softened * (grad_softened - row_inner)).astype(jnp.bfloat16)
    grad_queries = product(score_grad_low, key_all, "tk,kc->tc")
    profile_grad = diagonal_sums(score_grad_low)
    partial_keys = product(score_grad_low, queries, "tk,tc->kc")
    partial_values = product(softened_low, attend_grad_low, "tk,tv->kv")
    grad_keys, grad_values = (
        lax.psum_scatter(partial_keys, "blk", scatter_dimension=0, tiled=True),
        lax.psum_scatter(partial_values, "blk", scatter_dimension=0, tiled=True),
    )
    grad_shared = grad_queries * scaling * qk_gain[:ZD] + grad_keys * qk_gain[ZD:]
    qk_gain_grad = jnp.concatenate(
        [jnp.sum(grad_queries * scaling * shared, axis=0), jnp.sum(grad_keys * shared, axis=0)]
    )
    qk_shift_grad = jnp.concatenate(
        [jnp.sum(grad_queries * scaling, axis=0), jnp.sum(grad_keys, axis=0)]
    )
    value_grad_low = (grad_values * silu_grad(value_pre)).astype(jnp.bfloat16)
    grad_value_weight = product(inputs_low, value_grad_low, "td,tv->dv")
    mixed_grad_low = jnp.concatenate(
        [
            grad_update * update_gate * (1.0 - update_gate),
            grad_shared * silu_grad(shared_pre),
            grad_reset * silu_grad(reset_pre),
            hidden_grad_low.astype(jnp.float32),
        ],
        axis=1,
    ).astype(jnp.bfloat16)
    grad_mixer_weight = product(prime_low, mixed_grad_low, "td,tm->dm")
    grad_pre = product(mixed_grad_low, mixer_low, "tm,dm->td") * silu_grad(pre_act)
    local_adjoint = running(outflow[None] * grad_pre[:, :, None], decays, True)
    leaving = carried_in((whole_decay, decays * local_adjoint[0]), "blk", compose, identity, True)[
        1
    ]
    steps_behind = (length - 1 - jnp.arange(length, dtype=jnp.int32)).astype(jnp.float32)
    adjoint = local_adjoint + jnp.exp(log_decay[None] * steps_behind[:, None, None]) * leaving[None]
    previous = jnp.concatenate([entering[None], states[:-1]], axis=0)
    grad_decay = jnp.sum(adjoint * previous, axis=0)
    grad_inflow = jnp.sum(adjoint * inputs[:, :, None], axis=0)
    grad_outflow = jnp.sum(grad_pre[:, :, None] * states, axis=0)
    tokens_grad = (
        grad_first * (1.0 - update_gate)
        + product(value_grad_low, widen_low[0], "tv,dv->td")
        + grad_pre * omega_scale
        + jnp.sum(adjoint * inflow[None], axis=2)
    )
    grad_damping = -mixing * grad_decay + averager[2] * grad_inflow
    average_grad = jnp.stack(
        [
            grad_damping * damping * (1.0 - damping),
            -damping * grad_decay * mixing * (1.0 - mixing),
            damping * grad_inflow,
            grad_outflow * NH ** (-0.5),
        ]
    )
    row_grad = lax.dynamic_update_slice(
        jnp.zeros((2 * full_length,), jnp.float32), profile_grad, (begin,)
    )
    table_grad = jnp.dot(row_grad[:-1], selector, precision=lax.Precision.HIGHEST)
    vector_local = jnp.concatenate(
        [
            jnp.sum(mixed_grad_low, axis=0, dtype=jnp.float32),
            jnp.sum(value_grad_low, axis=0, dtype=jnp.float32),
            jnp.sum(hidden_grad_low, axis=0, dtype=jnp.float32),
            jnp.sum(expand_grad_low, axis=0, dtype=jnp.float32),
            jnp.sum(project_low, axis=0, dtype=jnp.float32),
            gain_one_grad,
            shift_one_grad,
            gain_two_grad,
            shift_two_grad,
            jnp.sum(grad_pre * inputs, axis=0),
            qk_gain_grad,
            qk_shift_grad,
            table_grad,
        ]
    )
    full_grads = (
        grad_mixer_weight,
        jnp.stack([grad_value_weight, grad_up]),
        jnp.stack([grad_hidden_weight, grad_down]),
    )
    column_grads = (
        lax.psum_scatter(
            full_grads[0].astype(jnp.bfloat16), "blk", scatter_dimension=1, tiled=True
        ).astype(jnp.float32),
        lax.psum_scatter(
            full_grads[1].astype(jnp.bfloat16), "blk", scatter_dimension=2, tiled=True
        ).astype(jnp.float32),
        lax.psum_scatter(
            full_grads[2].astype(jnp.bfloat16), "blk", scatter_dimension=2, tiled=True
        ).astype(jnp.float32),
    )
    mixer_part, widen_part, narrow_part = (
        lax.psum(column_grads[0].astype(jnp.bfloat16), "dp").astype(jnp.float32),
        lax.psum(column_grads[1].astype(jnp.bfloat16), "dp").astype(jnp.float32),
        lax.psum(column_grads[2].astype(jnp.bfloat16), "dp").astype(jnp.float32),
    )
    vector_sum, average_sum = lax.psum((vector_local, average_grad), ("dp", "blk"))
    stacks = (mixer_part[None], widen_part, narrow_part)
    masters = (mixer_weight[None], widen_weight, narrow_weight)
    rows_old = (mixer_rows[None], widen_rows, narrow_rows)
    columns_old = (mixer_cols[None], widen_cols, narrow_cols)
    column_total = (MX, VD, D)
    local_square = jnp.sum(vector_sum * vector_sum) + jnp.sum(average_sum * average_sum)
    grad_squares = tuple((jnp.sum(matrix * matrix, axis=(1, 2)) for matrix in stacks))
    weight_squares = tuple((jnp.sum(matrix * matrix, axis=(1, 2)) for matrix in masters))
    decay_rate = 1.0 - STEP ** (-0.8)
    summed = lax.psum(grad_squares + weight_squares, "blk")
    clip_norm = jnp.sqrt(
        jnp.sum(summed[0]) + jnp.sum(summed[1]) + jnp.sum(summed[2]) + local_square
    )
    factor = jnp.minimum(1.0, CLIP_NORM / clip_norm)
    clipped = tuple((matrix * factor for matrix in stacks))
    squares = tuple((matrix * matrix + EPS_ONE for matrix in clipped))
    row_sums = lax.psum(tuple((jnp.sum(square_part, axis=2) for square_part in squares)), "blk")
    column_means = tuple((jnp.mean(square_part, axis=1) for square_part in squares))
    weight_total = summed[3:6]
    rows_new = tuple(
        (
            decay_rate * rows_old[member]
            + (1.0 - decay_rate) * row_sums[member] / column_total[member]
            for member in range(3)
        )
    )
    columns_new = tuple(
        (
            decay_rate * columns_old[member] + (1.0 - decay_rate) * column_means[member]
            for member in range(3)
        )
    )
    updates = tuple(
        (
            clipped[member]
            * lax.rsqrt(
                rows_new[member][:, :, None]
                * columns_new[member][:, None, :]
                / jnp.mean(rows_new[member], axis=1)[:, None, None]
            )
            for member in range(3)
        )
    )
    update_squares = lax.psum(
        tuple((jnp.sum(update * update, axis=(1, 2)) for update in updates)), "blk"
    )
    new_list = []
    for member in range(3):
        entries = rows_old[member].shape[1] * column_total[member]
        rms_update = jnp.sqrt(update_squares[member] / entries)
        bounded = updates[member] / jnp.maximum(1.0, rms_update / CLIP_UPDATE)[:, None, None]
        rms_weight = jnp.sqrt(weight_total[member] / entries)
        new_list.append(
            masters[member] - RATE * jnp.maximum(EPS_TWO, rms_weight)[:, None, None] * bounded
        )
    vector_grad = vector_sum * factor
    averager_grad = average_sum * factor
    vector_new, moment_vector = plain_update(vectors, vector_grad, vector_moment, decay_rate)
    averager_new, moment_averager = plain_update(
        averager, averager_grad, averager_moment, decay_rate
    )
    return (
        block_out[None],
        tokens_grad[None],
        clipped[0][0],
        clipped[1],
        clipped[2],
        vector_grad,
        averager_grad,
        new_list[0][0],
        new_list[1],
        new_list[2],
        vector_new,
        averager_new,
        rows_new[0][0],
        columns_new[0][0],
        rows_new[1],
        columns_new[1],
        rows_new[2],
        columns_new[2],
        moment_vector,
        moment_averager,
        clip_norm,
    )


def on_device(
    tokens, cotangent, mixer_weight, widen_weight, narrow_weight, vectors, averager, bias_index,
    mixer_rows, mixer_cols, widen_rows, widen_cols, narrow_rows, narrow_cols, vector_moment, averager_moment,
):
    G = lax.axis_size("blk") // 4
    count = lax.axis_size("dp") // 2
    mix, wid, nar, avg, vv, index = prologue(
        mixer_weight, widen_weight, narrow_weight, vectors, averager, bias_index
    )
    r = main_call(
        G, count, tokens[0], cotangent[0], mix, wid, nar, avg, vv, index, (mixer_rows.reshape(D // 128, 128), widen_rows, narrow_rows),
        (mixer_cols[None], widen_cols, narrow_cols),
    )
    out = step_call(
        G, (r["gm"], r["gw"], r["gn"], r["sums"], r["ma"]), (mix, wid, nar),
        (r["rm"], r["rw"], r["rn"], r["cm"], r["cw"], r["cn"], r["scal"]), vectors.reshape(NVEC // 128, 128),
        vector_moment.reshape(NVEC // 128, 128), avg, jnp.swapaxes(averager_moment, 1, 2), r["block"], r["tok"],
    )
    gm, gw, gn, vg, ag, nm, nw, nn, nv, na, rm, cm, rw, cw, rn, cn, vmom, amom, clip, block, tok = out
    ag, na, amom, gw, gn, nw, nn = (jnp.swapaxes(v, 1, 2) for v in (ag, na, amom, gw, gn, nw, nn))
    gm, nm = gm.T, nm.T
    return (
        block[None], tok[None], gm, gw, gn, vg.reshape(NVEC), ag, nm, nw, nn, nv.reshape(NVEC), na,
        rm.reshape(D), cm[0], rw, cw, rn, cn, vmom.reshape(NVEC), amom, clip.reshape(()),
    )


def solution(mesh):
    in_specs = (
        P("dp", "blk", None), P("dp", "blk", None), P(None, "blk"), P(None, None, "blk"), P(None, None, "blk"),
        P(), P(), P(), P(), P("blk"), P(), P(None, "blk"), P(), P(None, "blk"), P(), P(),
    )
    out_specs = (
        P("dp", "blk", None), P("dp", "blk", None), P(None, "blk"), P(None, None, "blk"), P(None, None, "blk"),
        P(), P(), P(None, "blk"), P(None, None, "blk"), P(None, None, "blk"), P(), P(), P(), P("blk"), P(),
        P(None, "blk"), P(), P(None, "blk"), P(), P(), P(),
    )
    small = mesh.shape["dp"] % 2 == 0 and mesh.shape["blk"] in (8, 16)
    body = on_device if small else with_collectives
    return jax.shard_map(
        body, mesh=mesh, in_specs=in_specs, out_specs=out_specs, check_vma=False
    )
```
